32 devices in a mesh: pipe: 4 (over y, core), dp: 8 (over z, x).
Axes of the slice: x: 2, y: 2, z: 4, core: 2. Of those that a mesh axis runs over, the one named last changes fastest.
Arguments:
- block_input: bfloat16 [8, 1024, 768], P('dp', 'pipe'), may hold values from -6 to 6
- ln_gain: float32 [4, 2, 768], P('pipe'), may hold values from 0.5 to 1.5
- ln_bias: float32 [4, 2, 768], P('pipe'), may hold values from -0.6 to 0.6
- tm_mix: float32 [4, 3, 768], P('pipe'), may hold values from 0 to 1
- cm_mix: float32 [4, 2, 768], P('pipe'), may hold values from 0 to 1
- time_decay: float32 [4, 768], P('pipe'), may hold values from -5 to 1
- time_first: float32 [4, 768], P('pipe'), may hold values from -1 to 1
- tm_in: bfloat16 [4, 3, 768, 768], P('pipe'), may hold values from -0.21875 to 0.21875
- tm_out: bfloat16 [4, 768, 768], P('pipe'), may hold values from -0.4375 to 0.4375
- cm_key: bfloat16 [4, 768, 3072], P('pipe'), may hold values from -0.21875 to 0.21875
- cm_value: bfloat16 [4, 3072, 768], P('pipe'), may hold values from -0.109375 to 0.109375
- cm_recept: bfloat16 [4, 768, 768], P('pipe'), may hold values from -0.21875 to 0.21875
- wkv_num: float32 [4, 8, 768], P('pipe', 'dp'), may hold values from -6 to 6
- wkv_den: float32 [4, 8, 768], P('pipe', 'dp'), may hold values from 0.5 to 4
- last_rows: float32 [4, 2, 8, 768], P('pipe', None, 'dp'), may hold values from -6 to 6
- cotangent: bfloat16 [8, 1024, 768], P('dp', 'pipe'), may hold values from -6 to 6
Outputs:
- block_output: float32 [8, 1024, 768], P('dp', 'pipe')
- grad_block_input: float32 [8, 1024, 768], P('dp', 'pipe')
- grad_ln_gain: float32 [4, 2, 768], P('pipe')
- grad_ln_bias: float32 [4, 2, 768], P('pipe')
- grad_tm_mix: float32 [4, 3, 768], P('pipe')
- grad_cm_mix: float32 [4, 2, 768], P('pipe')
- grad_time_decay: float32 [4, 768], P('pipe')
- grad_time_first: float32 [4, 768], P('pipe')
- grad_tm_in: float32 [4, 3, 768, 768], P('pipe')
- grad_tm_out: float32 [4, 768, 768], P('pipe')
- grad_cm_key: float32 [4, 768, 3072], P('pipe')
- grad_cm_value: float32 [4, 3072, 768], P('pipe')
- grad_cm_recept: float32 [4, 768, 768], P('pipe')
- final_num: float32 [4, 8, 768], P('pipe', 'dp')
- final_den: float32 [4, 8, 768], P('pipe', 'dp')
- final_rows: float32 [4, 2, 8, 768], P('pipe', None, 'dp')
The draws below stay inside these ranges and needn't reach their ends.
All inputs are finite; a program needn't handle non-finite values.
Results may differ from the reference program's by a relative error of at most 0.02.
Values may be sent and summed in bfloat16 or wider, within the bound.
A program may use at most 512 MiB of HBM per device.

```python
import math
import jax
import jax.numpy as jnp
from jax import lax

D = 768
FF = 3072
LAYERS = 4
LENGTH = 1024
SEQS = 8


def shard_levels(own_key, shape, cuts, least, largest):
    level, own = 1.0, jax.random.fold_in(own_key, 6)
    for position, parts in cuts:
        steps = jnp.exp(jax.random.uniform(jax.random.fold_in(own, position), (parts,), jnp.float32, least / len(cuts), largest / len(cuts)))
        level = level * jnp.repeat(steps, shape[position] // parts).reshape([-1 if axis == position else 1 for axis in range(len(shape))])
    return level


def gaussian(own_key, shape, deviation, limit, pieces=(), dtype=jnp.bfloat16):
    result = jax.random.normal(own_key, shape, jnp.float32) * deviation
    if len(pieces) > 0:
        result = shard_levels(own_key, shape, pieces, -0.22, 0.18) * result
    return jnp.clip(result, min=-limit, max=limit).astype(dtype)


def setup_inputs(seed: int = 0) -> dict:
    streams_of = jax.random.split(jax.random.key(seed), 17)
    block_input = gaussian(streams_of[0], (SEQS, LENGTH, D), 1.0, 6.0, ((0, 8), (1, 4)))
    ln_gain = jnp.clip(1.0 + 0.1 * jax.random.normal(streams_of[1], (LAYERS, 2, D), jnp.float32), 0.5, 1.5)
    ln_bias = gaussian(streams_of[2], (LAYERS, 2, D), 0.2, 0.6, ((0, 4),), jnp.float32)
    tm_mix = jnp.clip(1.0 * jax.random.uniform(streams_of[3], (LAYERS, 3, D), jnp.float32) ** shard_levels(streams_of[3], (LAYERS, 3, D), ((0, 4),), -0.2, 0.2), 0.0, 1.0)
    cm_mix = jnp.clip(1.0 * jax.random.uniform(streams_of[4], (LAYERS, 2, D), jnp.float32) ** shard_levels(streams_of[4], (LAYERS, 2, D), ((0, 4),), -0.2, 0.2), 0.0, 1.0)
    time_decay = jnp.clip(-5.0 + 6.0 * jax.random.uniform(streams_of[5], (LAYERS, D), jnp.float32) ** shard_levels(streams_of[5], (LAYERS, D), ((0, 4),), -0.2, 0.2), -5.0, 1.0)
    time_first = jnp.clip(jax.random.uniform(streams_of[6], (LAYERS, D), jnp.float32, -1.0, 1.0) * shard_levels(streams_of[6], (LAYERS, D), ((0, 4),), -0.4, 0.0), -1.0, 1.0)
    tm_in = gaussian(streams_of[7], (LAYERS, 3, D, D), D ** -0.5, 0.21875, ((0, 4),))
    tm_out = gaussian(streams_of[8], (LAYERS, D, D), (D // 4) ** -0.5, 0.4375, ((0, 4),))
    cm_key = gaussian(streams_of[9], (LAYERS, D, FF), D ** -0.5, 0.21875, ((0, 4),))
    cm_value = gaussian(streams_of[10], (LAYERS, FF, D), FF ** -0.5, 0.109375, ((0, 4),))
    cm_recept = gaussian(streams_of[11], (LAYERS, D, D), D ** -0.5, 0.21875, ((0, 4),))
    wkv_num = gaussian(streams_of[12], (LAYERS, SEQS, D), 1.0, 6.0, ((0, 4), (1, 8)), jnp.float32)
    wkv_den = jnp.clip(jnp.exp(math.log(4.0) - 2.0794415 * jax.random.uniform(streams_of[13], (LAYERS, SEQS, D), jnp.float32) ** shard_levels(streams_of[13], (LAYERS, SEQS, D), ((0, 4), (1, 8)), -0.2, 0.2)), 0.5, 4.0)
    last_rows = gaussian(streams_of[14], (LAYERS, 2, SEQS, D), 1.0, 6.0, ((0, 4), (2, 8)), jnp.float32)
    cotangent = gaussian(streams_of[15], (SEQS, LENGTH, D), 1.0, 6.0, ((0, 8), (1, 4)))
    return {"block_input": block_input, "ln_gain": ln_gain, "ln_bias": ln_bias, "tm_mix": tm_mix, "cm_mix": cm_mix, "time_decay": time_decay, "time_first": time_first, "tm_in": tm_in, "tm_out": tm_out, "cm_key": cm_key, "cm_value": cm_value, "cm_recept": cm_recept, "wkv_num": wkv_num, "wkv_den": wkv_den, "last_rows": last_rows, "cotangent": cotangent}


highest_product_accuracy = lax.Precision.HIGHEST

@jax.custom_vjp
def low(v):
    return lax.optimization_barrier(v.astype(jnp.bfloat16)).astype(jnp.float32)

@jax.custom_vjp
def low_back(v):
    return v

def low_keep(v):
    return (low(v), None)

def low_pass(kept, grad):
    return (grad,)

def back_keep(v):
    return (v, None)

def back_low(kept, grad):
    return (low(grad),)
low.defvjp(low_keep, low_pass)
low_back.defvjp(back_keep, back_low)

def norm_rows(payload_lines, gain_row, bias_row):
    centre = lax.optimization_barrier(jnp.mean(payload_lines, axis=-1, keepdims=True))
    centred = payload_lines - centre
    spread = lax.optimization_barrier(jnp.mean(centred * centred, axis=-1, keepdims=True))
    return centred * lax.rsqrt(spread + 1e-05) * gain_row + bias_row

def mix_rows(payload_lines, gain_row, bias_row, mixing, previous):
    normed = norm_rows(payload_lines, gain_row, bias_row)
    shifted = jnp.concatenate([previous[:, None, :], normed[:, :-1, :]], axis=1)
    weights = mixing[:, None, None, :]
    return (normed[None] * weights + shifted[None] * (1.0 - weights), normed[:, -1, :])

def averaged_pair_iterations(lookup_word_lines, payload_lines, upper_sum_initial, lower_sum_initial, fading_log_rate, leading_word_reward):
    factor = jnp.exp(-jnp.exp(fading_log_rate))

    def advance(carried_pair, step_pair):
        upper_sum_carry, lower_sum_carry = carried_pair
        lookup_present, payload_present = step_pair
        reward_scaled_addend = jnp.exp(leading_word_reward + lookup_present)
        weight = jnp.exp(lookup_present)
        returned_quantity = (upper_sum_carry + reward_scaled_addend * payload_present) / (lower_sum_carry + reward_scaled_addend)
        return ((factor * upper_sum_carry + weight * payload_present, factor * lower_sum_carry + weight), returned_quantity)
    (upper_sum_carry, lower_sum_carry), outputs = lax.scan(jax.checkpoint(advance), (upper_sum_initial, lower_sum_initial), (jnp.moveaxis(lookup_word_lines, 1, 0), jnp.moveaxis(payload_lines, 1, 0)))
    return (jnp.moveaxis(outputs, 0, 1), upper_sum_carry, lower_sum_carry)

def run_layer(input_rows, learned_nested_collection, carried):
    scale_layered, offset_layered, temporal_blend_unit, feature_blend_unit, fading_log_rate, leading_word_reward, incoming_coefficients, outgoing_coefficients, lookup_coefficient_array, payload_coefficient_array, acceptance_coefficients = learned_nested_collection
    upper_sum_initial, lower_sum_initial, prev_time, prev_chan = carried
    mixed_rows, last_time = mix_rows(input_rows, scale_layered[0], offset_layered[0], temporal_blend_unit, prev_time)
    mixed_rows = low(mixed_rows)
    mapped_lines = low_back(jnp.einsum('csld,cde->csle', mixed_rows, incoming_coefficients, precision=highest_product_accuracy))
    averaged_pair_lines, upper_sum_final, lower_sum_final = averaged_pair_iterations(mapped_lines[0], mapped_lines[1], upper_sum_initial, lower_sum_initial, fading_log_rate, leading_word_reward)
    gated_output_rows = low(jax.nn.sigmoid(mapped_lines[2]) * averaged_pair_lines)
    after_time_mixing = input_rows + low_back(jnp.einsum('jcy,yh->jch', gated_output_rows, outgoing_coefficients, precision=highest_product_accuracy))
    feature_lines, last_chan = mix_rows(after_time_mixing, scale_layered[1], offset_layered[1], feature_blend_unit, prev_chan)
    feature_lines = low(feature_lines)
    lookup_linear_part = low_back(jnp.einsum('jfx,xg->jfg', feature_lines[0], lookup_coefficient_array, precision=highest_product_accuracy))
    squared_relu = low(jnp.square(jnp.maximum(lookup_linear_part, 0.0)))
    value_output = low_back(jnp.einsum('cok,kz->coz', squared_relu, payload_coefficient_array, precision=highest_product_accuracy))
    receptance_preactivation = low_back(jnp.einsum('jcy,yh->jch', feature_lines[1], acceptance_coefficients, precision=highest_product_accuracy))
    after_chan = after_time_mixing + jax.nn.sigmoid(receptance_preactivation) * value_output
    return (after_chan, (upper_sum_final, lower_sum_final, last_time, last_chan))

def reference(block_input, ln_gain, ln_bias, tm_mix, cm_mix, time_decay, time_first, tm_in, tm_out, cm_key, cm_value, cm_recept, wkv_num, wkv_den, last_rows, cotangent):
    weights = tuple((array.astype(jnp.float32) for array in (ln_gain, ln_bias, tm_mix, cm_mix, time_decay, time_first, tm_in, tm_out, cm_key, cm_value, cm_recept)))
    seq_items = (block_input, cotangent, jnp.moveaxis(wkv_num, 1, 0), jnp.moveaxis(wkv_den, 1, 0), jnp.moveaxis(last_rows, 2, 0))

    def one_sequence(totals, seq_item):
        seq_input, seq_grad, upper_sum_initial, lower_sum_initial, rows_start = seq_item

        def forward(learned_nested_collection, input_rows):
            hidden = input_rows[None]
            finals = []
            for layer_at in range(LAYERS):
                if layer_at > 0:
                    hidden = low_back(low(hidden))
                layer_params = tuple((param[layer_at] for param in learned_nested_collection))
                carried = (upper_sum_initial[layer_at][None], lower_sum_initial[layer_at][None], rows_start[layer_at, 0][None], rows_start[layer_at, 1][None])
                hidden, layer_final = run_layer(hidden, layer_params, carried)
                finals.append(layer_final)
            stacked = tuple((jnp.stack([layer_final[member][0] for layer_final in finals]) for member in range(4)))
            return (hidden[0], stacked)
        output, pull_back, stacked = jax.vjp(forward, weights, seq_input.astype(jnp.float32), has_aux=True)
        grad_params, grad_input = pull_back(seq_grad.astype(jnp.float32))
        totals = jax.tree.map(lambda summed, increment: summed + increment, totals, grad_params)
        return (totals, (output, grad_input, stacked[0], stacked[1], jnp.stack([stacked[2], stacked[3]], axis=1)))
    zero_grads = jax.tree.map(jnp.zeros_like, weights)
    totals, (outputs, grad_inputs, final_num, final_den, final_rows) = lax.scan(one_sequence, zero_grads, seq_items)
    return (outputs, grad_inputs, totals[0], totals[1], totals[2], totals[3], totals[4], totals[5], totals[6], totals[7], totals[8], totals[9], totals[10], jnp.moveaxis(final_num, 0, 1), jnp.moveaxis(final_den, 0, 1), jnp.moveaxis(final_rows, 0, 2))
```

```python
import functools

import jax
import jax.numpy as jnp
from jax import lax
from jax.experimental import pallas as pl
from jax.experimental.pallas import tpu as pltpu
from jax.sharding import PartitionSpec as P

MESH = pl.DeviceIdType.MESH
BF, F32 = jnp.bfloat16, jnp.float32
TOKENS = 128
SPLIT = 3
LAG = 2
VMEM_BYTES = 62 * 1024 * 1024


def position():
    p, i = lax.axis_index("pipe"), lax.axis_index("dp")
    y = lax.div(p, 2)
    k = p - 2 * y
    first = 2 * lax.div(i, 2)
    s = i - first
    return p, i, y, k, first, s, lax.rem(s + y, 2)


def home(layer, k, first):
    y = lax.div(layer, 2)
    return 2 * y + k, first + lax.rem(layer - y, 2)


def local(src, dst, sem):
    return pltpu.make_async_copy(src, dst, sem)


def remote(src, dst, send, recv, p, i):
    return pltpu.make_async_remote_copy(
        src_ref=src, dst_ref=dst, send_sem=send, recv_sem=recv, device_id=(p, i), device_id_type=MESH
    )


def drain(ref, sem):
    pltpu.make_async_copy(ref, ref, sem).wait()


def dot(a, b):
    return lax.dot_general(a, b, (((1,), (0,)), ((), ())), preferred_element_type=F32)


def dot_t(a, b):
    return lax.dot_general(a, b, (((1,), (1,)), ((), ())), preferred_element_type=F32)


def later(v, row):
    at = lax.broadcasted_iota(jnp.int32, v.shape, 0)
    return jnp.where(at == 0, row, pltpu.roll(v, 1, 0))


def earlier(v, row):
    n = v.shape[0]
    at = lax.broadcasted_iota(jnp.int32, v.shape, 0)
    return jnp.where(at == n - 1, row, pltpu.roll(v, n - 1, 0))


def scan_down(v, rate):
    n, by = v.shape[0], 1
    while by < n:
        fade = jnp.exp(-float(by) * rate)
        if by < 8:
            at = lax.broadcasted_iota(jnp.int32, v.shape, 0)
            v = v + jnp.where(at >= by, fade * pltpu.roll(v, by, 0), 0.0)
        else:
            v = jnp.concatenate([v[:by], v[by:] + fade * v[: n - by]], axis=0)
        by *= 2
    return v


def scan_up(v, rate):
    n, by = v.shape[0], 1
    while by < n:
        fade = jnp.exp(-float(by) * rate)
        if by < 8:
            at = lax.broadcasted_iota(jnp.int32, v.shape, 0)
            v = v + jnp.where(at < n - by, fade * pltpu.roll(v, n - by, 0), 0.0)
        else:
            v = jnp.concatenate([v[: n - by] + fade * v[by:], v[n - by :]], axis=0)
        by *= 2
    return v


def centred(v):
    c = v - jnp.mean(v, axis=-1, keepdims=True)
    r = lax.rsqrt(jnp.mean(c * c, axis=-1, keepdims=True) + 1e-05)
    return c * r, r


def layers_kernel(
    npipe,
    x_hbm, cot_hbm, gain_hbm, bias_hbm, tmix_hbm, cmix_hbm, decay_hbm, first_hbm, num_hbm, den_hbm, rows_hbm,
    win_hbm, wout_hbm, wck_hbm, wcv_hbm, wcr_hbm,
    xo, go, small, fin_num, fin_den, fin_rows, ob, gb, turned,
    w, gain, bias, tmix, cmix, decay, bonus_s, num_s, den_s, rows_s, inbox, gbox,
    e_s, v_s, n_s, d_s, s_s, xh1, xh2, s2_s, c2_s, relu, r1, r2, car1, car2, back, acc, xst, gst,
    w_send, w_recv, in_send, in_recv, g_send, g_recv, x0_send, cot_send, ob_recv, gb_recv,
    st_send, st_recv, fin_send, fin_recv, x_sem, go_sem, relu_sem, turn_out, turn_in,
):
    p, i, y, k, first, s, m_chip = position()
    layer = 2 * y + m_chip
    last = npipe - 1
    nm, nt, width = inbox.shape
    nq = relu.shape[1] // nt
    per = x_hbm.shape[1] // nt
    nblocks = w.shape[0]
    key, val, rec = 4, 4 + nq, 4 + 2 * nq

    weights = [(gain_hbm.at[0], gain), (bias_hbm.at[0], bias), (tmix_hbm.at[0], tmix), (cmix_hbm.at[0], cmix),
               (decay_hbm, decay), (first_hbm, bonus_s)]
    base = len(weights)
    order = [0, 1, 2, 3] + [at for q in range(nq) for at in (key + q, val + q)] + [rec]
    source = {rec: wcr_hbm.at[0], 3: wout_hbm.at[0]}
    for c in range(3):
        source[c] = win_hbm.at[0, c]
    for q in range(nq):
        source[key + q] = wck_hbm.at[0, :, q * width : (q + 1) * width]
        source[val + q] = wcv_hbm.at[0, q * width : (q + 1) * width]
    weights += [(source[at], w.at[at]) for at in order]
    place = {at: base + n for n, at in enumerate(order)}
    owner = k == m_chip

    @pl.when(owner)
    def _():
        for a, (src, dst) in enumerate(weights):
            local(src, dst, w_recv.at[a]).start()

    barrier = pltpu.get_barrier_semaphore()
    for step in range(1, 2 * npipe):
        at = lax.rem(2 * p + s + step, 2 * npipe)
        op = lax.div(at, 2)
        pl.semaphore_signal(barrier, inc=1, device_id=(op, first + at - 2 * op), device_id_type=MESH)
    pl.semaphore_wait(barrier, 2 * npipe - 1)

    ip, ii = home(0, s, first)
    in_self = jnp.logical_and(ip == p, ii == i)
    cp, ci = home(last, s, first)
    cot_self = jnp.logical_and(cp == p, ci == i)
    tp, ti = home(p, s, first)
    st_self = jnp.logical_and(tp == p, ti == i)

    def give(src, dst, send, recv, dp, di, mine):
        @pl.when(mine)
        def _():
            local(src, dst, recv).start()

        @pl.when(jnp.logical_not(mine))
        def _():
            remote(src, dst, send, recv, dp, di).start()

    states = ((num_hbm.at[0], num_s), (den_hbm.at[0], den_s), (rows_hbm.at[0, :, 0], rows_s))

    @pl.when(owner)
    def _():
        for a, (src, dst) in enumerate(weights[:base]):
            remote(src, dst, w_send.at[a], w_recv.at[a], 2 * y + 1 - k, i).start()

    for u in range(per):
        give(x_hbm.at[0, pl.ds(u * nt, nt)], inbox.at[p * per + u], x0_send.at[u], in_recv.at[p * per + u], ip, ii, in_self)
    for a, (src, dst) in enumerate(states):
        give(src, dst, st_send.at[a], st_recv.at[a], tp, ti, st_self)

    @pl.when(owner)
    def _():
        for a, (src, dst) in enumerate(weights[base:]):
            remote(src, dst, w_send.at[base + a], w_recv.at[base + a], 2 * y + 1 - k, i).start()

    for u in range(per):
        give(cot_hbm.at[0, pl.ds(u * nt, nt)], gbox.at[p * per + u], cot_send.at[u], g_recv.at[p * per + u], cp, ci, cot_self)

    for a in range(base):
        drain(weights[a][1], w_recv.at[a])
    for a, (src, dst) in enumerate(states):
        drain(dst, st_recv.at[a])
    np_, ni = home(layer + 1, k, first)
    bp, bi = home(layer - 1, k, first)
    rate = jnp.exp(decay[...])
    bonus = jnp.exp(bonus_s[...])
    fade = jnp.exp(-rate)

    @pl.when(layer == last)
    def _():
        for at in order:
            drain(w.at[at], w_recv.at[place[at]])

        def turn(at, none):
            slot = lax.rem(at, 2)

            @pl.when(at >= 2)
            def _():
                drain(gst.at[slot, pl.ds(0, width)], turn_out.at[slot])

            gst[slot, 0:width] = w[at].T
            local(gst.at[slot, pl.ds(0, width)], turned.at[at], turn_out.at[slot]).start()
            return none

        lax.fori_loop(0, nblocks, turn, 0)
        for slot in range(2):
            drain(gst.at[slot, pl.ds(0, width)], turn_out.at[slot])

    def forward(m, none, begin=False):
        slot = lax.rem(m, 2)

        def ready(*blocks):
            if begin:

                @pl.when(layer < last)
                def _():
                    for at in blocks:
                        drain(w.at[at], w_recv.at[place[at]])

        if not begin:

            @pl.when(m >= 2)
            def _():
                drain(xst.at[slot], x_sem.at[slot])

        drain(inbox.at[m], in_recv.at[m])
        h = inbox[m].astype(F32)
        xh, rs = centred(h)
        xh1[m] = xh.astype(BF)
        r1[m] = rs
        xn = xh * gain[0:1] + bias[0:1]
        prev = rows_s[0:1]
        car1[m, 0:1] = prev
        xp = later(xn, prev)
        rows_s[0:1] = xn[nt - 1 :]
        d = xn - xp
        proj = []
        for c in range(3):
            mixed = (xp + tmix[c : c + 1] * d).astype(BF)
            xst[slot, c * nt : (c + 1) * nt] = mixed
            ready(c)
            proj.append(dot(mixed, w[c]))
        e = jnp.exp(proj[0])
        v = proj[1]
        ev = e * v
        num = scan_down(later(ev, num_s[...]), rate)
        den = scan_down(later(e, den_s[...]), rate)
        num_s[...] = fade * num[nt - 1 :] + ev[nt - 1 :]
        den_s[...] = fade * den[nt - 1 :] + e[nt - 1 :]
        e_s[m] = e
        v_s[m] = v
        n_s[m] = num
        d_s[m] = den
        b = bonus * e
        gate = jax.nn.sigmoid(proj[2])
        s_s[m] = gate.astype(BF)
        gated = (gate * ((num + b * v) / (den + b))).astype(BF)
        xst[slot, 3 * nt : 4 * nt] = gated
        ready(3)
        mid = h + dot(gated, w[3])
        xh, rs = centred(mid)
        xh2[m] = xh.astype(BF)
        r2[m] = rs
        xn = xh * gain[1:2] + bias[1:2]
        prev = rows_s[1:2]
        car2[m, 0:1] = prev
        xp = later(xn, prev)
        rows_s[1:2] = xn[nt - 1 :]
        d = xn - xp
        mixed0 = (xp + cmix[0:1] * d).astype(BF)
        mixed1 = (xp + cmix[1:2] * d).astype(BF)
        xst[slot, 4 * nt : 5 * nt] = mixed0
        xst[slot, 5 * nt : 6 * nt] = mixed1
        out = None
        for q in range(nq):
            ready(key + q)
            r = jnp.maximum(dot(mixed0, w[key + q]), 0.0)
            relu[m, q * nt : (q + 1) * nt] = r.astype(BF)
            ready(val + q)
            part = dot((r * r).astype(BF), w[val + q])
            out = part if out is None else out + part
        ready(rec)
        gate = jax.nn.sigmoid(dot(mixed1, w[rec]))
        s2_s[m] = gate.astype(BF)
        c2_s[m] = (out * gate * (1.0 - gate)).astype(BF)
        inbox[m] = (mid + gate * out).astype(BF)

        @pl.when(layer < last)
        def _():
            remote(inbox.at[m], inbox.at[m], in_send.at[m], in_recv.at[m], np_, ni).start()

        @pl.when(layer == last)
        def _():
            q = lax.div(m, per)
            u = m - q * per
            mine = jnp.logical_and(q == p, first + k == i)
            give(inbox.at[m], ob.at[pl.ds(pl.multiple_of(u * nt, nt), nt)], in_send.at[m], ob_recv.at[u], q, first + k, mine)

        local(xst.at[slot], xo.at[m, pl.ds(0, 6 * nt)], x_sem.at[slot]).start()
        local(relu.at[m], xo.at[m, pl.ds(6 * nt, nq * nt)], relu_sem.at[m]).start()
        return none

    forward(0, 0, True)
    lax.fori_loop(1, nm, forward, 0)

    wanted = [at for q in range(nq) for at in (val + q, key + q)] + [rec, 3, 0, 1, 2]

    @pl.when(layer == last)
    def _():
        for at in wanted:
            local(turned.at[at], w.at[at], turn_in.at[at]).start()

    finals = ((num_s, fin_num.at[0]), (den_s, fin_den.at[0]), (rows_s, fin_rows.at[0, :, 0]))
    fp, fi = layer, first + k
    fin_self = jnp.logical_and(fp == p, fi == i)
    for a, (src, dst) in enumerate(finals):
        give(src, dst, fin_send.at[a], fin_recv.at[a], fp, fi, fin_self)

    @pl.when(layer < last)
    def _():
        def turn(at, none):
            w[at] = w[at].T
            return none

        lax.fori_loop(0, nblocks, turn, 0)

    back[...] = jnp.zeros_like(back)
    acc[...] = jnp.zeros_like(acc)

    def mix_back(grads, xh, rs, prev, gain_row, bias_row, mixes, back_at, acc_gain, acc_bias, acc_mix):
        xn = xh * gain_row + bias_row
        d = xn - later(xn, prev)
        here, total = None, None
        for at, (g, mix) in enumerate(zip(grads, mixes)):
            acc[acc_mix + at : acc_mix + at + 1] += jnp.sum(g * d, axis=0, keepdims=True)
            here = g * mix if here is None else here + g * mix
            total = g if total is None else total + g
        shifted = total - here
        gx = here + earlier(shifted, back[back_at : back_at + 1])
        back[back_at : back_at + 1] = shifted[0:1]
        acc[acc_gain : acc_gain + 1] += jnp.sum(gx * xh, axis=0, keepdims=True)
        acc[acc_bias : acc_bias + 1] += jnp.sum(gx, axis=0, keepdims=True)
        gp = gx * gain_row
        return rs * (gp - jnp.mean(gp, axis=-1, keepdims=True) - xh * jnp.mean(gp * xh, axis=-1, keepdims=True))

    def backward(step, none, begin=False):
        m = nm - 1 - step
        slot = lax.rem(step, 2)

        def ready(*blocks):
            if begin:

                @pl.when(layer == last)
                def _():
                    for at in blocks:
                        drain(w.at[at], turn_in.at[at])

        if not begin:

            @pl.when(step >= 2)
            def _():
                drain(gst.at[slot], go_sem.at[slot])

        drain(gbox.at[m], g_recv.at[m])
        g = gbox[m].astype(F32)
        gvo = (g * s2_s[m].astype(F32)).astype(BF)
        grp = (g * c2_s[m].astype(F32)).astype(BF)
        gst[slot, (4 + nq) * nt : (5 + nq) * nt] = gvo
        gst[slot, (5 + nq) * nt : (6 + nq) * nt] = grp
        gm0 = None
        for q in range(nq):
            ready(val + q)
            gs = dot(gvo, w[val + q])
            gk = (gs * (2.0 * relu[m, q * nt : (q + 1) * nt].astype(F32))).astype(BF)
            gst[slot, (4 + q) * nt : (5 + q) * nt] = gk
            ready(key + q)
            part = dot(gk, w[key + q])
            gm0 = part if gm0 is None else gm0 + part
        ready(rec)
        gm1 = dot(grp, w[rec])
        gmid = g + mix_back(
            (gm0, gm1), xh2[m].astype(F32), r2[m], car2[m, 0:1], gain[1:2], bias[1:2], (cmix[0:1], cmix[1:2]), 3, 1, 3, 7
        )
        gbranch = gmid.astype(BF)
        gst[slot, 3 * nt : 4 * nt] = gbranch
        ready(3)
        gg = dot(gbranch, w[3])
        gate = s_s[m].astype(F32)
        e, v, num, den = e_s[m], v_s[m], n_s[m], d_s[m]
        b = bonus * e
        inv = 1.0 / (den + b)
        wkv = (num + b * v) * inv
        gn = gg * gate * inv
        gr = gg * wkv * gate * (1.0 - gate)
        gd = -gn * wkv
        an = scan_up(earlier(gn, back[0:1]), rate)
        ad = scan_up(earlier(gd, back[1:2]), rate)
        back[0:1] = gn[0:1] + fade * an[0:1]
        back[1:2] = gd[0:1] + fade * ad[0:1]
        now = b * (gn * v + gd)
        acc[10:11] += jnp.sum(now, axis=0, keepdims=True)
        acc[9:10] += jnp.sum(an * num + ad * den, axis=0, keepdims=True)
        gproj = (
            (e * (an * v + ad) + now).astype(BF),
            (b * gn + e * an).astype(BF),
            gr.astype(BF),
        )
        ready(0, 1, 2)
        grads = []
        for c in range(3):
            gst[slot, c * nt : (c + 1) * nt] = gproj[c]
            grads.append(dot(gproj[c], w[c]))
        gh = gmid + mix_back(
            grads, xh1[m].astype(F32), r1[m], car1[m, 0:1], gain[0:1], bias[0:1],
            (tmix[0:1], tmix[1:2], tmix[2:3]), 2, 0, 2, 4,
        )
        gbox[m] = gh.astype(BF)

        @pl.when(layer > 0)
        def _():
            remote(gbox.at[m], gbox.at[m], g_send.at[m], g_recv.at[m], bp, bi).start()

        @pl.when(layer == 0)
        def _():
            q = lax.div(m, per)
            u = m - q * per
            mine = jnp.logical_and(q == p, first + k == i)
            give(gbox.at[m], gb.at[pl.ds(pl.multiple_of(u * nt, nt), nt)], g_send.at[m], gb_recv.at[u], q, first + k, mine)

        local(gst.at[slot], go.at[m], go_sem.at[slot]).start()
        return none

    backward(0, 0, True)
    lax.fori_loop(1, nm, backward, 0)
    small[...] = acc[...]
    small[9:10] = acc[9:10] * (-rate * fade)

    for slot in range(min(2, nm)):
        drain(xst.at[slot], x_sem.at[slot])
        drain(gst.at[slot], go_sem.at[slot])

    def finish(m, none):
        drain(relu.at[m], relu_sem.at[m])
        mine = jnp.logical_and(lax.div(m, per) == p, first + k == i)

        @pl.when(jnp.logical_not(jnp.logical_and(layer == last, mine)))
        def _():
            drain(inbox.at[m], in_send.at[m])

        @pl.when(jnp.logical_not(jnp.logical_and(layer == 0, mine)))
        def _():
            drain(gbox.at[m], g_send.at[m])

        return none

    lax.fori_loop(0, nm, finish, 0)
    for u in range(per):
        part = pl.ds(u * nt, nt)
        drain(ob.at[part], ob_recv.at[u])
        drain(gb.at[part], gb_recv.at[u])

        @pl.when(jnp.logical_not(in_self))
        def _():
            drain(x_hbm.at[0, part], x0_send.at[u])

        @pl.when(jnp.logical_not(cot_self))
        def _():
            drain(cot_hbm.at[0, part], cot_send.at[u])

    @pl.when(jnp.logical_not(st_self))
    def _():
        for a, (src, dst) in enumerate(states):
            drain(dst, st_send.at[a])

    @pl.when(jnp.logical_not(fin_self))
    def _():
        for a, (src, dst) in enumerate(finals):
            drain(src, fin_send.at[a])

    for a, (src, dst) in enumerate(finals):
        drain(dst, fin_recv.at[a])

    @pl.when(owner)
    def _():
        for a, (src, dst) in enumerate(weights):
            drain(dst, w_send.at[a])


def sums_kernel(
    npipe, ngroups, x_hbm, g_hbm, small, out, out_small,
    xb, gbuf, dws, xs, own, rx, rr, ag, xs_s, own_s, rx_s, rr_s, ag_s,
    x_sem, g_sem, ex_send, ex_recv, r_send, r_recv, a_send, a_recv, o_send, o_recv, small_send, small_recv,
):
    p, i, y, k, first, s, m_chip = position()
    j = lax.div(i, 2)
    sib = 2 * y + 1 - k
    nc, half, width = own.shape
    quarter = half // 2
    rows_c = 2 * half
    split = width // rows_c
    nm, nt = xb.shape[1:3]
    nq = x_hbm.shape[1] // nt - 6
    hops = (ngroups - 1 - j, j)
    dist = (j, ngroups - 1 - j)
    step_by = (-1, 1)
    dest = 2 * y + m_chip
    other = first + 1 - s

    barrier = pltpu.get_barrier_semaphore()
    for bp, bi in ((sib, i), (p, other), (sib, other)):
        pl.semaphore_signal(barrier, inc=1, device_id=(bp, bi), device_id_type=MESH)

    @pl.when(j > 0)
    def _():
        pl.semaphore_signal(barrier, inc=1, device_id=(p, i - 2), device_id_type=MESH)

    @pl.when(j < ngroups - 1)
    def _():
        pl.semaphore_signal(barrier, inc=1, device_id=(p, i + 2), device_id_type=MESH)

    def blocks(c):
        b = lax.div(c, split)
        xi = jnp.where(b < 4, b, jnp.where(b < 4 + nq, 4, jnp.where(b < 4 + 2 * nq, b - nq + 2, 5)))
        gi = jnp.where(b < 4 + nq, b, jnp.where(b < 4 + 2 * nq, 4 + nq, 5 + nq))
        return b, xi, gi

    def loads(c, slot):
        b, xi, gi = blocks(c)
        part = c - b * split
        cols = pl.ds(pl.multiple_of(part * rows_c, rows_c), rows_c)
        return (
            local(x_hbm.at[:, pl.ds(pl.multiple_of(xi * nt, nt), nt), cols], xb.at[slot], x_sem.at[slot]),
            local(g_hbm.at[:, pl.ds(pl.multiple_of(gi * nt, nt), nt)], gbuf.at[slot], g_sem.at[slot]),
        )

    for copy in loads(0, 0):
        copy.start()

    neighbours = 3 + jnp.where(j > 0, 1, 0) + jnp.where(j < ngroups - 1, 1, 0)
    pl.semaphore_wait(barrier, neighbours)

    def produce(c):
        slot = lax.rem(c, 2)

        @pl.when(c + 1 < nc)
        def _():
            for copy in loads(c + 1, 1 - slot):
                copy.start()

        for copy in loads(c, slot):
            copy.wait()
        b = lax.div(c, split)

        @pl.when(jnp.logical_and(b >= 4 + nq, b < 4 + 2 * nq))
        def _():
            r = xb[slot].astype(F32)
            xb[slot] = (r * r).astype(BF)

        dws[...] = lax.dot_general(
            xb[slot].reshape(nm * nt, rows_c), gbuf[slot].reshape(nm * nt, width), (((0,), (0,)), ((), ())),
            preferred_element_type=F32,
        )

        @pl.when(c >= 2)
        def _():
            drain(xs.at[slot], ex_send.at[slot])

        xs[slot] = dws[pl.ds(pl.multiple_of((1 - k) * half, half), half)].astype(BF)
        remote(xs.at[slot], rx.at[c], ex_send.at[slot], ex_recv.at[c], sib, i).start()
        own[c] = dws[pl.ds(pl.multiple_of(k * half, half), half)]

        @pl.when(c == 0)
        def _():
            n = small.shape[0]
            mine = jnp.where(k == 0, 1.0, 0.0)
            own_s[...] = jnp.zeros_like(own_s)
            xs_s[...] = jnp.zeros_like(xs_s)
            own_s[0:n] = small[...] * mine
            xs_s[0:n] = (small[...] * (1.0 - mine)).astype(BF)
            remote(xs_s, rx_s, small_send.at[0], ex_recv.at[nc], sib, i).start()

    def exchange(c):
        drain(rx.at[c], ex_recv.at[c])
        own[c] = own[c] + rx[c].astype(F32)

        @pl.when(c == 0)
        def _():
            drain(rx_s, ex_recv.at[nc])
            own_s[...] = own_s[...] + rx_s[...].astype(F32)

    def reduce(c, d):
        def one(value, rr_at, ag_at, send, recv):
            @pl.when(hops[d] == 0)
            def _():
                rr_at[...] = value().astype(BF)

            @pl.when(hops[d] > 0)
            def _():
                drain(rr_at, recv)

                @pl.when(dist[d] > 0)
                def _():
                    rr_at[...] = (value() + rr_at[...].astype(F32)).astype(BF)

                @pl.when(dist[d] == 0)
                def _():
                    ag_at[...] = (value() + rr_at[...].astype(F32)).astype(BF)

            @pl.when(dist[d] > 0)
            def _():
                remote(rr_at, rr_at, send, recv, p, i + 2 * step_by[d]).start()

            @pl.when(jnp.logical_and(dist[d] == 0, hops[d] == 0))
            def _():
                ag_at[...] = rr_at[...]

        one(lambda: own[c, d * quarter : (d + 1) * quarter], rr.at[d, c], ag.at[d, c], r_send.at[d], r_recv.at[d, c])

        @pl.when(c == 0)
        def _():
            n = rr_s.shape[1]
            one(lambda: own_s[d * n : (d + 1) * n], rr_s.at[d], ag_s.at[d], small_send.at[1 + d], r_recv.at[d, nc])

    def spread(c, d):
        def one(ag_at, to, forward_send, recv, local_send, far_send, out_recv):
            @pl.when(dist[d] > 0)
            def _():
                drain(ag_at, recv)

            @pl.when(hops[d] > 0)
            def _():
                remote(ag_at, ag_at, forward_send, recv, p, i - 2 * step_by[d]).start()

            remote(ag_at, to, far_send, out_recv, dest, other).start()

            @pl.when(p == dest)
            def _():
                local(ag_at, to, out_recv).start()

            @pl.when(p != dest)
            def _():
                remote(ag_at, to, local_send, out_recv, dest, i).start()

        b = lax.div(c, split)
        row = (c - b * split) * rows_c + k * half + d * quarter
        to = out.at[b, pl.ds(pl.multiple_of(row, quarter), quarter)]
        one(ag.at[d, c], to, a_send.at[d], a_recv.at[d, c], o_send.at[0], o_send.at[1], o_recv.at[0])

        @pl.when(c == 0)
        def _():
            n = rr_s.shape[1]
            to_s = out_small.at[pl.ds(pl.multiple_of(k * 2 * n + d * n, n), n)]
            one(ag_s.at[d], to_s, small_send.at[3 + d], a_recv.at[d, nc], small_send.at[5 + d], small_send.at[7 + d], small_recv.at[0])

    def inside(c, f):
        @pl.when(jnp.logical_and(c >= 0, c < nc))
        def _():
            f(c)

    def step(t, none):
        inside(t, produce)
        inside(t - 1, exchange)
        for d in range(2):
            inside(t - 1 - LAG * hops[d], lambda c: reduce(c, d))
        for d in range(2):
            inside(t - 1 - LAG * (ngroups - 1 + dist[d]), lambda c: spread(c, d))
        return none

    lax.fori_loop(0, nc + 1 + 2 * LAG * (ngroups - 1), step, 0)

    for slot in range(min(2, nc)):
        drain(xs.at[slot], ex_send.at[slot])
    drain(xs_s, small_send.at[0])
    for d in range(2):

        @pl.when(dist[d] > 0)
        def _():
            drain(rr.at[d], r_send.at[d])
            drain(rr_s.at[d], small_send.at[1 + d])

        @pl.when(hops[d] > 0)
        def _():
            drain(ag.at[d], a_send.at[d])
            drain(ag_s.at[d], small_send.at[3 + d])

        @pl.when(p != dest)
        def _():
            drain(ag_s.at[d], small_send.at[5 + d])

        drain(ag_s.at[d], small_send.at[7 + d])

    @pl.when(p != dest)
    def _():
        drain(ag, o_send.at[0])

    drain(ag, o_send.at[1])
    drain(out, o_recv.at[0])
    drain(out_small, small_recv.at[0])


def widen_kernel(
    ob, gb, rows, w_in, w_out, w_key, w_val, w_rec,
    out, grad, gain, bias, tmix, cmix, decay, bonus, g_in, g_out, g_key, g_val, g_rec,
):
    for src, dst in ((ob, out), (gb, grad), (w_in, g_in), (w_out, g_out), (w_val, g_val), (w_rec, g_rec)):
        dst[...] = src[...].astype(F32)
    nq, _, width = w_key.shape
    for q in range(nq):
        g_key[:, q * width : (q + 1) * width] = w_key[q].astype(F32)
    at = 0
    for dst in (gain, bias, tmix, cmix, decay, bonus):
        dst[...] = rows[at : at + dst.shape[0]].astype(F32)
        at += dst.shape[0]


def body(
    block_input, ln_gain, ln_bias, tm_mix, cm_mix, time_decay, time_first, tm_in, tm_out,
    cm_key, cm_value, cm_recept, wkv_num, wkv_den, last_rows, cotangent,
):
    npipe, ndp = lax.axis_size("pipe"), lax.axis_size("dp")
    seg, width = block_input.shape[1:]
    hidden = cm_key.shape[2]
    nq = hidden // width
    length = seg * npipe
    nt = min(TOKENS, seg)
    nm, per = length // nt, seg // nt
    anywhere = pl.BlockSpec(memory_space=pl.ANY)
    vmem = pl.BlockSpec(memory_space=pltpu.VMEM)
    dma = pltpu.SemaphoreType.DMA
    shape = jax.ShapeDtypeStruct
    nb = 6 + nq
    nblocks = 5 + 2 * nq
    xs, gs, small, fin_num, fin_den, fin_rows, ob, gb, turned = pl.pallas_call(
        functools.partial(layers_kernel, npipe),
        name="layers",
        out_shape=[
            shape((nm, nb * nt, width), BF),
            shape((nm, nb * nt, width), BF),
            shape((16, width), F32),
            shape((1, 1, width), F32),
            shape((1, 1, width), F32),
            shape((1, 2, 1, width), F32),
            shape((seg, width), BF),
            shape((seg, width), BF),
            shape((nblocks, width, width), BF),
        ],
        in_specs=[anywhere] * 16,
        out_specs=[anywhere, anywhere, vmem] + [anywhere] * 6,
        scratch_shapes=[
            pltpu.VMEM((nblocks, width, width), BF),
            pltpu.VMEM((2, width), F32),
            pltpu.VMEM((2, width), F32),
            pltpu.VMEM((3, width), F32),
            pltpu.VMEM((2, width), F32),
            pltpu.VMEM((1, width), F32),
            pltpu.VMEM((1, width), F32),
            pltpu.VMEM((1, width), F32),
            pltpu.VMEM((1, width), F32),
            pltpu.VMEM((2, width), F32),
            pltpu.VMEM((nm, nt, width), BF),
            pltpu.VMEM((nm, nt, width), BF),
            *[pltpu.VMEM((nm, nt, width), F32)] * 4,
            *[pltpu.VMEM((nm, nt, width), BF)] * 5,
            pltpu.VMEM((nm, nq * nt, width), BF),
            *[pltpu.VMEM((nm, nt, 1), F32)] * 2,
            *[pltpu.VMEM((nm, 8, width), F32)] * 2,
            pltpu.VMEM((8, width), F32),
            pltpu.VMEM((16, width), F32),
            pltpu.VMEM((2, 6 * nt, width), BF),
            pltpu.VMEM((2, nb * nt, width), BF),
            dma((6 + nblocks,)), dma((6 + nblocks,)), dma((nm,)), dma((nm,)), dma((nm,)), dma((nm,)),
            dma((per,)), dma((per,)), dma((per,)), dma((per,)),
            dma((3,)), dma((3,)), dma((3,)), dma((3,)), dma((2,)), dma((2,)), dma((nm,)), dma((2,)), dma((nblocks,)),
        ],
        compiler_params=pltpu.CompilerParams(collective_id=0, has_side_effects=True, vmem_limit_bytes=VMEM_BYTES),
    )(block_input, cotangent, ln_gain, ln_bias, tm_mix, cm_mix, time_decay, time_first, wkv_num, wkv_den, last_rows,
      tm_in, tm_out, cm_key, cm_value, cm_recept)

    rows_c = width // SPLIT if width % (128 * SPLIT) == 0 else width // 2
    nc, half = nblocks * (width // rows_c), rows_c // 2
    quarter = half // 2
    out, out_small = pl.pallas_call(
        functools.partial(sums_kernel, npipe, ndp // 2),
        name="sums",
        out_shape=[shape((nblocks, width, width), BF), shape((64, width), BF)],
        in_specs=[anywhere, anywhere, vmem],
        out_specs=[anywhere, anywhere],
        scratch_shapes=[
            pltpu.VMEM((2, nm, nt, rows_c), BF),
            pltpu.VMEM((2, nm, nt, width), BF),
            pltpu.VMEM((rows_c, width), F32),
            pltpu.VMEM((2, half, width), BF),
            pltpu.VMEM((nc, half, width), F32),
            pltpu.VMEM((nc, half, width), BF),
            pltpu.VMEM((2, nc, quarter, width), BF),
            pltpu.VMEM((2, nc, quarter, width), BF),
            pltpu.VMEM((32, width), BF),
            pltpu.VMEM((32, width), F32),
            pltpu.VMEM((32, width), BF),
            pltpu.VMEM((2, 16, width), BF),
            pltpu.VMEM((2, 16, width), BF),
            dma((2,)), dma((2,)), dma((2,)), dma((nc + 1,)), dma((2,)), dma((2, nc + 1)), dma((2,)), dma((2, nc + 1)),
            dma((2,)), dma((1,)), dma((9,)), dma((1,)),
        ],
        compiler_params=pltpu.CompilerParams(collective_id=1, has_side_effects=True, vmem_limit_bytes=VMEM_BYTES),
    )(xs, gs, small)

    cuts = 16 if width % 256 == 0 else 2
    step = width // cuts

    def whole(*dims):
        return pl.BlockSpec(dims, lambda c: (0,) * len(dims))

    def part(rows, columns=width):
        return pl.BlockSpec((rows, columns), lambda c: (c, 0))

    def blocks(count, at):
        return pl.BlockSpec((count, step, width), lambda c: (at // count, c, 0))

    wide = pl.pallas_call(
        widen_kernel,
        name="widen",
        grid=(cuts,),
        out_shape=[
            shape((seg, width), F32), shape((seg, width), F32), shape((2, width), F32), shape((2, width), F32),
            shape((3, width), F32), shape((2, width), F32), shape((1, width), F32), shape((1, width), F32),
            shape((3, width, width), F32), shape((1, width, width), F32), shape((width, hidden), F32),
            shape((nq, width, width), F32), shape((1, width, width), F32),
        ],
        in_specs=[
            part(seg // cuts), part(seg // cuts), whole(64, width), blocks(3, 0), blocks(1, 3), blocks(nq, 4),
            blocks(nq, 4 + nq), blocks(1, 4 + 2 * nq),
        ],
        out_specs=[
            part(seg // cuts), part(seg // cuts), whole(2, width), whole(2, width), whole(3, width), whole(2, width),
            whole(1, width), whole(1, width), blocks(3, 0), blocks(1, 0), part(step, hidden), blocks(nq, 0), blocks(1, 0),
        ],
    )(ob, gb, out_small, out, out, out, out, out)
    return (
        wide[0][None],
        wide[1][None],
        wide[2][None],
        wide[3][None],
        wide[4][None],
        wide[5][None],
        wide[6],
        wide[7],
        wide[8][None],
        wide[9],
        wide[10][None],
        wide[11].reshape(1, hidden, width),
        wide[12],
        fin_num,
        fin_den,
        fin_rows,
    )


def solution(mesh):
    args = (
        P("dp", "pipe", None),
        P("pipe", None, None),
        P("pipe", None, None),
        P("pipe", None, None),
        P("pipe", None, None),
        P("pipe", None),
        P("pipe", None),
        P("pipe", None, None, None),
        P("pipe", None, None),
        P("pipe", None, None),
        P("pipe", None, None),
        P("pipe", None, None),
        P("pipe", "dp", None),
        P("pipe", "dp", None),
        P("pipe", None, "dp", None),
        P("dp", "pipe", None),
    )
    outs = (
        P("dp", "pipe", None),
        P("dp", "pipe", None),
        P("pipe", None, None),
        P("pipe", None, None),
        P("pipe", None, None),
        P("pipe", None, None),
        P("pipe", None),
        P("pipe", None),
        P("pipe", None, None, None),
        P("pipe", None, None),
        P("pipe", None, None),
        P("pipe", None, None),
        P("pipe", None, None),
        P("pipe", "dp", None),
        P("pipe", "dp", None),
        P("pipe", None, "dp", None),
    )
    return jax.shard_map(body, mesh=mesh, in_specs=args, out_specs=outs, check_vma=False)
```

```python
import functools

import jax
import jax.numpy as jnp
from jax import lax
from jax.experimental import pallas as pl
from jax.experimental.pallas import tpu as pltpu
from jax.sharding import PartitionSpec as P

ON_CHIP = pltpu.VMEM
MESH = pl.DeviceIdType.MESH
BF, F32 = jnp.bfloat16, jnp.float32
TOKENS = 128
ROWS = 16
SPLIT = 3
LAG = 2
VMEM_BYTES = 62 * 1024 * 1024
SUMS_BYTES = 46 * 1024 * 1024
WIDEN_BYTES = 16 * 1024 * 1024


def position():
    p, i = lax.axis_index("pipe"), lax.axis_index("dp")
    y = lax.div(p, 2)
    k = p - 2 * y
    first = 2 * lax.div(i, 2)
    s = i - first
    return p, i, y, k, first, s, lax.rem(s + y, 2)


def home(layer, k, first):
    y = lax.div(layer, 2)
    return 2 * y + k, first + lax.rem(layer - y, 2)


def local(src, dst, sem):
    return pltpu.make_async_copy(src, dst, sem)


def remote(src, dst, send, recv, p, i):
    return pltpu.make_async_remote_copy(
        src_ref=src, dst_ref=dst, send_sem=send, recv_sem=recv, device_id=(p, i), device_id_type=MESH
    )


def drain(ref, sem):
    pltpu.make_async_copy(ref, ref, sem).wait()


def dot(a, b):
    return lax.dot_general(a, b, (((1,), (0,)), ((), ())), preferred_element_type=F32)


def dot_t(a, b):
    return lax.dot_general(a, b, (((1,), (1,)), ((), ())), preferred_element_type=F32)


def later(v, row):
    at = lax.broadcasted_iota(jnp.int32, v.shape, 0)
    return jnp.where(at == 0, row, pltpu.roll(v, 1, 0))


def earlier(v, row):
    n = v.shape[0]
    at = lax.broadcasted_iota(jnp.int32, v.shape, 0)
    return jnp.where(at == n - 1, row, pltpu.roll(v, n - 1, 0))


def fade_tables(table, rate):
    at = lax.broadcasted_iota(jnp.int32, table.shape[1:], 0)
    for n, by in enumerate((1, 2, 4)):
        fade = jnp.exp(-float(by) * rate)
        table[n] = jnp.where(at >= by, fade, 0.0)
        table[4 + n] = jnp.where(at < 8 - by, fade, 0.0)
    far = at.astype(F32)
    table[3] = jnp.exp(-(far + 1.0) * rate)
    table[7] = jnp.exp(-(8.0 - far) * rate)


def sums_before(v, carry, table):
    for n, by in enumerate((1, 2, 4)):
        v = v + table[n] * pltpu.roll(v, by, 0)
    v = v + table[3] * carry
    return later(v, carry), v[7:8]


def sums_behind(v, carry, table):
    for n, by in enumerate((1, 2, 4)):
        v = v + table[4 + n] * pltpu.roll(v, 8 - by, 0)
    v = v + table[7] * carry
    return earlier(v, carry), v[0:1]


def centred(v):
    c = v - jnp.mean(v, axis=-1, keepdims=True)
    r = lax.rsqrt(jnp.mean(c * c, axis=-1, keepdims=True) + 1e-05)
    return c * r, r


def layers_kernel(
    npipe,
    x_hbm, cot_hbm, gain_hbm, bias_hbm, tmix_hbm, cmix_hbm, decay_hbm, first_hbm, num_hbm, den_hbm, rows_hbm,
    win_hbm, wout_hbm, wck_hbm, wcv_hbm, wcr_hbm,
    xo, go, small, fin_num, fin_den, fin_rows, ob, gb, turned,
    w, gain, bias, tmix, cmix, decay, bonus_s, num_s, den_s, rows_s, inbox, gbox,
    e_s, v_s, n_s, d_s, s_s, xh1, xh2, s2_s, c2_s, relu, r1, r2, car1, car2, back, acc, xst, gst, table, t0, t1, t2, t3,
    w_send, w_recv, in_send, in_recv, g_send, g_recv, x0_send, cot_send, ob_recv, gb_recv,
    st_send, st_recv, fin_send, fin_recv, x_sem, go_sem, relu_sem, turn_out, turn_in,
):
    p, i, y, k, first, s, m_chip = position()
    layer = 2 * y + m_chip
    last = npipe - 1
    nm, nt, width = inbox.shape
    nq = relu.shape[1] // nt
    per = x_hbm.shape[1] // nt
    nblocks = w.shape[0]
    key, val, rec = 4, 4 + nq, 4 + 2 * nq

    weights = [(gain_hbm.at[0], gain), (bias_hbm.at[0], bias), (tmix_hbm, tmix), (cmix_hbm.at[0], cmix),
               (decay_hbm, decay), (first_hbm, bonus_s)]
    base = len(weights)
    order = [0, 1, 2, 3] + [at for q in range(nq) for at in (key + q, val + q)] + [rec]
    source = {rec: wcr_hbm.at[0], 3: wout_hbm.at[0]}
    for c in range(3):
        source[c] = win_hbm.at[0, c]
    for q in range(nq):
        source[key + q] = wck_hbm.at[0, :, q * width : (q + 1) * width]
        source[val + q] = wcv_hbm.at[0, q * width : (q + 1) * width]
    weights += [(source[at], w.at[at]) for at in order]
    place = {at: base + n for n, at in enumerate(order)}
    owner = k == m_chip

    @pl.when(owner)
    def _():
        for a, (src, dst) in enumerate(weights):
            local(src, dst, w_recv.at[a]).start()

    barrier = pltpu.get_barrier_semaphore()
    for step in range(1, 2 * npipe):
        at = lax.rem(2 * p + s + step, 2 * npipe)
        op = lax.div(at, 2)
        pl.semaphore_signal(barrier, inc=1, device_id=(op, first + at - 2 * op), device_id_type=MESH)
    pl.semaphore_wait(barrier, 2 * npipe - 1)

    ip, ii = home(0, s, first)
    in_self = jnp.logical_and(ip == p, ii == i)
    cp, ci = home(last, s, first)
    cot_self = jnp.logical_and(cp == p, ci == i)
    tp, ti = home(p, s, first)
    st_self = jnp.logical_and(tp == p, ti == i)

    def give(src, dst, send, recv, dp, di, mine):
        @pl.when(mine)
        def _():
            local(src, dst, recv).start()

        @pl.when(jnp.logical_not(mine))
        def _():
            remote(src, dst, send, recv, dp, di).start()

    states = ((num_hbm.at[0], num_s), (den_hbm.at[0], den_s), (rows_hbm.at[0, :, 0], rows_s))

    @pl.when(owner)
    def _():
        for a, (src, dst) in enumerate(weights[:base]):
            remote(src, dst, w_send.at[a], w_recv.at[a], 2 * y + 1 - k, i).start()

    for u in range(per):
        give(x_hbm.at[0, pl.ds(u * nt, nt)], inbox.at[p * per + u], x0_send.at[u], in_recv.at[p * per + u], ip, ii, in_self)
    for a, (src, dst) in enumerate(states):
        give(src, dst, st_send.at[a], st_recv.at[a], tp, ti, st_self)

    @pl.when(owner)
    def _():
        for a, (src, dst) in enumerate(weights[base:]):
            remote(src, dst, w_send.at[base + a], w_recv.at[base + a], 2 * y + 1 - k, i).start()

    for u in range(per):
        give(cot_hbm.at[0, pl.ds(u * nt, nt)], gbox.at[p * per + u], cot_send.at[u], g_recv.at[p * per + u], cp, ci, cot_self)

    for a in range(base):
        drain(weights[a][1], w_recv.at[a])
    for a, (src, dst) in enumerate(states):
        drain(dst, st_recv.at[a])
    np_, ni = home(layer + 1, k, first)
    bp, bi = home(layer - 1, k, first)
    rate = jnp.exp(decay[...])
    bonus = jnp.exp(bonus_s[...])
    fade = jnp.exp(-rate)
    fade_tables(table, rate)
    tmixes = [tmix[c] for c in range(3)]
    cmixes = [cmix[c : c + 1] for c in range(2)]

    @pl.when(layer == last)
    def _():
        for at in order:
            drain(w.at[at], w_recv.at[place[at]])

        def turn(at, none):
            slot = lax.rem(at, 2)

            @pl.when(at >= 2)
            def _():
                drain(gst.at[slot, pl.ds(0, width)], turn_out.at[slot])

            gst[slot, 0:width] = w[at].T
            local(gst.at[slot, pl.ds(0, width)], turned.at[at], turn_out.at[slot]).start()
            return none

        lax.fori_loop(0, nblocks, turn, 0)
        for slot in range(2):
            drain(gst.at[slot, pl.ds(0, width)], turn_out.at[slot])

    def forward(m, none, begin=False):
        slot = lax.rem(m, 2)

        def ready(*blocks):
            if begin:

                @pl.when(layer < last)
                def _():
                    for at in blocks:
                        drain(w.at[at], w_recv.at[place[at]])

        if not begin:

            @pl.when(m >= 2)
            def _():
                drain(xst.at[slot], x_sem.at[slot])

        drain(inbox.at[m], in_recv.at[m])
        def norm_mix(rows_of, which, xh_s, r_s, car, mixes, to):
            before = rows_s[which : which + 1]
            car[m, 0:1] = before
            for r in range(0, nt, ROWS):
                here = slice(r, r + ROWS)
                xh, rs = centred(rows_of(here))
                xh_s[m, here] = xh.astype(BF)
                r_s[m, here] = rs
                xn = xh * gain[which : which + 1] + bias[which : which + 1]
                xp = later(xn, before)
                before = xn[ROWS - 1 :]
                d = xn - xp
                for c, mix in enumerate(mixes):
                    xst[slot, (to + c) * nt + r : (to + c) * nt + r + ROWS] = (xp + mix * d).astype(BF)
            rows_s[which : which + 1] = before

        norm_mix(lambda here: inbox[m, here].astype(F32), 0, xh1, r1, car1, tmixes, 0)
        ready(0)
        t0[...] = dot(xst[slot, 0:nt], w[0])
        ready(1)
        v_s[m] = dot(xst[slot, nt : 2 * nt], w[1])
        ready(2)
        t2[...] = dot(xst[slot, 2 * nt : 3 * nt], w[2])
        nc, dc = num_s[...], den_s[...]
        for r in range(0, nt, ROWS):
            here = slice(r, r + ROWS)
            gate = jax.nn.sigmoid(t2[here])
            s_s[m, here] = gate.astype(BF)
            wkv = []
            for r8 in range(r, r + ROWS, 8):
                rows = slice(r8, r8 + 8)
                e = jnp.exp(t0[rows])
                v = v_s[m, rows]
                num, nc = sums_before(e * v, nc, table)
                den, dc = sums_before(e, dc, table)
                e_s[m, rows] = e
                n_s[m, rows] = num
                d_s[m, rows] = den
                b = bonus * e
                wkv.append((num + b * v) / (den + b))
            xst[slot, 3 * nt + r : 3 * nt + r + ROWS] = (gate * jnp.concatenate(wkv, axis=0)).astype(BF)
        num_s[...] = nc
        den_s[...] = dc
        ready(3)
        t1[...] = dot(xst[slot, 3 * nt : 4 * nt], w[3])

        def middle(here):
            mid = inbox[m, here].astype(F32) + t1[here]
            t1[here] = mid
            return mid

        norm_mix(middle, 1, xh2, r2, car2, cmixes, 4)
        squares = []
        for q in range(nq):
            ready(key + q)
            r = jnp.maximum(dot(xst[slot, 4 * nt : 5 * nt], w[key + q]), 0.0)
            relu[m, q * nt : (q + 1) * nt] = r.astype(BF)
            squares.append((r * r).astype(BF))
        ready(rec)
        t2[...] = dot(xst[slot, 5 * nt : 6 * nt], w[rec])
        for q in range(nq):
            ready(val + q)
        t0[...] = dot(jnp.concatenate(squares, axis=1), w[val : val + nq].reshape(nq * width, width))
        for r in range(0, nt, ROWS):
            here = slice(r, r + ROWS)
            gate = jax.nn.sigmoid(t2[here])
            out = t0[here]
            s2_s[m, here] = gate.astype(BF)
            gated = gate * out
            c2_s[m, here] = (gated * (1.0 - gate)).astype(BF)
            inbox[m, here] = (t1[here] + gated).astype(BF)

        @pl.when(layer < last)
        def _():
            remote(inbox.at[m], inbox.at[m], in_send.at[m], in_recv.at[m], np_, ni).start()

        @pl.when(layer == last)
        def _():
            q = lax.div(m, per)
            u = m - q * per
            mine = jnp.logical_and(q == p, first + k == i)
            give(inbox.at[m], ob.at[pl.ds(pl.multiple_of(u * nt, nt), nt)], in_send.at[m], ob_recv.at[u], q, first + k, mine)

        local(xst.at[slot], xo.at[m, pl.ds(0, 6 * nt)], x_sem.at[slot]).start()
        local(relu.at[m], xo.at[m, pl.ds(6 * nt, nq * nt)], relu_sem.at[m]).start()
        return none

    forward(0, 0, True)
    lax.fori_loop(1, nm, forward, 0)

    wanted = [at for q in range(nq) for at in (val + q, key + q)] + [rec, 3, 0, 1, 2]

    @pl.when(layer == last)
    def _():
        for at in wanted:
            local(turned.at[at], w.at[at], turn_in.at[at]).start()

    finals = ((num_s, fin_num.at[0]), (den_s, fin_den.at[0]), (rows_s, fin_rows.at[0, :, 0]))
    fp, fi = layer, first + k
    fin_self = jnp.logical_and(fp == p, fi == i)
    for a, (src, dst) in enumerate(finals):
        give(src, dst, fin_send.at[a], fin_recv.at[a], fp, fi, fin_self)

    @pl.when(layer < last)
    def _():
        def turn(at, none):
            w[at] = w[at].T
            return none

        lax.fori_loop(0, nblocks, turn, 0)

    back[...] = jnp.zeros_like(back)
    acc[...] = jnp.zeros_like(acc)

    def note(at, v):
        acc[at] += v[0:8] + v[8:16]

    def mix_back(m, parts, xh_s, r_s, car, which, mixes, rows_of, put, back_at, acc_mix):
        gain_row, bias_row = gain[which : which + 1], bias[which : which + 1]
        behind = back[back_at : back_at + 1]
        for r in reversed(range(0, nt, ROWS)):
            here = slice(r, r + ROWS)
            xh = xh_s[m, here].astype(F32)
            xn = xh * gain_row + bias_row
            if r == 0:
                before = car[m, 0:1]
            else:
                before = xh_s[m, r - ROWS : r].astype(F32)[ROWS - 1 :] * gain_row + bias_row
            d = xn - later(xn, before)
            own, total = None, None
            for c, part in enumerate(parts):
                g = part[here]
                note(acc_mix + c, g * d)
                mixed = g * mixes[c]
                own = mixed if own is None else own + mixed
                total = g if total is None else total + g
            shifted = total - own
            gx = own + earlier(shifted, behind)
            behind = shifted[0:1]
            note(which, gx * xh)
            note(2 + which, gx)
            gp = gx * gain_row
            centre = jnp.mean(gp, axis=-1, keepdims=True)
            slope = jnp.mean(gp * xh, axis=-1, keepdims=True)
            put(here, rows_of(here) + r_s[m, here] * (gp - centre - xh * slope))
        back[back_at : back_at + 1] = behind

    def backward(step, none, begin=False):
        m = nm - 1 - step
        slot = lax.rem(step, 2)

        def ready(*blocks):
            if begin:

                @pl.when(layer == last)
                def _():
                    for at in blocks:
                        drain(w.at[at], turn_in.at[at])

        if not begin:

            @pl.when(step >= 2)
            def _():
                drain(gst.at[slot], go_sem.at[slot])

        drain(gbox.at[m], g_recv.at[m])
        for r in range(0, nt, ROWS):
            here = slice(r, r + ROWS)
            g = gbox[m, here].astype(F32)
            gst[slot, (4 + nq) * nt + r : (4 + nq) * nt + r + ROWS] = (g * s2_s[m, here].astype(F32)).astype(BF)
            gst[slot, (5 + nq) * nt + r : (5 + nq) * nt + r + ROWS] = (g * c2_s[m, here].astype(F32)).astype(BF)
        keys = []
        for q in range(nq):
            ready(val + q)
            gs = dot(gst[slot, (4 + nq) * nt : (5 + nq) * nt], w[val + q]).astype(BF)
            r = relu[m, q * nt : (q + 1) * nt]
            gk = gs * (r + r)
            gst[slot, (4 + q) * nt : (5 + q) * nt] = gk
            keys.append(gk)
        ready(rec)
        t1[...] = dot(gst[slot, (5 + nq) * nt : (6 + nq) * nt], w[rec])
        for q in range(nq):
            ready(key + q)
        t0[...] = dot(jnp.concatenate(keys, axis=1), w[key : key + nq].reshape(nq * width, width))

        def put_mid(here, v):
            t3[here] = v
            gst[slot, 3 * nt + here.start : 3 * nt + here.stop] = v.astype(BF)

        mix_back(m, (t0, t1), xh2, r2, car2, 1, cmixes, lambda here: gbox[m, here].astype(F32), put_mid, 3, 7)
        ready(3)
        t0[...] = dot(gst[slot, 3 * nt : 4 * nt], w[3])
        nc, dc = back[0:1], back[1:2]
        for r in reversed(range(0, nt, ROWS)):
            here = slice(r, r + ROWS)
            gates = s_s[m, here].astype(F32)
            outs = []
            for r8 in (r + 8, r):
                rows = slice(r8, r8 + 8)
                gg = t0[rows]
                gate = gates[r8 - r : r8 - r + 8]
                e, v, num, den = e_s[m, rows], v_s[m, rows], n_s[m, rows], d_s[m, rows]
                b = bonus * e
                inv = 1.0 / (den + b)
                wkv = (num + b * v) * inv
                gw = gg * gate
                gn = gw * inv
                gr = gw * wkv * (1.0 - gate)
                gd = -gn * wkv
                an, nc = sums_behind(gn, nc, table)
                ad, dc = sums_behind(gd, dc, table)
                now = b * (gn * v + gd)
                acc[10] += now
                acc[9] += an * num + ad * den
                outs.append((e * (an * v + ad) + now, b * gn + e * an, gr))
            for c in range(3):
                both = jnp.concatenate([outs[1][c], outs[0][c]], axis=0)
                gst[slot, c * nt + r : c * nt + r + ROWS] = both.astype(BF)
        back[0:1] = nc
        back[1:2] = dc
        ready(0, 1, 2)
        for c, t in enumerate((t0, t1, t2)):
            t[...] = dot(gst[slot, c * nt : (c + 1) * nt], w[c])

        def put_out(here, v):
            gbox[m, here] = v.astype(BF)

        mix_back(m, (t0, t1, t2), xh1, r1, car1, 0, tmixes, lambda here: t3[here], put_out, 2, 4)

        @pl.when(layer > 0)
        def _():
            remote(gbox.at[m], gbox.at[m], g_send.at[m], g_recv.at[m], bp, bi).start()

        @pl.when(layer == 0)
        def _():
            q = lax.div(m, per)
            u = m - q * per
            mine = jnp.logical_and(q == p, first + k == i)
            give(gbox.at[m], gb.at[pl.ds(pl.multiple_of(u * nt, nt), nt)], g_send.at[m], gb_recv.at[u], q, first + k, mine)

        local(gst.at[slot], go.at[m], go_sem.at[slot]).start()
        return none

    backward(0, 0, True)
    lax.fori_loop(1, nm, backward, 0)
    for at in range(16):
        row = jnp.sum(acc[at], axis=0, keepdims=True)
        small[at : at + 1] = row * (-rate * fade) if at == 9 else row

    for slot in range(min(2, nm)):
        drain(xst.at[slot], x_sem.at[slot])
        drain(gst.at[slot], go_sem.at[slot])

    def finish(m, none):
        drain(relu.at[m], relu_sem.at[m])
        mine = jnp.logical_and(lax.div(m, per) == p, first + k == i)

        @pl.when(jnp.logical_not(jnp.logical_and(layer == last, mine)))
        def _():
            drain(inbox.at[m], in_send.at[m])

        @pl.when(jnp.logical_not(jnp.logical_and(layer == 0, mine)))
        def _():
            drain(gbox.at[m], g_send.at[m])

        return none

    lax.fori_loop(0, nm, finish, 0)
    for u in range(per):
        part = pl.ds(u * nt, nt)
        drain(ob.at[part], ob_recv.at[u])
        drain(gb.at[part], gb_recv.at[u])

        @pl.when(jnp.logical_not(in_self))
        def _():
            drain(x_hbm.at[0, part], x0_send.at[u])

        @pl.when(jnp.logical_not(cot_self))
        def _():
            drain(cot_hbm.at[0, part], cot_send.at[u])

    @pl.when(jnp.logical_not(st_self))
    def _():
        for a, (src, dst) in enumerate(states):
            drain(dst, st_send.at[a])

    @pl.when(jnp.logical_not(fin_self))
    def _():
        for a, (src, dst) in enumerate(finals):
            drain(src, fin_send.at[a])

    for a, (src, dst) in enumerate(finals):
        drain(dst, fin_recv.at[a])

    @pl.when(owner)
    def _():
        for a, (src, dst) in enumerate(weights):
            drain(dst, w_send.at[a])


def sums_kernel(
    npipe, ngroups, x_hbm, g_hbm, small, out, out_small,
    xb, gbuf, dws, xs, own, rx, rr, ag, xs_s, own_s, rx_s, rr_s, ag_s,
    x_sem, g_sem, ex_send, ex_recv, r_send, r_recv, a_send, a_recv, o_send, o_recv, small_send, small_recv,
):
    p, i, y, k, first, s, m_chip = position()
    j = lax.div(i, 2)
    sib = 2 * y + 1 - k
    nc, half, width = own.shape
    quarter = half // 2
    rows_c = 2 * half
    split = width // rows_c
    nm, nt = xb.shape[1:3]
    nq = x_hbm.shape[1] // nt - 6
    hops = (ngroups - 1 - j, j)
    dist = (j, ngroups - 1 - j)
    step_by = (-1, 1)
    dest = 2 * y + m_chip
    other = first + 1 - s

    barrier = pltpu.get_barrier_semaphore()
    for bp, bi in ((sib, i), (p, other), (sib, other)):
        pl.semaphore_signal(barrier, inc=1, device_id=(bp, bi), device_id_type=MESH)

    @pl.when(j > 0)
    def _():
        pl.semaphore_signal(barrier, inc=1, device_id=(p, i - 2), device_id_type=MESH)

    @pl.when(j < ngroups - 1)
    def _():
        pl.semaphore_signal(barrier, inc=1, device_id=(p, i + 2), device_id_type=MESH)

    def blocks(c):
        b = lax.div(c, split)
        xi = jnp.where(b < 4, b, jnp.where(b < 4 + nq, 4, jnp.where(b < 4 + 2 * nq, b - nq + 2, 5)))
        gi = jnp.where(b < 4 + nq, b, jnp.where(b < 4 + 2 * nq, 4 + nq, 5 + nq))
        return b, xi, gi

    def loads(c, slot):
        b, xi, gi = blocks(c)
        part = c - b * split
        cols = pl.ds(pl.multiple_of(part * rows_c, rows_c), rows_c)
        return (
            local(x_hbm.at[:, pl.ds(pl.multiple_of(xi * nt, nt), nt), cols], xb.at[slot], x_sem.at[slot]),
            local(g_hbm.at[:, pl.ds(pl.multiple_of(gi * nt, nt), nt)], gbuf.at[slot], g_sem.at[slot]),
        )

    for copy in loads(0, 0):
        copy.start()

    neighbours = 3 + jnp.where(j > 0, 1, 0) + jnp.where(j < ngroups - 1, 1, 0)
    pl.semaphore_wait(barrier, neighbours)

    def produce(c):
        slot = lax.rem(c, 2)

        @pl.when(c + 1 < nc)
        def _():
            for copy in loads(c + 1, 1 - slot):
                copy.start()

        for copy in loads(c, slot):
            copy.wait()
        b = lax.div(c, split)

        @pl.when(jnp.logical_and(b >= 4 + nq, b < 4 + 2 * nq))
        def _():
            r = xb[slot].astype(F32)
            xb[slot] = (r * r).astype(BF)

        dws[...] = lax.dot_general(
            xb[slot].reshape(nm * nt, rows_c), gbuf[slot].reshape(nm * nt, width), (((0,), (0,)), ((), ())),
            preferred_element_type=F32,
        )

        @pl.when(c >= 2)
        def _():
            drain(xs.at[slot], ex_send.at[slot])

        xs[slot] = dws[pl.ds(pl.multiple_of((1 - k) * half, half), half)].astype(BF)
        remote(xs.at[slot], rx.at[c], ex_send.at[slot], ex_recv.at[c], sib, i).start()
        own[c] = dws[pl.ds(pl.multiple_of(k * half, half), half)]

        @pl.when(c == 0)
        def _():
            n = small.shape[0]
            mine = jnp.where(k == 0, 1.0, 0.0)
            own_s[...] = jnp.zeros_like(own_s)
            xs_s[...] = jnp.zeros_like(xs_s)
            own_s[0:n] = small[...] * mine
            xs_s[0:n] = (small[...] * (1.0 - mine)).astype(BF)
            remote(xs_s, rx_s, small_send.at[0], ex_recv.at[nc], sib, i).start()

    def exchange(c):
        drain(rx.at[c], ex_recv.at[c])
        own[c] = own[c] + rx[c].astype(F32)

        @pl.when(c == 0)
        def _():
            drain(rx_s, ex_recv.at[nc])
            own_s[...] = own_s[...] + rx_s[...].astype(F32)

    def reduce(c, d):
        def one(value, rr_at, ag_at, send, recv):
            @pl.when(hops[d] == 0)
            def _():
                rr_at[...] = value().astype(BF)

            @pl.when(hops[d] > 0)
            def _():
                drain(rr_at, recv)

                @pl.when(dist[d] > 0)
                def _():
                    rr_at[...] = (value() + rr_at[...].astype(F32)).astype(BF)

                @pl.when(dist[d] == 0)
                def _():
                    ag_at[...] = (value() + rr_at[...].astype(F32)).astype(BF)

            @pl.when(dist[d] > 0)
            def _():
                remote(rr_at, rr_at, send, recv, p, i + 2 * step_by[d]).start()

            @pl.when(jnp.logical_and(dist[d] == 0, hops[d] == 0))
            def _():
                ag_at[...] = rr_at[...]

        one(lambda: own[c, d * quarter : (d + 1) * quarter], rr.at[d, c], ag.at[d, c], r_send.at[d], r_recv.at[d, c])

        @pl.when(c == 0)
        def _():
            n = rr_s.shape[1]
            one(lambda: own_s[d * n : (d + 1) * n], rr_s.at[d], ag_s.at[d], small_send.at[1 + d], r_recv.at[d, nc])

    def spread(c, d):
        def one(ag_at, to, forward_send, recv, local_send, far_send, out_recv):
            @pl.when(dist[d] > 0)
            def _():
                drain(ag_at, recv)

            @pl.when(hops[d] > 0)
            def _():
                remote(ag_at, ag_at, forward_send, recv, p, i - 2 * step_by[d]).start()

            remote(ag_at, to, far_send, out_recv, dest, other).start()

            @pl.when(p == dest)
            def _():
                local(ag_at, to, out_recv).start()

            @pl.when(p != dest)
            def _():
                remote(ag_at, to, local_send, out_recv, dest, i).start()

        b = lax.div(c, split)
        row = (c - b * split) * rows_c + k * half + d * quarter
        to = out.at[b, pl.ds(pl.multiple_of(row, quarter), quarter)]
        one(ag.at[d, c], to, a_send.at[d], a_recv.at[d, c], o_send.at[0], o_send.at[1], o_recv.at[0])

        @pl.when(c == 0)
        def _():
            n = rr_s.shape[1]
            to_s = out_small.at[pl.ds(pl.multiple_of(k * 2 * n + d * n, n), n)]
            one(ag_s.at[d], to_s, small_send.at[3 + d], a_recv.at[d, nc], small_send.at[5 + d], small_send.at[7 + d], small_recv.at[0])

    def inside(c, f):
        @pl.when(jnp.logical_and(c >= 0, c < nc))
        def _():
            f(c)

    def step(t, none):
        inside(t, produce)
        inside(t - 1, exchange)
        for d in range(2):
            inside(t - 1 - LAG * hops[d], lambda c: reduce(c, d))
        for d in range(2):
            inside(t - 1 - LAG * (ngroups - 1 + dist[d]), lambda c: spread(c, d))
        return none

    lax.fori_loop(0, nc + 1 + 2 * LAG * (ngroups - 1), step, 0)

    for slot in range(min(2, nc)):
        drain(xs.at[slot], ex_send.at[slot])
    drain(xs_s, small_send.at[0])
    for d in range(2):

        @pl.when(dist[d] > 0)
        def _():
            drain(rr.at[d], r_send.at[d])
            drain(rr_s.at[d], small_send.at[1 + d])

        @pl.when(hops[d] > 0)
        def _():
            drain(ag.at[d], a_send.at[d])
            drain(ag_s.at[d], small_send.at[3 + d])

        @pl.when(p != dest)
        def _():
            drain(ag_s.at[d], small_send.at[5 + d])

        drain(ag_s.at[d], small_send.at[7 + d])

    @pl.when(p != dest)
    def _():
        drain(ag, o_send.at[0])

    drain(ag, o_send.at[1])
    drain(out, o_recv.at[0])
    drain(out_small, small_recv.at[0])


def widen_kernel(
    ob, gb, rows, w, num, den, last,
    out, grad, g_in, g_out, g_key, g_val, g_rec, gain, bias, tmix, cmix, decay, bonus, fin_num, fin_den, fin_rows,
    stage, narrow, wide, sem, in_sem, out_sem,
):
    nblocks, width, _ = w.shape
    slots, step, _ = stage.shape
    nq, cuts = (nblocks - 5) // 2, width // step
    for n, src in enumerate((ob, gb)):
        local(src, narrow.at[n], in_sem.at[n]).start()

    def one(t, none):
        slot = lax.rem(t, slots)
        b = lax.div(t, cuts)
        cut = pl.ds(pl.multiple_of((t - b * cuts) * step, step), step)

        @pl.when(t >= slots)
        def _():
            drain(stage.at[slot], sem.at[slot])

        stage[slot] = w[b, cut].astype(F32)

        @pl.when(b < 3)
        def _():
            local(stage.at[slot], g_in.at[b, cut], sem.at[slot]).start()

        @pl.when(b == 3)
        def _():
            local(stage.at[slot], g_out.at[0, cut], sem.at[slot]).start()

        for q in range(nq):

            @pl.when(b == 4 + q)
            def _():
                local(stage.at[slot], g_key.at[cut, q * width : (q + 1) * width], sem.at[slot]).start()

        @pl.when(jnp.logical_and(b >= 4 + nq, b < 4 + 2 * nq))
        def _():
            local(stage.at[slot], g_val.at[b - 4 - nq, cut], sem.at[slot]).start()

        @pl.when(b == 4 + 2 * nq)
        def _():
            local(stage.at[slot], g_rec.at[0, cut], sem.at[slot]).start()

        return none

    lax.fori_loop(0, nblocks * cuts, one, 0)
    for n, dst in enumerate((out, grad)):
        drain(narrow.at[n], in_sem.at[n])
        wide[n] = narrow[n].astype(F32)
        local(wide.at[n], dst, out_sem.at[n]).start()
    at = 0
    for dst in (gain, bias, tmix, cmix, decay, bonus):
        n = dst.shape[0]
        dst[...] = rows[at : at + n].astype(F32).reshape(dst.shape)
        at += n
    for src, dst in ((num, fin_num), (den, fin_den), (last, fin_rows)):
        dst[...] = src[...]
    for slot in range(slots):
        drain(stage.at[slot], sem.at[slot])
    for n in range(2):
        drain(wide.at[n], out_sem.at[n])


def body(
    block_input, ln_gain, ln_bias, tm_mix, cm_mix, time_decay, time_first, tm_in, tm_out,
    cm_key, cm_value, cm_recept, wkv_num, wkv_den, last_rows, cotangent,
):
    npipe, ndp = lax.axis_size("pipe"), lax.axis_size("dp")
    seg, width = block_input.shape[1:]
    hidden = cm_key.shape[2]
    nq = hidden // width
    length = seg * npipe
    nt = min(TOKENS, seg)
    nm, per = length // nt, seg // nt
    anywhere = pl.BlockSpec(memory_space=pl.ANY)
    vmem = pl.BlockSpec(memory_space=pltpu.VMEM)
    dma = pltpu.SemaphoreType.DMA
    shape = jax.ShapeDtypeStruct
    nb = 6 + nq
    nblocks = 5 + 2 * nq
    xs, gs, small, fin_num, fin_den, fin_rows, ob, gb, turned = pl.pallas_call(
        functools.partial(layers_kernel, npipe),
        name="layers",
        out_shape=[
            shape((nm, nb * nt, width), BF),
            shape((nm, nb * nt, width), BF),
            shape((16, width), F32),
            shape((1, 1, width), F32),
            shape((1, 1, width), F32),
            shape((1, 2, 1, width), F32),
            shape((seg, width), BF),
            shape((seg, width), BF),
            shape((nblocks, width, width), BF),
        ],
        in_specs=[anywhere] * 16,
        out_specs=[anywhere, anywhere, vmem] + [anywhere] * 6,
        scratch_shapes=[
            pltpu.VMEM((nblocks, width, width), BF),
            pltpu.VMEM((2, width), F32),
            pltpu.VMEM((2, width), F32),
            pltpu.VMEM((3, 1, width), F32),
            pltpu.VMEM((2, width), F32),
            pltpu.VMEM((1, width), F32),
            pltpu.VMEM((1, width), F32),
            pltpu.VMEM((1, width), F32),
            pltpu.VMEM((1, width), F32),
            pltpu.VMEM((2, width), F32),
            pltpu.VMEM((nm, nt, width), BF),
            pltpu.VMEM((nm, nt, width), BF),
            *[pltpu.VMEM((nm, nt, width), F32)] * 4,
            *[pltpu.VMEM((nm, nt, width), BF)] * 5,
            pltpu.VMEM((nm, nq * nt, width), BF),
            *[pltpu.VMEM((nm, nt, 1), F32)] * 2,
            *[pltpu.VMEM((nm, 8, width), F32)] * 2,
            pltpu.VMEM((8, width), F32),
            pltpu.VMEM((16, 8, width), F32),
            pltpu.VMEM((2, 6 * nt, width), BF),
            pltpu.VMEM((2, nb * nt, width), BF),
            pltpu.VMEM((8, 8, width), F32),
            *[pltpu.VMEM((nt, width), F32)] * 4,
            dma((6 + nblocks,)), dma((6 + nblocks,)), dma((nm,)), dma((nm,)), dma((nm,)), dma((nm,)),
            dma((per,)), dma((per,)), dma((per,)), dma((per,)),
            dma((3,)), dma((3,)), dma((3,)), dma((3,)), dma((2,)), dma((2,)), dma((nm,)), dma((2,)), dma((nblocks,)),
        ],
        compiler_params=pltpu.CompilerParams(collective_id=0, has_side_effects=True, vmem_limit_bytes=VMEM_BYTES),
    )(block_input, cotangent, ln_gain, ln_bias, jnp.swapaxes(tm_mix, 0, 1), cm_mix, time_decay, time_first, wkv_num, wkv_den, last_rows,
      tm_in, tm_out, cm_key, cm_value, cm_recept)

    rows_c = width // SPLIT if width % (128 * SPLIT) == 0 else width // 2
    nc, half = nblocks * (width // rows_c), rows_c // 2
    quarter = half // 2
    out, out_small = pl.pallas_call(
        functools.partial(sums_kernel, npipe, ndp // 2),
        name="sums",
        out_shape=[ON_CHIP((nblocks, width, width), BF), ON_CHIP((64, width), BF)],
        in_specs=[anywhere, anywhere, vmem],
        out_specs=[vmem, vmem],
        scratch_shapes=[
            pltpu.VMEM((2, nm, nt, rows_c), BF),
            pltpu.VMEM((2, nm, nt, width), BF),
            pltpu.VMEM((rows_c, width), F32),
            pltpu.VMEM((2, half, width), BF),
            pltpu.VMEM((nc, half, width), F32),
            pltpu.VMEM((nc, half, width), BF),
            pltpu.VMEM((2, nc, quarter, width), BF),
            pltpu.VMEM((2, nc, quarter, width), BF),
            pltpu.VMEM((32, width), BF),
            pltpu.VMEM((32, width), F32),
            pltpu.VMEM((32, width), BF),
            pltpu.VMEM((2, 16, width), BF),
            pltpu.VMEM((2, 16, width), BF),
            dma((2,)), dma((2,)), dma((2,)), dma((nc + 1,)), dma((2,)), dma((2, nc + 1)), dma((2,)), dma((2, nc + 1)),
            dma((2,)), dma((1,)), dma((9,)), dma((1,)),
        ],
        compiler_params=pltpu.CompilerParams(collective_id=1, has_side_effects=True, vmem_limit_bytes=SUMS_BYTES),
    )(xs, gs, small)

    in_vmem = pltpu.with_memory_space_constraint(out, pltpu.VMEM)
    wide = pl.pallas_call(
        widen_kernel,
        name="widen",
        out_shape=[
            shape((seg, width), F32), shape((seg, width), F32), shape((3, width, width), F32), shape((1, width, width), F32),
            shape((width, hidden), F32), shape((nq, width, width), F32), shape((1, width, width), F32),
            shape((2, width), F32), shape((2, width), F32), shape((3, 1, width), F32), shape((2, width), F32),
            shape((1, width), F32), shape((1, width), F32),
            shape((1, 1, width), F32), shape((1, 1, width), F32), shape((1, 2, 1, width), F32),
        ],
        in_specs=[anywhere, anywhere, vmem, vmem, vmem, vmem, vmem],
        out_specs=[anywhere] * 7 + [vmem] * 9,
        scratch_shapes=[
            pltpu.VMEM((4, width // 2, width), F32),
            pltpu.VMEM((2, seg, width), BF),
            pltpu.VMEM((2, seg, width), F32),
            dma((4,)), dma((2,)), dma((2,)),
        ],
        compiler_params=pltpu.CompilerParams(vmem_limit_bytes=WIDEN_BYTES),
    )(ob, gb, out_small, in_vmem, fin_num, fin_den, fin_rows)
    return (
        wide[0][None],
        wide[1][None],
        wide[7][None],
        wide[8][None],
        jnp.swapaxes(wide[9], 0, 1),
        wide[10][None],
        wide[11],
        wide[12],
        wide[2][None],
        wide[3],
        wide[4][None],
        wide[5].reshape(1, hidden, width),
        wide[6],
        wide[13],
        wide[14],
        wide[15],
    )


def solution(mesh):
    args = (
        P("dp", "pipe", None),
        P("pipe", None, None),
        P("pipe", None, None),
        P("pipe", None, None),
        P("pipe", None, None),
        P("pipe", None),
        P("pipe", None),
        P("pipe", None, None, None),
        P("pipe", None, None),
        P("pipe", None, None),
        P("pipe", None, None),
        P("pipe", None, None),
        P("pipe", "dp", None),
        P("pipe", "dp", None),
        P("pipe", None, "dp", None),
        P("dp", "pipe", None),
    )
    outs = (
        P("dp", "pipe", None),
        P("dp", "pipe", None),
        P("pipe", None, None),
        P("pipe", None, None),
        P("pipe", None, None),
        P("pipe", None, None),
        P("pipe", None),
        P("pipe", None),
        P("pipe", None, None, None),
        P("pipe", None, None),
        P("pipe", None, None),
        P("pipe", None, None),
        P("pipe", None, None),
        P("pipe", "dp", None),
        P("pipe", "dp", None),
        P("pipe", None, "dp", None),
    )
    return jax.shard_map(body, mesh=mesh, in_specs=args, out_specs=outs, check_vma=False)
```

```python
import functools

import jax
import jax.numpy as jnp
from jax import lax
from jax.experimental import pallas as pl
from jax.experimental.pallas import tpu as pltpu
from jax.sharding import PartitionSpec as P

ON_CHIP = pltpu.VMEM
MESH = pl.DeviceIdType.MESH
BF, F32 = jnp.bfloat16, jnp.float32
TOKENS = 128
ROWS = 16
SPLIT = 3
LAG = 2
GUESTS = 2
GUEST_AT = 4
GUEST_TURN = 20
VMEM_BYTES = 62 * 1024 * 1024
SUMS_BYTES = 47 * 1024 * 1024
WIDEN_BYTES = 16 * 1024 * 1024


def position():
    p, i = lax.axis_index("pipe"), lax.axis_index("dp")
    y = lax.div(p, 2)
    k = p - 2 * y
    first = 2 * lax.div(i, 2)
    s = i - first
    return p, i, y, k, first, s, lax.rem(s + y, 2)


def home(layer, k, first):
    y = lax.div(layer, 2)
    return 2 * y + k, first + lax.rem(layer - y, 2)


def local(src, dst, sem):
    return pltpu.make_async_copy(src, dst, sem)


def remote(src, dst, send, recv, p, i):
    return pltpu.make_async_remote_copy(
        src_ref=src, dst_ref=dst, send_sem=send, recv_sem=recv, device_id=(p, i), device_id_type=MESH
    )


def drain(ref, sem):
    pltpu.make_async_copy(ref, ref, sem).wait()


def dot(a, b):
    return lax.dot_general(a, b, (((1,), (0,)), ((), ())), preferred_element_type=F32)


def dot_t(a, b):
    return lax.dot_general(a, b, (((1,), (1,)), ((), ())), preferred_element_type=F32)


def later(v, row):
    at = lax.broadcasted_iota(jnp.int32, v.shape, 0)
    return jnp.where(at == 0, row, pltpu.roll(v, 1, 0))


def earlier(v, row):
    n = v.shape[0]
    at = lax.broadcasted_iota(jnp.int32, v.shape, 0)
    return jnp.where(at == n - 1, row, pltpu.roll(v, n - 1, 0))


def fade_tables(table, rate):
    at = lax.broadcasted_iota(jnp.int32, table.shape[1:], 0)
    for n, by in enumerate((1, 2, 4)):
        fade = jnp.exp(-float(by) * rate)
        table[n] = jnp.where(at >= by, fade, 0.0)
        table[4 + n] = jnp.where(at < 8 - by, fade, 0.0)
    far = at.astype(F32)
    table[3] = jnp.exp(-(far + 1.0) * rate)
    table[7] = jnp.exp(-(8.0 - far) * rate)


def sums_before(v, carry, table):
    for n, by in enumerate((1, 2, 4)):
        v = v + table[n] * pltpu.roll(v, by, 0)
    v = v + table[3] * carry
    return later(v, carry), v[7:8]


def sums_behind(v, carry, table):
    for n, by in enumerate((1, 2, 4)):
        v = v + table[4 + n] * pltpu.roll(v, 8 - by, 0)
    v = v + table[7] * carry
    return earlier(v, carry), v[0:1]


def centred(v):
    c = v - jnp.mean(v, axis=-1, keepdims=True)
    r = lax.rsqrt(jnp.mean(c * c, axis=-1, keepdims=True) + 1e-05)
    return c * r, r


def layers_kernel(
    npipe,
    x_hbm, cot_hbm, gain_hbm, bias_hbm, tmix_hbm, cmix_hbm, decay_hbm, first_hbm, num_hbm, den_hbm, rows_hbm,
    win_hbm, wout_hbm, wck_hbm, wcv_hbm, wcr_hbm,
    xo, go, small, fin_num, fin_den, fin_rows, ob, gb, turned,
    w, gain, bias, tmix, cmix, decay, bonus_s, num_s, den_s, rows_s, inbox, gbox,
    e_s, v_s, n_s, d_s, s_s, xh1, xh2, s2_s, c2_s, relu, r1, r2, car1, car2, back, acc, xst, gst, table, t0, t1, t2, t3,
    w_send, w_recv, in_send, in_recv, g_send, g_recv, x0_send, cot_send, ob_recv, gb_recv,
    st_send, st_recv, fin_send, fin_recv, x_sem, go_sem, relu_sem, turn_out, turn_in,
):
    p, i, y, k, first, s, m_chip = position()
    layer = 2 * y + m_chip
    last = npipe - 1
    nm, nt, width = inbox.shape
    nq = relu.shape[1] // nt
    per = x_hbm.shape[1] // nt
    nblocks = w.shape[0]
    key, val, rec = 4, 4 + nq, 4 + 2 * nq

    weights = [(gain_hbm.at[0], gain), (bias_hbm.at[0], bias), (tmix_hbm, tmix), (cmix_hbm.at[0], cmix),
               (decay_hbm, decay), (first_hbm, bonus_s)]
    base = len(weights)
    order = [0, 1, 2, 3] + [at for q in range(nq) for at in (key + q, val + q)] + [rec]
    source = {rec: wcr_hbm.at[0], 3: wout_hbm.at[0]}
    for c in range(3):
        source[c] = win_hbm.at[0, c]
    for q in range(nq):
        source[key + q] = wck_hbm.at[0, :, q * width : (q + 1) * width]
        source[val + q] = wcv_hbm.at[0, q * width : (q + 1) * width]
    weights += [(source[at], w.at[at]) for at in order]
    place = {at: base + n for n, at in enumerate(order)}
    owner = k == m_chip

    @pl.when(owner)
    def _():
        for a, (src, dst) in enumerate(weights):
            local(src, dst, w_recv.at[a]).start()

    barrier = pltpu.get_barrier_semaphore()
    for step in range(1, 2 * npipe):
        at = lax.rem(2 * p + s + step, 2 * npipe)
        op = lax.div(at, 2)
        pl.semaphore_signal(barrier, inc=1, device_id=(op, first + at - 2 * op), device_id_type=MESH)
    pl.semaphore_wait(barrier, 2 * npipe - 1)

    ip, ii = home(0, s, first)
    in_self = jnp.logical_and(ip == p, ii == i)
    cp, ci = home(last, s, first)
    cot_self = jnp.logical_and(cp == p, ci == i)
    tp, ti = home(p, s, first)
    st_self = jnp.logical_and(tp == p, ti == i)

    def give(src, dst, send, recv, dp, di, mine):
        @pl.when(mine)
        def _():
            local(src, dst, recv).start()

        @pl.when(jnp.logical_not(mine))
        def _():
            remote(src, dst, send, recv, dp, di).start()

    states = ((num_hbm.at[0], num_s), (den_hbm.at[0], den_s), (rows_hbm.at[0, :, 0], rows_s))

    @pl.when(owner)
    def _():
        for a, (src, dst) in enumerate(weights[:base]):
            remote(src, dst, w_send.at[a], w_recv.at[a], 2 * y + 1 - k, i).start()

    for u in range(per):
        give(x_hbm.at[0, pl.ds(u * nt, nt)], inbox.at[p * per + u], x0_send.at[u], in_recv.at[p * per + u], ip, ii, in_self)
    for a, (src, dst) in enumerate(states):
        give(src, dst, st_send.at[a], st_recv.at[a], tp, ti, st_self)

    @pl.when(owner)
    def _():
        for a, (src, dst) in enumerate(weights[base:]):
            remote(src, dst, w_send.at[base + a], w_recv.at[base + a], 2 * y + 1 - k, i).start()

    for u in range(per):
        give(cot_hbm.at[0, pl.ds(u * nt, nt)], gbox.at[p * per + u], cot_send.at[u], g_recv.at[p * per + u], cp, ci, cot_self)

    for a in range(base):
        drain(weights[a][1], w_recv.at[a])
    for a, (src, dst) in enumerate(states):
        drain(dst, st_recv.at[a])
    np_, ni = home(layer + 1, k, first)
    bp, bi = home(layer - 1, k, first)
    rate = jnp.exp(decay[...])
    bonus = jnp.exp(bonus_s[...])
    fade = jnp.exp(-rate)
    fade_tables(table, rate)
    tmixes = [tmix[c] for c in range(3)]
    cmixes = [cmix[c : c + 1] for c in range(2)]

    @pl.when(layer == last)
    def _():
        for at in order:
            drain(w.at[at], w_recv.at[place[at]])

        def turn(at, none):
            slot = lax.rem(at, 2)

            @pl.when(at >= 2)
            def _():
                drain(gst.at[slot, pl.ds(0, width)], turn_out.at[slot])

            gst[slot, 0:width] = w[at].T
            local(gst.at[slot, pl.ds(0, width)], turned.at[at], turn_out.at[slot]).start()
            return none

        lax.fori_loop(0, nblocks, turn, 0)
        for slot in range(2):
            drain(gst.at[slot, pl.ds(0, width)], turn_out.at[slot])

    def forward(m, none, begin=False):
        slot = lax.rem(m, 2)

        def ready(*blocks):
            if begin:

                @pl.when(layer < last)
                def _():
                    for at in blocks:
                        drain(w.at[at], w_recv.at[place[at]])

        if not begin:

            @pl.when(m >= 2)
            def _():
                drain(xst.at[slot], x_sem.at[slot])

        drain(inbox.at[m], in_recv.at[m])
        def norm_mix(rows_of, which, xh_s, r_s, car, mixes, to):
            before = rows_s[which : which + 1]
            car[m, 0:1] = before
            for r in range(0, nt, ROWS):
                here = slice(r, r + ROWS)
                xh, rs = centred(rows_of(here))
                xh_s[m, here] = xh.astype(BF)
                r_s[m, here] = rs
                xn = xh * gain[which : which + 1] + bias[which : which + 1]
                xp = later(xn, before)
                before = xn[ROWS - 1 :]
                d = xn - xp
                for c, mix in enumerate(mixes):
                    xst[slot, (to + c) * nt + r : (to + c) * nt + r + ROWS] = (xp + mix * d).astype(BF)
            rows_s[which : which + 1] = before

        norm_mix(lambda here: inbox[m, here].astype(F32), 0, xh1, r1, car1, tmixes, 0)
        ready(0)
        t0[...] = dot(xst[slot, 0:nt], w[0])
        ready(1)
        v_s[m] = dot(xst[slot, nt : 2 * nt], w[1])
        ready(2)
        t2[...] = dot(xst[slot, 2 * nt : 3 * nt], w[2])
        nc, dc = num_s[...], den_s[...]
        for r in range(0, nt, ROWS):
            here = slice(r, r + ROWS)
            gate = jax.nn.sigmoid(t2[here])
            s_s[m, here] = gate.astype(BF)
            wkv = []
            for r8 in range(r, r + ROWS, 8):
                rows = slice(r8, r8 + 8)
                e = jnp.exp(t0[rows])
                v = v_s[m, rows]
                num, nc = sums_before(e * v, nc, table)
                den, dc = sums_before(e, dc, table)
                e_s[m, rows] = e
                n_s[m, rows] = num
                d_s[m, rows] = den
                b = bonus * e
                wkv.append((num + b * v) / (den + b))
            xst[slot, 3 * nt + r : 3 * nt + r + ROWS] = (gate * jnp.concatenate(wkv, axis=0)).astype(BF)
        num_s[...] = nc
        den_s[...] = dc
        ready(3)
        t1[...] = dot(xst[slot, 3 * nt : 4 * nt], w[3])

        def middle(here):
            mid = inbox[m, here].astype(F32) + t1[here]
            t1[here] = mid
            return mid

        norm_mix(middle, 1, xh2, r2, car2, cmixes, 4)
        squares = []
        for q in range(nq):
            ready(key + q)
            r = jnp.maximum(dot(xst[slot, 4 * nt : 5 * nt], w[key + q]), 0.0)
            relu[m, q * nt : (q + 1) * nt] = r.astype(BF)
            squares.append((r * r).astype(BF))
        ready(rec)
        t2[...] = dot(xst[slot, 5 * nt : 6 * nt], w[rec])
        for q in range(nq):
            ready(val + q)
        t0[...] = dot(jnp.concatenate(squares, axis=1), w[val : val + nq].reshape(nq * width, width))
        for r in range(0, nt, ROWS):
            here = slice(r, r + ROWS)
            gate = jax.nn.sigmoid(t2[here])
            out = t0[here]
            s2_s[m, here] = gate.astype(BF)
            gated = gate * out
            c2_s[m, here] = (gated * (1.0 - gate)).astype(BF)
            inbox[m, here] = (t1[here] + gated).astype(BF)

        @pl.when(layer < last)
        def _():
            remote(inbox.at[m], inbox.at[m], in_send.at[m], in_recv.at[m], np_, ni).start()

        @pl.when(layer == last)
        def _():
            q = lax.div(m, per)
            u = m - q * per
            mine = jnp.logical_and(q == p, first + k == i)
            give(inbox.at[m], ob.at[pl.ds(pl.multiple_of(u * nt, nt), nt)], in_send.at[m], ob_recv.at[u], q, first + k, mine)

        local(xst.at[slot], xo.at[m, pl.ds(0, 6 * nt)], x_sem.at[slot]).start()
        local(relu.at[m], xo.at[m, pl.ds(6 * nt, nq * nt)], relu_sem.at[m]).start()
        return none

    forward(0, 0, True)
    lax.fori_loop(1, nm, forward, 0)

    wanted = [at for q in range(nq) for at in (val + q, key + q)] + [rec, 3, 0, 1, 2]

    @pl.when(layer == last)
    def _():
        for at in wanted:
            local(turned.at[at], w.at[at], turn_in.at[at]).start()

    finals = ((num_s, fin_num.at[0]), (den_s, fin_den.at[0]), (rows_s, fin_rows.at[0, :, 0]))
    fp, fi = layer, first + k
    fin_self = jnp.logical_and(fp == p, fi == i)
    for a, (src, dst) in enumerate(finals):
        give(src, dst, fin_send.at[a], fin_recv.at[a], fp, fi, fin_self)

    @pl.when(layer < last)
    def _():
        def turn(at, none):
            w[at] = w[at].T
            return none

        lax.fori_loop(0, nblocks, turn, 0)

    back[...] = jnp.zeros_like(back)
    acc[...] = jnp.zeros_like(acc)

    def note(at, v):
        acc[at] += v[0:8] + v[8:16]

    def mix_back(m, parts, xh_s, r_s, car, which, mixes, rows_of, put, back_at, acc_mix):
        gain_row, bias_row = gain[which : which + 1], bias[which : which + 1]
        behind = back[back_at : back_at + 1]
        for r in reversed(range(0, nt, ROWS)):
            here = slice(r, r + ROWS)
            xh = xh_s[m, here].astype(F32)
            xn = xh * gain_row + bias_row
            if r == 0:
                before = car[m, 0:1]
            else:
                before = xh_s[m, r - ROWS : r].astype(F32)[ROWS - 1 :] * gain_row + bias_row
            d = xn - later(xn, before)
            own, total = None, None
            for c, part in enumerate(parts):
                g = part[here]
                note(acc_mix + c, g * d)
                mixed = g * mixes[c]
                own = mixed if own is None else own + mixed
                total = g if total is None else total + g
            shifted = total - own
            gx = own + earlier(shifted, behind)
            behind = shifted[0:1]
            note(which, gx * xh)
            note(2 + which, gx)
            gp = gx * gain_row
            centre = jnp.mean(gp, axis=-1, keepdims=True)
            slope = jnp.mean(gp * xh, axis=-1, keepdims=True)
            put(here, rows_of(here) + r_s[m, here] * (gp - centre - xh * slope))
        back[back_at : back_at + 1] = behind

    def backward(step, none, begin=False):
        m = nm - 1 - step
        slot = lax.rem(step, 2)

        def ready(*blocks):
            if begin:

                @pl.when(layer == last)
                def _():
                    for at in blocks:
                        drain(w.at[at], turn_in.at[at])

        if not begin:

            @pl.when(step >= 2)
            def _():
                drain(gst.at[slot], go_sem.at[slot])

        drain(gbox.at[m], g_recv.at[m])
        for r in range(0, nt, ROWS):
            here = slice(r, r + ROWS)
            g = gbox[m, here].astype(F32)
            gst[slot, (4 + nq) * nt + r : (4 + nq) * nt + r + ROWS] = (g * s2_s[m, here].astype(F32)).astype(BF)
            gst[slot, (5 + nq) * nt + r : (5 + nq) * nt + r + ROWS] = (g * c2_s[m, here].astype(F32)).astype(BF)
        keys = []
        for q in range(nq):
            ready(val + q)
            gs = dot(gst[slot, (4 + nq) * nt : (5 + nq) * nt], w[val + q]).astype(BF)
            r = relu[m, q * nt : (q + 1) * nt]
            gk = gs * (r + r)
            gst[slot, (4 + q) * nt : (5 + q) * nt] = gk
            keys.append(gk)
        ready(rec)
        t1[...] = dot(gst[slot, (5 + nq) * nt : (6 + nq) * nt], w[rec])
        for q in range(nq):
            ready(key + q)
        t0[...] = dot(jnp.concatenate(keys, axis=1), w[key : key + nq].reshape(nq * width, width))

        def put_mid(here, v):
            t3[here] = v
            gst[slot, 3 * nt + here.start : 3 * nt + here.stop] = v.astype(BF)

        mix_back(m, (t0, t1), xh2, r2, car2, 1, cmixes, lambda here: gbox[m, here].astype(F32), put_mid, 3, 7)
        ready(3)
        t0[...] = dot(gst[slot, 3 * nt : 4 * nt], w[3])
        nc, dc = back[0:1], back[1:2]
        for r in reversed(range(0, nt, ROWS)):
            here = slice(r, r + ROWS)
            gates = s_s[m, here].astype(F32)
            outs = []
            for r8 in (r + 8, r):
                rows = slice(r8, r8 + 8)
                gg = t0[rows]
                gate = gates[r8 - r : r8 - r + 8]
                e, v, num, den = e_s[m, rows], v_s[m, rows], n_s[m, rows], d_s[m, rows]
                b = bonus * e
                inv = 1.0 / (den + b)
                wkv = (num + b * v) * inv
                gw = gg * gate
                gn = gw * inv
                gr = gw * wkv * (1.0 - gate)
                gd = -gn * wkv
                an, nc = sums_behind(gn, nc, table)
                ad, dc = sums_behind(gd, dc, table)
                now = b * (gn * v + gd)
                acc[10] += now
                acc[9] += an * num + ad * den
                outs.append((e * (an * v + ad) + now, b * gn + e * an, gr))
            for c in range(3):
                both = jnp.concatenate([outs[1][c], outs[0][c]], axis=0)
                gst[slot, c * nt + r : c * nt + r + ROWS] = both.astype(BF)
        back[0:1] = nc
        back[1:2] = dc
        ready(0, 1, 2)
        for c, t in enumerate((t0, t1, t2)):
            t[...] = dot(gst[slot, c * nt : (c + 1) * nt], w[c])

        def put_out(here, v):
            gbox[m, here] = v.astype(BF)

        mix_back(m, (t0, t1, t2), xh1, r1, car1, 0, tmixes, lambda here: t3[here], put_out, 2, 4)

        @pl.when(layer > 0)
        def _():
            remote(gbox.at[m], gbox.at[m], g_send.at[m], g_recv.at[m], bp, bi).start()

        @pl.when(layer == 0)
        def _():
            q = lax.div(m, per)
            u = m - q * per
            mine = jnp.logical_and(q == p, first + k == i)
            give(gbox.at[m], gb.at[pl.ds(pl.multiple_of(u * nt, nt), nt)], g_send.at[m], gb_recv.at[u], q, first + k, mine)

        local(gst.at[slot], go.at[m], go_sem.at[slot]).start()
        return none

    backward(0, 0, True)
    lax.fori_loop(1, nm, backward, 0)
    for at in range(16):
        row = jnp.sum(acc[at], axis=0, keepdims=True)
        small[at : at + 1] = row * (-rate * fade) if at == 9 else row

    for slot in range(min(2, nm)):
        drain(xst.at[slot], x_sem.at[slot])
        drain(gst.at[slot], go_sem.at[slot])

    def finish(m, none):
        drain(relu.at[m], relu_sem.at[m])
        mine = jnp.logical_and(lax.div(m, per) == p, first + k == i)

        @pl.when(jnp.logical_not(jnp.logical_and(layer == last, mine)))
        def _():
            drain(inbox.at[m], in_send.at[m])

        @pl.when(jnp.logical_not(jnp.logical_and(layer == 0, mine)))
        def _():
            drain(gbox.at[m], g_send.at[m])

        return none

    lax.fori_loop(0, nm, finish, 0)
    for u in range(per):
        part = pl.ds(u * nt, nt)
        drain(ob.at[part], ob_recv.at[u])
        drain(gb.at[part], gb_recv.at[u])

        @pl.when(jnp.logical_not(in_self))
        def _():
            drain(x_hbm.at[0, part], x0_send.at[u])

        @pl.when(jnp.logical_not(cot_self))
        def _():
            drain(cot_hbm.at[0, part], cot_send.at[u])

    @pl.when(jnp.logical_not(st_self))
    def _():
        for a, (src, dst) in enumerate(states):
            drain(dst, st_send.at[a])

    @pl.when(jnp.logical_not(fin_self))
    def _():
        for a, (src, dst) in enumerate(finals):
            drain(src, fin_send.at[a])

    for a, (src, dst) in enumerate(finals):
        drain(dst, fin_recv.at[a])

    @pl.when(owner)
    def _():
        for a, (src, dst) in enumerate(weights):
            drain(dst, w_send.at[a])


def sums_kernel(
    npipe, ngroups, guests, x_hbm, g_hbm, small, out, out_small,
    xb, gbuf, dws, xs, own, rx, rr, ag, xs_s, own_s, rx_s, rr_s, ag_s, gx, gsrc,
    x_sem, g_sem, ex_send, ex_recv, r_send, r_recv, a_send, a_recv, o_send, o_recv, small_send, small_recv,
    gx_send, gx_recv, guest_send, guest_ready,
):
    p, i, y, k, first, s, m_chip = position()
    j = lax.div(i, 2)
    sib = 2 * y + 1 - k
    half, width = own.shape[1:]
    nc = rx.shape[0]
    low, high = GUEST_AT, GUEST_AT + guests
    lower = y == 0
    upper = y == 1
    quarter = half // 2
    rows_c = 2 * half
    split = width // rows_c
    nm, nt = xb.shape[1:3]
    nq = x_hbm.shape[1] // nt - 6
    hops = (ngroups - 1 - j, j)
    dist = (j, ngroups - 1 - j)
    step_by = (-1, 1)
    dest = 2 * y + m_chip
    other = first + 1 - s

    barrier = pltpu.get_barrier_semaphore()
    for bp, bi in ((sib, i), (p, other), (sib, other)):
        pl.semaphore_signal(barrier, inc=1, device_id=(bp, bi), device_id_type=MESH)

    @pl.when(j > 0)
    def _():
        pl.semaphore_signal(barrier, inc=1, device_id=(p, i - 2), device_id_type=MESH)

    @pl.when(j < ngroups - 1)
    def _():
        pl.semaphore_signal(barrier, inc=1, device_id=(p, i + 2), device_id_type=MESH)

    greeted = 3 + jnp.where(j > 0, 1, 0) + jnp.where(j < ngroups - 1, 1, 0)
    if guests:

        @pl.when(upper)
        def _():
            for bp, bi in ((k, i), (s, first), (s, first + 1)):
                pl.semaphore_signal(barrier, inc=1, device_id=(bp, bi), device_id_type=MESH)

        greeted = greeted + jnp.where(lower, 3, 0)

    def enter():
        pl.semaphore_wait(barrier, greeted)
        if guests:

            @pl.when(lower)
            def _():
                for op in (2, 3):
                    pl.semaphore_signal(guest_ready, inc=1, device_id=(op, first + k), device_id_type=MESH)

    def blocks(c):
        b = lax.div(c, split)
        xi = jnp.where(b < 4, b, jnp.where(b < 4 + nq, 4, jnp.where(b < 4 + 2 * nq, b - nq + 2, 5)))
        gi = jnp.where(b < 4 + nq, b, jnp.where(b < 4 + 2 * nq, 4 + nq, 5 + nq))
        return b, xi, gi

    def loads(c, slot):
        b, xi, gi = blocks(c)
        part = c - b * split
        cols = pl.ds(pl.multiple_of(part * rows_c, rows_c), rows_c)
        return (
            local(x_hbm.at[:, pl.ds(pl.multiple_of(xi * nt, nt), nt), cols], xb.at[slot], x_sem.at[slot]),
            local(g_hbm.at[:, pl.ds(pl.multiple_of(gi * nt, nt), nt)], gbuf.at[slot], g_sem.at[slot]),
        )

    for copy in loads(0, 0):
        copy.start()

    def produce(c):
        slot = lax.rem(c, 2)

        @pl.when(c + 1 < nc)
        def _():
            for copy in loads(c + 1, 1 - slot):
                copy.start()

        for copy in loads(c, slot):
            copy.wait()
        b = lax.div(c, split)

        @pl.when(jnp.logical_and(b >= 4 + nq, b < 4 + 2 * nq))
        def _():
            r = xb[slot].astype(F32)
            xb[slot] = (r * r).astype(BF)

        dws[...] = lax.dot_general(
            xb[slot].reshape(nm * nt, rows_c), gbuf[slot].reshape(nm * nt, width), (((0,), (0,)), ((), ())),
            preferred_element_type=F32,
        )

        @pl.when(c >= 2)
        def _():
            drain(xs.at[slot], ex_send.at[slot])

        @pl.when(c == 0)
        def _():
            enter()

        xs[slot] = dws[pl.ds(pl.multiple_of((1 - k) * half, half), half)].astype(BF)
        remote(xs.at[slot], rx.at[c], ex_send.at[slot], ex_recv.at[c], sib, i).start()
        own[c] = dws[pl.ds(pl.multiple_of(k * half, half), half)]

        @pl.when(c == 0)
        def _():
            n = small.shape[0]
            mine = jnp.where(k == 0, 1.0, 0.0)
            own_s[...] = jnp.zeros_like(own_s)
            xs_s[...] = jnp.zeros_like(xs_s)
            own_s[0:n] = small[...] * mine
            xs_s[0:n] = (small[...] * (1.0 - mine)).astype(BF)
            remote(xs_s, rx_s, small_send.at[0], ex_recv.at[nc], sib, i).start()

    def welcome(c):
        @pl.when(c == nc)
        def _():
            pl.semaphore_wait(guest_ready, 2)

        drain(gx.at[c - nc], gx_recv.at[c - nc])
        own[c] = gx[c - nc].astype(F32)

    def exchange(c):
        drain(rx.at[c], ex_recv.at[c])
        own[c] = own[c] + rx[c].astype(F32)
        if guests:

            @pl.when(jnp.logical_and(lower, jnp.logical_and(c >= low, c < high)))
            def _():
                gsrc[c - low] = own[c].astype(BF)
                remote(gsrc.at[c - low], gx.at[c - low], gx_send.at[0], gx_recv.at[c - low], p + 2, i).start()

        @pl.when(c == 0)
        def _():
            drain(rx_s, ex_recv.at[nc])
            own_s[...] = own_s[...] + rx_s[...].astype(F32)

    def reduce(c, d):
        def one(value, rr_at, ag_at, send, recv):
            @pl.when(hops[d] == 0)
            def _():
                rr_at[...] = value().astype(BF)

            @pl.when(hops[d] > 0)
            def _():
                drain(rr_at, recv)

                @pl.when(dist[d] > 0)
                def _():
                    rr_at[...] = (value() + rr_at[...].astype(F32)).astype(BF)

                @pl.when(dist[d] == 0)
                def _():
                    ag_at[...] = (value() + rr_at[...].astype(F32)).astype(BF)

            @pl.when(dist[d] > 0)
            def _():
                remote(rr_at, rr_at, send, recv, p, i + 2 * step_by[d]).start()

            @pl.when(jnp.logical_and(dist[d] == 0, hops[d] == 0))
            def _():
                ag_at[...] = rr_at[...]

        one(lambda: own[c, d * quarter : (d + 1) * quarter], rr.at[d, c], ag.at[d, c], r_send.at[d], r_recv.at[d, c])

        @pl.when(c == 0)
        def _():
            n = rr_s.shape[1]
            one(lambda: own_s[d * n : (d + 1) * n], rr_s.at[d], ag_s.at[d], small_send.at[1 + d], r_recv.at[d, nc + guests])

    def spread(c, d):
        def come(ag_at, forward_send, recv):
            @pl.when(dist[d] > 0)
            def _():
                drain(ag_at, recv)

            @pl.when(hops[d] > 0)
            def _():
                remote(ag_at, ag_at, forward_send, recv, p, i - 2 * step_by[d]).start()

        def one(ag_at, to, forward_send, recv, local_send, far_send, out_recv):
            come(ag_at, forward_send, recv)
            remote(ag_at, to, far_send, out_recv, dest, other).start()

            @pl.when(p == dest)
            def _():
                local(ag_at, to, out_recv).start()

            @pl.when(p != dest)
            def _():
                remote(ag_at, to, local_send, out_recv, dest, i).start()

        def place(c):
            b = lax.div(c, split)
            row = (c - b * split) * rows_c + k * half + d * quarter
            return out.at[b, pl.ds(pl.multiple_of(row, quarter), quarter)]

        def own_chunk():
            one(ag.at[d, c], place(c), a_send.at[d], a_recv.at[d, c], o_send.at[0], o_send.at[1], o_recv.at[0])

        if guests:
            pl.when(c < nc)(own_chunk)

            @pl.when(c >= nc)
            def _():
                come(ag.at[d, c], a_send.at[d], a_recv.at[d, c])
                to = place(c - nc + low)
                remote(ag.at[d, c], to, guest_send.at[0], o_recv.at[0], s, i).start()
                remote(ag.at[d, c], to, guest_send.at[1], o_recv.at[0], s, other).start()
        else:
            own_chunk()

        @pl.when(c == 0)
        def _():
            n = rr_s.shape[1]
            to_s = out_small.at[pl.ds(pl.multiple_of(k * 2 * n + d * n, n), n)]
            one(ag_s.at[d], to_s, small_send.at[3 + d], a_recv.at[d, nc + guests], small_send.at[5 + d], small_send.at[7 + d], small_recv.at[0])

    def turn(u, own_work, guest_work=None):
        if not guests:

            @pl.when(jnp.logical_and(u >= 0, u < nc))
            def _():
                own_work(u)

            return
        at = min(GUEST_TURN, nc)
        c = jnp.where(u < at, u, jnp.where(u < at + guests, nc + u - at, u - guests))
        c = jnp.where(upper, c, u)
        mine = jnp.logical_and(u >= 0, u < nc + jnp.where(upper, guests, 0))
        if guest_work is not own_work:

            @pl.when(jnp.logical_and(mine, c < nc))
            def _():
                own_work(c)

            if guest_work is not None:

                @pl.when(jnp.logical_and(mine, c >= nc))
                def _():
                    guest_work(c)

        else:
            away = jnp.logical_and(lower, jnp.logical_and(c >= low, c < high))

            @pl.when(jnp.logical_and(mine, jnp.logical_not(away)))
            def _():
                own_work(c)

    def step(t, none):
        turn(t, produce)
        turn(t - 1, exchange, welcome)
        for d in range(2):
            work = functools.partial(reduce, d=d)
            turn(t - 1 - LAG * hops[d], work, work)
        for d in range(2):
            work = functools.partial(spread, d=d)
            turn(t - 1 - LAG * (ngroups - 1 + dist[d]), work, work)
        return none

    lax.fori_loop(0, nc + guests + 1 + 2 * LAG * (ngroups - 1), step, 0)

    def settle(ref, sem):
        if not guests:
            drain(ref, sem)
            return

        @pl.when(upper)
        def _():
            drain(ref, sem)

        @pl.when(lower)
        def _():
            drain(ref.at[pl.ds(0, low)], sem)
            drain(ref.at[pl.ds(high, nc - high)], sem)

    def settle_own(ref, sem):
        if not guests:
            drain(ref, sem)
            return
        drain(ref.at[pl.ds(0, low)], sem)
        drain(ref.at[pl.ds(high, nc - high)], sem)

        @pl.when(upper)
        def _():
            drain(ref.at[pl.ds(low, guests)], sem)

    for slot in range(min(2, nc)):
        drain(xs.at[slot], ex_send.at[slot])
    drain(xs_s, small_send.at[0])
    for d in range(2):

        @pl.when(dist[d] > 0)
        def _():
            settle(rr.at[d], r_send.at[d])
            drain(rr_s.at[d], small_send.at[1 + d])

        @pl.when(hops[d] > 0)
        def _():
            settle(ag.at[d], a_send.at[d])
            drain(ag_s.at[d], small_send.at[3 + d])

        @pl.when(p != dest)
        def _():
            drain(ag_s.at[d], small_send.at[5 + d])

        drain(ag_s.at[d], small_send.at[7 + d])

    for d in range(2):

        @pl.when(p != dest)
        def _():
            settle_own(ag.at[d], o_send.at[0])

        settle_own(ag.at[d], o_send.at[1])
    if guests:

        @pl.when(lower)
        def _():
            drain(gsrc, gx_send.at[0])

        @pl.when(upper)
        def _():
            for d in range(2):
                drain(ag.at[d, pl.ds(nc, guests)], guest_send.at[0])
                drain(ag.at[d, pl.ds(nc, guests)], guest_send.at[1])

    drain(out, o_recv.at[0])
    drain(out_small, small_recv.at[0])


def widen_kernel(
    ob, gb, rows, w, num, den, last,
    out, grad, g_in, g_out, g_key, g_val, g_rec, gain, bias, tmix, cmix, decay, bonus, fin_num, fin_den, fin_rows,
    stage, narrow, wide, sem, in_sem, out_sem,
):
    nblocks, width, _ = w.shape
    slots, step, _ = stage.shape
    nq, cuts = (nblocks - 5) // 2, width // step
    for n, src in enumerate((ob, gb)):
        local(src, narrow.at[n], in_sem.at[n]).start()

    def one(t, none):
        slot = lax.rem(t, slots)
        b = lax.div(t, cuts)
        cut = pl.ds(pl.multiple_of((t - b * cuts) * step, step), step)

        @pl.when(t >= slots)
        def _():
            drain(stage.at[slot], sem.at[slot])

        stage[slot] = w[b, cut].astype(F32)

        @pl.when(b < 3)
        def _():
            local(stage.at[slot], g_in.at[b, cut], sem.at[slot]).start()

        @pl.when(b == 3)
        def _():
            local(stage.at[slot], g_out.at[0, cut], sem.at[slot]).start()

        for q in range(nq):

            @pl.when(b == 4 + q)
            def _():
                local(stage.at[slot], g_key.at[cut, q * width : (q + 1) * width], sem.at[slot]).start()

        @pl.when(jnp.logical_and(b >= 4 + nq, b < 4 + 2 * nq))
        def _():
            local(stage.at[slot], g_val.at[b - 4 - nq, cut], sem.at[slot]).start()

        @pl.when(b == 4 + 2 * nq)
        def _():
            local(stage.at[slot], g_rec.at[0, cut], sem.at[slot]).start()

        return none

    lax.fori_loop(0, nblocks * cuts, one, 0)
    for n, dst in enumerate((out, grad)):
        drain(narrow.at[n], in_sem.at[n])
        wide[n] = narrow[n].astype(F32)
        local(wide.at[n], dst, out_sem.at[n]).start()
    at = 0
    for dst in (gain, bias, tmix, cmix, decay, bonus):
        n = dst.shape[0]
        dst[...] = rows[at : at + n].astype(F32).reshape(dst.shape)
        at += n
    for src, dst in ((num, fin_num), (den, fin_den), (last, fin_rows)):
        dst[...] = src[...]
    for slot in range(slots):
        drain(stage.at[slot], sem.at[slot])
    for n in range(2):
        drain(wide.at[n], out_sem.at[n])


def body(
    block_input, ln_gain, ln_bias, tm_mix, cm_mix, time_decay, time_first, tm_in, tm_out,
    cm_key, cm_value, cm_recept, wkv_num, wkv_den, last_rows, cotangent,
):
    npipe, ndp = lax.axis_size("pipe"), lax.axis_size("dp")
    seg, width = block_input.shape[1:]
    hidden = cm_key.shape[2]
    nq = hidden // width
    length = seg * npipe
    nt = min(TOKENS, seg)
    nm, per = length // nt, seg // nt
    anywhere = pl.BlockSpec(memory_space=pl.ANY)
    vmem = pl.BlockSpec(memory_space=pltpu.VMEM)
    dma = pltpu.SemaphoreType.DMA
    shape = jax.ShapeDtypeStruct
    nb = 6 + nq
    nblocks = 5 + 2 * nq
    xs, gs, small, fin_num, fin_den, fin_rows, ob, gb, turned = pl.pallas_call(
        functools.partial(layers_kernel, npipe),
        name="layers",
        out_shape=[
            shape((nm, nb * nt, width), BF),
            shape((nm, nb * nt, width), BF),
            shape((16, width), F32),
            shape((1, 1, width), F32),
            shape((1, 1, width), F32),
            shape((1, 2, 1, width), F32),
            shape((seg, width), BF),
            shape((seg, width), BF),
            shape((nblocks, width, width), BF),
        ],
        in_specs=[anywhere] * 16,
        out_specs=[anywhere, anywhere, vmem] + [anywhere] * 6,
        scratch_shapes=[
            pltpu.VMEM((nblocks, width, width), BF),
            pltpu.VMEM((2, width), F32),
            pltpu.VMEM((2, width), F32),
            pltpu.VMEM((3, 1, width), F32),
            pltpu.VMEM((2, width), F32),
            pltpu.VMEM((1, width), F32),
            pltpu.VMEM((1, width), F32),
            pltpu.VMEM((1, width), F32),
            pltpu.VMEM((1, width), F32),
            pltpu.VMEM((2, width), F32),
            pltpu.VMEM((nm, nt, width), BF),
            pltpu.VMEM((nm, nt, width), BF),
            *[pltpu.VMEM((nm, nt, width), F32)] * 4,
            *[pltpu.VMEM((nm, nt, width), BF)] * 5,
            pltpu.VMEM((nm, nq * nt, width), BF),
            *[pltpu.VMEM((nm, nt, 1), F32)] * 2,
            *[pltpu.VMEM((nm, 8, width), F32)] * 2,
            pltpu.VMEM((8, width), F32),
            pltpu.VMEM((16, 8, width), F32),
            pltpu.VMEM((2, 6 * nt, width), BF),
            pltpu.VMEM((2, nb * nt, width), BF),
            pltpu.VMEM((8, 8, width), F32),
            *[pltpu.VMEM((nt, width), F32)] * 4,
            dma((6 + nblocks,)), dma((6 + nblocks,)), dma((nm,)), dma((nm,)), dma((nm,)), dma((nm,)),
            dma((per,)), dma((per,)), dma((per,)), dma((per,)),
            dma((3,)), dma((3,)), dma((3,)), dma((3,)), dma((2,)), dma((2,)), dma((nm,)), dma((2,)), dma((nblocks,)),
        ],
        compiler_params=pltpu.CompilerParams(collective_id=0, has_side_effects=True, vmem_limit_bytes=VMEM_BYTES),
    )(block_input, cotangent, ln_gain, ln_bias, jnp.swapaxes(tm_mix, 0, 1), cm_mix, time_decay, time_first, wkv_num, wkv_den, last_rows,
      tm_in, tm_out, cm_key, cm_value, cm_recept)

    rows_c = width // SPLIT if width % (128 * SPLIT) == 0 else width // 2
    nc, half = nblocks * (width // rows_c), rows_c // 2
    quarter = half // 2
    guests = GUESTS if npipe == 4 else 0
    all_c = nc + guests
    out, out_small = pl.pallas_call(
        functools.partial(sums_kernel, npipe, ndp // 2, guests),
        name="sums",
        out_shape=[ON_CHIP((nblocks, width, width), BF), ON_CHIP((64, width), BF)],
        in_specs=[anywhere, anywhere, vmem],
        out_specs=[vmem, vmem],
        scratch_shapes=[
            pltpu.VMEM((2, nm, nt, rows_c), BF),
            pltpu.VMEM((2, nm, nt, width), BF),
            pltpu.VMEM((rows_c, width), F32),
            pltpu.VMEM((2, half, width), BF),
            pltpu.VMEM((all_c, half, width), F32),
            pltpu.VMEM((nc, half, width), BF),
            pltpu.VMEM((2, all_c, quarter, width), BF),
            pltpu.VMEM((2, all_c, quarter, width), BF),
            pltpu.VMEM((32, width), BF),
            pltpu.VMEM((32, width), F32),
            pltpu.VMEM((32, width), BF),
            pltpu.VMEM((2, 16, width), BF),
            pltpu.VMEM((2, 16, width), BF),
            pltpu.VMEM((max(guests, 1), half, width), BF),
            pltpu.VMEM((max(guests, 1), half, width), BF),
            dma((2,)), dma((2,)), dma((2,)), dma((nc + 1,)), dma((2,)), dma((2, all_c + 1)), dma((2,)), dma((2, all_c + 1)),
            dma((2,)), dma((1,)), dma((9,)), dma((1,)), dma((1,)), dma((max(guests, 1),)), dma((2,)), pltpu.SemaphoreType.REGULAR,
        ],
        compiler_params=pltpu.CompilerParams(collective_id=1, has_side_effects=True, vmem_limit_bytes=SUMS_BYTES),
    )(xs, gs, small)

    in_vmem = pltpu.with_memory_space_constraint(out, pltpu.VMEM)
    wide = pl.pallas_call(
        widen_kernel,
        name="widen",
        out_shape=[
            shape((seg, width), F32), shape((seg, width), F32), shape((3, width, width), F32), shape((1, width, width), F32),
            shape((width, hidden), F32), shape((nq, width, width), F32), shape((1, width, width), F32),
            shape((2, width), F32), shape((2, width), F32), shape((3, 1, width), F32), shape((2, width), F32),
            shape((1, width), F32), shape((1, width), F32),
            shape((1, 1, width), F32), shape((1, 1, width), F32), shape((1, 2, 1, width), F32),
        ],
        in_specs=[anywhere, anywhere, vmem, vmem, vmem, vmem, vmem],
        out_specs=[anywhere] * 7 + [vmem] * 9,
        scratch_shapes=[
            pltpu.VMEM((4, width // 2, width), F32),
            pltpu.VMEM((2, seg, width), BF),
            pltpu.VMEM((2, seg, width), F32),
            dma((4,)), dma((2,)), dma((2,)),
        ],
        compiler_params=pltpu.CompilerParams(vmem_limit_bytes=WIDEN_BYTES),
    )(ob, gb, out_small, in_vmem, fin_num, fin_den, fin_rows)
    return (
        wide[0][None],
        wide[1][None],
        wide[7][None],
        wide[8][None],
        jnp.swapaxes(wide[9], 0, 1),
        wide[10][None],
        wide[11],
        wide[12],
        wide[2][None],
        wide[3],
        wide[4][None],
        wide[5].reshape(1, hidden, width),
        wide[6],
        wide[13],
        wide[14],
        wide[15],
    )


def solution(mesh):
    args = (
        P("dp", "pipe", None),
        P("pipe", None, None),
        P("pipe", None, None),
        P("pipe", None, None),
        P("pipe", None, None),
        P("pipe", None),
        P("pipe", None),
        P("pipe", None, None, None),
        P("pipe", None, None),
        P("pipe", None, None),
        P("pipe", None, None),
        P("pipe", None, None),
        P("pipe", "dp", None),
        P("pipe", "dp", None),
        P("pipe", None, "dp", None),
        P("dp", "pipe", None),
    )
    outs = (
        P("dp", "pipe", None),
        P("dp", "pipe", None),
        P("pipe", None, None),
        P("pipe", None, None),
        P("pipe", None, None),
        P("pipe", None, None),
        P("pipe", None),
        P("pipe", None),
        P("pipe", None, None, None),
        P("pipe", None, None),
        P("pipe", None, None),
        P("pipe", None, None),
        P("pipe", None, None),
        P("pipe", "dp", None),
        P("pipe", "dp", None),
        P("pipe", None, "dp", None),
    )
    return jax.shard_map(body, mesh=mesh, in_specs=args, out_specs=outs, check_vma=False)
```

```python
import functools

import jax
import jax.numpy as jnp
from jax import lax
from jax.experimental import pallas as pl
from jax.experimental.pallas import tpu as pltpu
from jax.sharding import PartitionSpec as P

ON_CHIP = pltpu.VMEM
MESH = pl.DeviceIdType.MESH
BF, F32 = jnp.bfloat16, jnp.float32
TOKENS = 128
ROWS = 16
SPLIT = 6
LAG = 3
GUESTS = 4
GUEST_AT = 24
GUEST_TURN = 50
VMEM_BYTES = 62 * 1024 * 1024
SUMS_BYTES = 47 * 1024 * 1024
WIDEN_BYTES = 16 * 1024 * 1024


def position():
    p, i = lax.axis_index("pipe"), lax.axis_index("dp")
    y = lax.div(p, 2)
    k = p - 2 * y
    first = 2 * lax.div(i, 2)
    s = i - first
    return p, i, y, k, first, s, lax.rem(s + y, 2)


def home(layer, k, first):
    y = lax.div(layer, 2)
    return 2 * y + k, first + lax.rem(layer - y, 2)


def local(src, dst, sem):
    return pltpu.make_async_copy(src, dst, sem)


def remote(src, dst, send, recv, p, i):
    return pltpu.make_async_remote_copy(
        src_ref=src, dst_ref=dst, send_sem=send, recv_sem=recv, device_id=(p, i), device_id_type=MESH
    )


def drain(ref, sem):
    pltpu.make_async_copy(ref, ref, sem).wait()


def dot(a, b):
    return lax.dot_general(a, b, (((1,), (0,)), ((), ())), preferred_element_type=F32)


def dot_t(a, b):
    return lax.dot_general(a, b, (((1,), (1,)), ((), ())), preferred_element_type=F32)


def later(v, row):
    at = lax.broadcasted_iota(jnp.int32, v.shape, 0)
    return jnp.where(at == 0, row, pltpu.roll(v, 1, 0))


def earlier(v, row):
    n = v.shape[0]
    at = lax.broadcasted_iota(jnp.int32, v.shape, 0)
    return jnp.where(at == n - 1, row, pltpu.roll(v, n - 1, 0))


def fade_tables(table, rate):
    at = lax.broadcasted_iota(jnp.int32, table.shape[1:], 0)
    for n, by in enumerate((1, 2, 4)):
        fade = jnp.exp(-float(by) * rate)
        table[n] = jnp.where(at >= by, fade, 0.0)
        table[4 + n] = jnp.where(at < 8 - by, fade, 0.0)
    far = at.astype(F32)
    table[3] = jnp.exp(-(far + 1.0) * rate)
    table[7] = jnp.exp(-(8.0 - far) * rate)


def sums_before(v, carry, table):
    for n, by in enumerate((1, 2, 4)):
        v = v + table[n] * pltpu.roll(v, by, 0)
    v = v + table[3] * carry
    return later(v, carry), v[7:8]


def sums_behind(v, carry, table):
    for n, by in enumerate((1, 2, 4)):
        v = v + table[4 + n] * pltpu.roll(v, 8 - by, 0)
    v = v + table[7] * carry
    return earlier(v, carry), v[0:1]


def centred(v):
    c = v - jnp.mean(v, axis=-1, keepdims=True)
    r = lax.rsqrt(jnp.mean(c * c, axis=-1, keepdims=True) + 1e-05)
    return c * r, r


def layers_kernel(
    npipe,
    x_hbm, cot_hbm, gain_hbm, bias_hbm, tmix_hbm, cmix_hbm, decay_hbm, first_hbm, num_hbm, den_hbm, rows_hbm,
    win_hbm, wout_hbm, wck_hbm, wcv_hbm, wcr_hbm,
    xo, go, small, fin_num, fin_den, fin_rows, ob, gb, turned,
    w, gain, bias, tmix, cmix, decay, bonus_s, num_s, den_s, rows_s, inbox, gbox,
    e_s, v_s, n_s, d_s, s_s, xh1, xh2, s2_s, c2_s, relu, r1, r2, car1, car2, back, acc, xst, gst, table, t0, t1, t2, t3,
    w_send, w_recv, in_send, in_recv, g_send, g_recv, x0_send, cot_send, ob_recv, gb_recv,
    st_send, st_recv, fin_send, fin_recv, x_sem, go_sem, relu_sem, turn_out, turn_in,
):
    p, i, y, k, first, s, m_chip = position()
    layer = 2 * y + m_chip
    last = npipe - 1
    nm, nt, width = inbox.shape
    nq = relu.shape[1] // nt
    per = x_hbm.shape[1] // nt
    nblocks = w.shape[0]
    key, val, rec = 4, 4 + nq, 4 + 2 * nq

    weights = [(gain_hbm.at[0], gain), (bias_hbm.at[0], bias), (tmix_hbm, tmix), (cmix_hbm.at[0], cmix),
               (decay_hbm, decay), (first_hbm, bonus_s)]
    base = len(weights)
    order = [0, 1, 2, 3] + [at for q in range(nq) for at in (key + q, val + q)] + [rec]
    source = {rec: wcr_hbm.at[0], 3: wout_hbm.at[0]}
    for c in range(3):
        source[c] = win_hbm.at[0, c]
    for q in range(nq):
        source[key + q] = wck_hbm.at[0, :, q * width : (q + 1) * width]
        source[val + q] = wcv_hbm.at[0, q * width : (q + 1) * width]
    weights += [(source[at], w.at[at]) for at in order]
    place = {at: base + n for n, at in enumerate(order)}
    owner = k == m_chip

    @pl.when(owner)
    def _():
        for a, (src, dst) in enumerate(weights):
            local(src, dst, w_recv.at[a]).start()

    barrier = pltpu.get_barrier_semaphore()
    for step in range(1, 2 * npipe):
        at = lax.rem(2 * p + s + step, 2 * npipe)
        op = lax.div(at, 2)
        pl.semaphore_signal(barrier, inc=1, device_id=(op, first + at - 2 * op), device_id_type=MESH)
    pl.semaphore_wait(barrier, 2 * npipe - 1)

    ip, ii = home(0, s, first)
    in_self = jnp.logical_and(ip == p, ii == i)
    cp, ci = home(last, s, first)
    cot_self = jnp.logical_and(cp == p, ci == i)
    tp, ti = home(p, s, first)
    st_self = jnp.logical_and(tp == p, ti == i)

    def give(src, dst, send, recv, dp, di, mine):
        @pl.when(mine)
        def _():
            local(src, dst, recv).start()

        @pl.when(jnp.logical_not(mine))
        def _():
            remote(src, dst, send, recv, dp, di).start()

    states = ((num_hbm.at[0], num_s), (den_hbm.at[0], den_s), (rows_hbm.at[0, :, 0], rows_s))

    @pl.when(owner)
    def _():
        for a, (src, dst) in enumerate(weights[:base]):
            remote(src, dst, w_send.at[a], w_recv.at[a], 2 * y + 1 - k, i).start()

    for u in range(per):
        give(x_hbm.at[0, pl.ds(u * nt, nt)], inbox.at[p * per + u], x0_send.at[u], in_recv.at[p * per + u], ip, ii, in_self)
    for a, (src, dst) in enumerate(states):
        give(src, dst, st_send.at[a], st_recv.at[a], tp, ti, st_self)

    @pl.when(owner)
    def _():
        for a, (src, dst) in enumerate(weights[base:]):
            remote(src, dst, w_send.at[base + a], w_recv.at[base + a], 2 * y + 1 - k, i).start()

    for u in range(per):
        give(cot_hbm.at[0, pl.ds(u * nt, nt)], gbox.at[p * per + u], cot_send.at[u], g_recv.at[p * per + u], cp, ci, cot_self)

    for a in range(base):
        drain(weights[a][1], w_recv.at[a])
    for a, (src, dst) in enumerate(states):
        drain(dst, st_recv.at[a])
    np_, ni = home(layer + 1, k, first)
    bp, bi = home(layer - 1, k, first)
    rate = jnp.exp(decay[...])
    bonus = jnp.exp(bonus_s[...])
    fade = jnp.exp(-rate)
    fade_tables(table, rate)
    tmixes = [tmix[c] for c in range(3)]
    cmixes = [cmix[c : c + 1] for c in range(2)]

    @pl.when(layer == last)
    def _():
        for at in order:
            drain(w.at[at], w_recv.at[place[at]])

        def turn(at, none):
            slot = lax.rem(at, 2)

            @pl.when(at >= 2)
            def _():
                drain(gst.at[slot, pl.ds(0, width)], turn_out.at[slot])

            gst[slot, 0:width] = w[at].T
            local(gst.at[slot, pl.ds(0, width)], turned.at[at], turn_out.at[slot]).start()
            return none

        lax.fori_loop(0, nblocks, turn, 0)
        for slot in range(2):
            drain(gst.at[slot, pl.ds(0, width)], turn_out.at[slot])

    def forward(m, none, begin=False):
        slot = lax.rem(m, 2)

        def ready(*blocks):
            if begin:

                @pl.when(layer < last)
                def _():
                    for at in blocks:
                        drain(w.at[at], w_recv.at[place[at]])

        if not begin:

            @pl.when(m >= 2)
            def _():
                drain(xst.at[slot], x_sem.at[slot])

        drain(inbox.at[m], in_recv.at[m])
        def norm_mix(rows_of, which, xh_s, r_s, car, mixes, to):
            before = rows_s[which : which + 1]
            car[m, 0:1] = before
            for r in range(0, nt, ROWS):
                here = slice(r, r + ROWS)
                xh, rs = centred(rows_of(here))
                xh_s[m, here] = xh.astype(BF)
                r_s[m, here] = rs
                xn = xh * gain[which : which + 1] + bias[which : which + 1]
                xp = later(xn, before)
                before = xn[ROWS - 1 :]
                d = xn - xp
                for c, mix in enumerate(mixes):
                    xst[slot, (to + c) * nt + r : (to + c) * nt + r + ROWS] = (xp + mix * d).astype(BF)
            rows_s[which : which + 1] = before

        norm_mix(lambda here: inbox[m, here].astype(F32), 0, xh1, r1, car1, tmixes, 0)
        ready(0)
        t0[...] = dot(xst[slot, 0:nt], w[0])
        ready(1)
        v_s[m] = dot(xst[slot, nt : 2 * nt], w[1])
        ready(2)
        t2[...] = dot(xst[slot, 2 * nt : 3 * nt], w[2])
        nc, dc = num_s[...], den_s[...]
        for r in range(0, nt, ROWS):
            here = slice(r, r + ROWS)
            gate = jax.nn.sigmoid(t2[here])
            s_s[m, here] = gate.astype(BF)
            wkv = []
            for r8 in range(r, r + ROWS, 8):
                rows = slice(r8, r8 + 8)
                e = jnp.exp(t0[rows])
                v = v_s[m, rows]
                num, nc = sums_before(e * v, nc, table)
                den, dc = sums_before(e, dc, table)
                e_s[m, rows] = e
                n_s[m, rows] = num
                d_s[m, rows] = den
                b = bonus * e
                wkv.append((num + b * v) / (den + b))
            xst[slot, 3 * nt + r : 3 * nt + r + ROWS] = (gate * jnp.concatenate(wkv, axis=0)).astype(BF)
        num_s[...] = nc
        den_s[...] = dc
        ready(3)
        t1[...] = dot(xst[slot, 3 * nt : 4 * nt], w[3])

        def middle(here):
            mid = inbox[m, here].astype(F32) + t1[here]
            t1[here] = mid
            return mid

        norm_mix(middle, 1, xh2, r2, car2, cmixes, 4)
        squares = []
        for q in range(nq):
            ready(key + q)
            r = jnp.maximum(dot(xst[slot, 4 * nt : 5 * nt], w[key + q]), 0.0)
            relu[m, q * nt : (q + 1) * nt] = r.astype(BF)
            squares.append((r * r).astype(BF))
        ready(rec)
        t2[...] = dot(xst[slot, 5 * nt : 6 * nt], w[rec])
        for q in range(nq):
            ready(val + q)
        t0[...] = dot(jnp.concatenate(squares, axis=1), w[val : val + nq].reshape(nq * width, width))
        for r in range(0, nt, ROWS):
            here = slice(r, r + ROWS)
            gate = jax.nn.sigmoid(t2[here])
            out = t0[here]
            s2_s[m, here] = gate.astype(BF)
            gated = gate * out
            c2_s[m, here] = (gated * (1.0 - gate)).astype(BF)
            inbox[m, here] = (t1[here] + gated).astype(BF)

        @pl.when(layer < last)
        def _():
            remote(inbox.at[m], inbox.at[m], in_send.at[m], in_recv.at[m], np_, ni).start()

        @pl.when(layer == last)
        def _():
            q = lax.div(m, per)
            u = m - q * per
            mine = jnp.logical_and(q == p, first + k == i)
            give(inbox.at[m], ob.at[pl.ds(pl.multiple_of(u * nt, nt), nt)], in_send.at[m], ob_recv.at[u], q, first + k, mine)

        local(xst.at[slot], xo.at[m, pl.ds(0, 6 * nt)], x_sem.at[slot]).start()
        local(relu.at[m], xo.at[m, pl.ds(6 * nt, nq * nt)], relu_sem.at[m]).start()
        return none

    forward(0, 0, True)
    lax.fori_loop(1, nm, forward, 0)

    wanted = [at for q in range(nq) for at in (val + q, key + q)] + [rec, 3, 0, 1, 2]

    @pl.when(layer == last)
    def _():
        for at in wanted:
            local(turned.at[at], w.at[at], turn_in.at[at]).start()

    finals = ((num_s, fin_num.at[0]), (den_s, fin_den.at[0]), (rows_s, fin_rows.at[0, :, 0]))
    fp, fi = layer, first + k
    fin_self = jnp.logical_and(fp == p, fi == i)
    for a, (src, dst) in enumerate(finals):
        give(src, dst, fin_send.at[a], fin_recv.at[a], fp, fi, fin_self)

    @pl.when(layer < last)
    def _():
        def turn(at, none):
            w[at] = w[at].T
            return none

        lax.fori_loop(0, nblocks, turn, 0)

    back[...] = jnp.zeros_like(back)
    acc[...] = jnp.zeros_like(acc)

    def note(at, v):
        acc[at] += v[0:8] + v[8:16]

    def mix_back(m, parts, xh_s, r_s, car, which, mixes, rows_of, put, back_at, acc_mix):
        gain_row, bias_row = gain[which : which + 1], bias[which : which + 1]
        behind = back[back_at : back_at + 1]
        for r in reversed(range(0, nt, ROWS)):
            here = slice(r, r + ROWS)
            xh = xh_s[m, here].astype(F32)
            xn = xh * gain_row + bias_row
            if r == 0:
                before = car[m, 0:1]
            else:
                before = xh_s[m, r - ROWS : r].astype(F32)[ROWS - 1 :] * gain_row + bias_row
            d = xn - later(xn, before)
            own, total = None, None
            for c, part in enumerate(parts):
                g = part[here]
                note(acc_mix + c, g * d)
                mixed = g * mixes[c]
                own = mixed if own is None else own + mixed
                total = g if total is None else total + g
            shifted = total - own
            gx = own + earlier(shifted, behind)
            behind = shifted[0:1]
            note(which, gx * xh)
            note(2 + which, gx)
            gp = gx * gain_row
            centre = jnp.mean(gp, axis=-1, keepdims=True)
            slope = jnp.mean(gp * xh, axis=-1, keepdims=True)
            put(here, rows_of(here) + r_s[m, here] * (gp - centre - xh * slope))
        back[back_at : back_at + 1] = behind

    def backward(step, none, begin=False):
        m = nm - 1 - step
        slot = lax.rem(step, 2)

        def ready(*blocks):
            if begin:

                @pl.when(layer == last)
                def _():
                    for at in blocks:
                        drain(w.at[at], turn_in.at[at])

        if not begin:

            @pl.when(step >= 2)
            def _():
                drain(gst.at[slot], go_sem.at[slot])

        drain(gbox.at[m], g_recv.at[m])
        for r in range(0, nt, ROWS):
            here = slice(r, r + ROWS)
            g = gbox[m, here].astype(F32)
            gst[slot, (4 + nq) * nt + r : (4 + nq) * nt + r + ROWS] = (g * s2_s[m, here].astype(F32)).astype(BF)
            gst[slot, (5 + nq) * nt + r : (5 + nq) * nt + r + ROWS] = (g * c2_s[m, here].astype(F32)).astype(BF)
        keys = []
        for q in range(nq):
            ready(val + q)
            gs = dot(gst[slot, (4 + nq) * nt : (5 + nq) * nt], w[val + q]).astype(BF)
            r = relu[m, q * nt : (q + 1) * nt]
            gk = gs * (r + r)
            gst[slot, (4 + q) * nt : (5 + q) * nt] = gk
            keys.append(gk)
        ready(rec)
        t1[...] = dot(gst[slot, (5 + nq) * nt : (6 + nq) * nt], w[rec])
        for q in range(nq):
            ready(key + q)
        t0[...] = dot(jnp.concatenate(keys, axis=1), w[key : key + nq].reshape(nq * width, width))

        def put_mid(here, v):
            t3[here] = v
            gst[slot, 3 * nt + here.start : 3 * nt + here.stop] = v.astype(BF)

        mix_back(m, (t0, t1), xh2, r2, car2, 1, cmixes, lambda here: gbox[m, here].astype(F32), put_mid, 3, 7)
        ready(3)
        t0[...] = dot(gst[slot, 3 * nt : 4 * nt], w[3])
        nc, dc = back[0:1], back[1:2]
        for r in reversed(range(0, nt, ROWS)):
            here = slice(r, r + ROWS)
            gates = s_s[m, here].astype(F32)
            outs = []
            for r8 in (r + 8, r):
                rows = slice(r8, r8 + 8)
                gg = t0[rows]
                gate = gates[r8 - r : r8 - r + 8]
                e, v, num, den = e_s[m, rows], v_s[m, rows], n_s[m, rows], d_s[m, rows]
                b = bonus * e
                inv = 1.0 / (den + b)
                wkv = (num + b * v) * inv
                gw = gg * gate
                gn = gw * inv
                gr = gw * wkv * (1.0 - gate)
                gd = -gn * wkv
                an, nc = sums_behind(gn, nc, table)
                ad, dc = sums_behind(gd, dc, table)
                now = b * (gn * v + gd)
                acc[10] += now
                acc[9] += an * num + ad * den
                outs.append((e * (an * v + ad) + now, b * gn + e * an, gr))
            for c in range(3):
                both = jnp.concatenate([outs[1][c], outs[0][c]], axis=0)
                gst[slot, c * nt + r : c * nt + r + ROWS] = both.astype(BF)
        back[0:1] = nc
        back[1:2] = dc
        ready(0, 1, 2)
        for c, t in enumerate((t0, t1, t2)):
            t[...] = dot(gst[slot, c * nt : (c + 1) * nt], w[c])

        def put_out(here, v):
            gbox[m, here] = v.astype(BF)

        mix_back(m, (t0, t1, t2), xh1, r1, car1, 0, tmixes, lambda here: t3[here], put_out, 2, 4)

        @pl.when(layer > 0)
        def _():
            remote(gbox.at[m], gbox.at[m], g_send.at[m], g_recv.at[m], bp, bi).start()

        @pl.when(layer == 0)
        def _():
            q = lax.div(m, per)
            u = m - q * per
            mine = jnp.logical_and(q == p, first + k == i)
            give(gbox.at[m], gb.at[pl.ds(pl.multiple_of(u * nt, nt), nt)], g_send.at[m], gb_recv.at[u], q, first + k, mine)

        local(gst.at[slot], go.at[m], go_sem.at[slot]).start()
        return none

    backward(0, 0, True)
    lax.fori_loop(1, nm, backward, 0)
    for at in range(16):
        row = jnp.sum(acc[at], axis=0, keepdims=True)
        small[at : at + 1] = row * (-rate * fade) if at == 9 else row

    for slot in range(min(2, nm)):
        drain(xst.at[slot], x_sem.at[slot])
        drain(gst.at[slot], go_sem.at[slot])

    def finish(m, none):
        drain(relu.at[m], relu_sem.at[m])
        mine = jnp.logical_and(lax.div(m, per) == p, first + k == i)

        @pl.when(jnp.logical_not(jnp.logical_and(layer == last, mine)))
        def _():
            drain(inbox.at[m], in_send.at[m])

        @pl.when(jnp.logical_not(jnp.logical_and(layer == 0, mine)))
        def _():
            drain(gbox.at[m], g_send.at[m])

        return none

    lax.fori_loop(0, nm, finish, 0)
    for u in range(per):
        part = pl.ds(u * nt, nt)
        drain(ob.at[part], ob_recv.at[u])
        drain(gb.at[part], gb_recv.at[u])

        @pl.when(jnp.logical_not(in_self))
        def _():
            drain(x_hbm.at[0, part], x0_send.at[u])

        @pl.when(jnp.logical_not(cot_self))
        def _():
            drain(cot_hbm.at[0, part], cot_send.at[u])

    @pl.when(jnp.logical_not(st_self))
    def _():
        for a, (src, dst) in enumerate(states):
            drain(dst, st_send.at[a])

    @pl.when(jnp.logical_not(fin_self))
    def _():
        for a, (src, dst) in enumerate(finals):
            drain(src, fin_send.at[a])

    for a, (src, dst) in enumerate(finals):
        drain(dst, fin_recv.at[a])

    @pl.when(owner)
    def _():
        for a, (src, dst) in enumerate(weights):
            drain(dst, w_send.at[a])


def sums_kernel(
    npipe, ngroups, guests, x_hbm, g_hbm, small, out, out_small,
    xb, gbuf, dws, xs, own, rx, rr, ag, xs_s, own_s, rx_s, rr_s, ag_s, gx, gsrc,
    x_sem, g_sem, ex_send, ex_recv, r_send, r_recv, a_send, a_recv, o_send, o_recv, small_send, small_recv,
    gx_send, gx_recv, guest_send, guest_ready,
):
    p, i, y, k, first, s, m_chip = position()
    j = lax.div(i, 2)
    sib = 2 * y + 1 - k
    half, width = own.shape[1:]
    nc = rx.shape[0]
    low, high = GUEST_AT, GUEST_AT + guests
    lower = y == 0
    upper = y == 1
    quarter = half // 2
    rows_c = 2 * half
    split = width // rows_c
    nm, nt = xb.shape[1:3]
    nq = x_hbm.shape[1] // nt - 6
    hops = (ngroups - 1 - j, j)
    dist = (j, ngroups - 1 - j)
    step_by = (-1, 1)
    dest = 2 * y + m_chip
    other = first + 1 - s

    barrier = pltpu.get_barrier_semaphore()
    for bp, bi in ((sib, i), (p, other), (sib, other)):
        pl.semaphore_signal(barrier, inc=1, device_id=(bp, bi), device_id_type=MESH)

    @pl.when(j > 0)
    def _():
        pl.semaphore_signal(barrier, inc=1, device_id=(p, i - 2), device_id_type=MESH)

    @pl.when(j < ngroups - 1)
    def _():
        pl.semaphore_signal(barrier, inc=1, device_id=(p, i + 2), device_id_type=MESH)

    greeted = 3 + jnp.where(j > 0, 1, 0) + jnp.where(j < ngroups - 1, 1, 0)
    if guests:

        @pl.when(upper)
        def _():
            for bp, bi in ((k, i), (s, first), (s, first + 1)):
                pl.semaphore_signal(barrier, inc=1, device_id=(bp, bi), device_id_type=MESH)

        greeted = greeted + jnp.where(lower, 3, 0)

    def enter():
        pl.semaphore_wait(barrier, greeted)
        if guests:

            @pl.when(lower)
            def _():
                for op in (2, 3):
                    pl.semaphore_signal(guest_ready, inc=1, device_id=(op, first + k), device_id_type=MESH)

    def blocks(c):
        b = lax.div(c, split)
        xi = jnp.where(b < 4, b, jnp.where(b < 4 + nq, 4, jnp.where(b < 4 + 2 * nq, b - nq + 2, 5)))
        gi = jnp.where(b < 4 + nq, b, jnp.where(b < 4 + 2 * nq, 4 + nq, 5 + nq))
        return b, xi, gi

    def loads(c, slot):
        b, xi, gi = blocks(c)
        part = c - b * split
        cols = pl.ds(pl.multiple_of(part * rows_c, rows_c), rows_c)
        return (
            local(x_hbm.at[:, pl.ds(pl.multiple_of(xi * nt, nt), nt), cols], xb.at[slot], x_sem.at[slot]),
            local(g_hbm.at[:, pl.ds(pl.multiple_of(gi * nt, nt), nt)], gbuf.at[slot], g_sem.at[slot]),
        )

    for copy in loads(0, 0):
        copy.start()

    def produce(c):
        slot = lax.rem(c, 2)

        @pl.when(c + 1 < nc)
        def _():
            for copy in loads(c + 1, 1 - slot):
                copy.start()

        for copy in loads(c, slot):
            copy.wait()
        b = lax.div(c, split)

        @pl.when(jnp.logical_and(b >= 4 + nq, b < 4 + 2 * nq))
        def _():
            r = xb[slot].astype(F32)
            xb[slot] = (r * r).astype(BF)

        dws[...] = lax.dot_general(
            xb[slot].reshape(nm * nt, rows_c), gbuf[slot].reshape(nm * nt, width), (((0,), (0,)), ((), ())),
            preferred_element_type=F32,
        )

        @pl.when(c >= 2)
        def _():
            drain(xs.at[slot], ex_send.at[slot])

        @pl.when(c == 0)
        def _():
            enter()

        xs[slot] = dws[pl.ds(pl.multiple_of((1 - k) * half, half), half)].astype(BF)
        remote(xs.at[slot], rx.at[c], ex_send.at[slot], ex_recv.at[c], sib, i).start()
        own[c] = dws[pl.ds(pl.multiple_of(k * half, half), half)]

        @pl.when(c == 0)
        def _():
            n = small.shape[0]
            mine = jnp.where(k == 0, 1.0, 0.0)
            own_s[...] = jnp.zeros_like(own_s)
            xs_s[...] = jnp.zeros_like(xs_s)
            own_s[0:n] = small[...] * mine
            xs_s[0:n] = (small[...] * (1.0 - mine)).astype(BF)
            remote(xs_s, rx_s, small_send.at[0], ex_recv.at[nc], sib, i).start()

    def welcome(c):
        @pl.when(c == nc)
        def _():
            pl.semaphore_wait(guest_ready, 2)

        drain(gx.at[c - nc], gx_recv.at[c - nc])
        own[c] = gx[c - nc].astype(F32)

    def exchange(c):
        drain(rx.at[c], ex_recv.at[c])
        own[c] = own[c] + rx[c].astype(F32)
        if guests:

            @pl.when(jnp.logical_and(lower, jnp.logical_and(c >= low, c < high)))
            def _():
                gsrc[c - low] = own[c].astype(BF)
                remote(gsrc.at[c - low], gx.at[c - low], gx_send.at[0], gx_recv.at[c - low], p + 2, i).start()

        @pl.when(c == 0)
        def _():
            drain(rx_s, ex_recv.at[nc])
            own_s[...] = own_s[...] + rx_s[...].astype(F32)

    def reduce(c, d):
        def one(value, rr_at, ag_at, send, recv):
            @pl.when(hops[d] == 0)
            def _():
                rr_at[...] = value().astype(BF)

            @pl.when(hops[d] > 0)
            def _():
                drain(rr_at, recv)

                @pl.when(dist[d] > 0)
                def _():
                    rr_at[...] = (value() + rr_at[...].astype(F32)).astype(BF)

                @pl.when(dist[d] == 0)
                def _():
                    ag_at[...] = (value() + rr_at[...].astype(F32)).astype(BF)

            @pl.when(dist[d] > 0)
            def _():
                remote(rr_at, rr_at, send, recv, p, i + 2 * step_by[d]).start()

            @pl.when(jnp.logical_and(dist[d] == 0, hops[d] == 0))
            def _():
                ag_at[...] = rr_at[...]

        one(lambda: own[c, d * quarter : (d + 1) * quarter], rr.at[d, c], ag.at[d, c], r_send.at[d], r_recv.at[d, c])

        @pl.when(c == 0)
        def _():
            n = rr_s.shape[1]
            one(lambda: own_s[d * n : (d + 1) * n], rr_s.at[d], ag_s.at[d], small_send.at[1 + d], r_recv.at[d, nc + guests])

    def spread(c, d):
        def come(ag_at, forward_send, recv):
            @pl.when(dist[d] > 0)
            def _():
                drain(ag_at, recv)

            @pl.when(hops[d] > 0)
            def _():
                remote(ag_at, ag_at, forward_send, recv, p, i - 2 * step_by[d]).start()

        def one(ag_at, to, forward_send, recv, local_send, far_send, out_recv):
            come(ag_at, forward_send, recv)
            remote(ag_at, to, far_send, out_recv, dest, other).start()

            @pl.when(p == dest)
            def _():
                local(ag_at, to, out_recv).start()

            @pl.when(p != dest)
            def _():
                remote(ag_at, to, local_send, out_recv, dest, i).start()

        def place(c):
            b = lax.div(c, split)
            row = (c - b * split) * rows_c + k * half + d * quarter
            return out.at[b, pl.ds(pl.multiple_of(row, quarter), quarter)]

        def own_chunk():
            one(ag.at[d, c], place(c), a_send.at[d], a_recv.at[d, c], o_send.at[0], o_send.at[1], o_recv.at[0])

        if guests:
            pl.when(c < nc)(own_chunk)

            @pl.when(c >= nc)
            def _():
                come(ag.at[d, c], a_send.at[d], a_recv.at[d, c])
                to = place(c - nc + low)
                remote(ag.at[d, c], to, guest_send.at[0], o_recv.at[0], s, i).start()
                remote(ag.at[d, c], to, guest_send.at[1], o_recv.at[0], s, other).start()
        else:
            own_chunk()

        @pl.when(c == 0)
        def _():
            n = rr_s.shape[1]
            to_s = out_small.at[pl.ds(pl.multiple_of(k * 2 * n + d * n, n), n)]
            one(ag_s.at[d], to_s, small_send.at[3 + d], a_recv.at[d, nc + guests], small_send.at[5 + d], small_send.at[7 + d], small_recv.at[0])

    def turn(u, own_work, guest_work=None):
        if not guests:

            @pl.when(jnp.logical_and(u >= 0, u < nc))
            def _():
                own_work(u)

            return
        at = min(GUEST_TURN, nc)
        c = jnp.where(u < at, u, jnp.where(u < at + guests, nc + u - at, u - guests))
        c = jnp.where(upper, c, u)
        mine = jnp.logical_and(u >= 0, u < nc + jnp.where(upper, guests, 0))
        if guest_work is not own_work:

            @pl.when(jnp.logical_and(mine, c < nc))
            def _():
                own_work(c)

            if guest_work is not None:

                @pl.when(jnp.logical_and(mine, c >= nc))
                def _():
                    guest_work(c)

        else:
            away = jnp.logical_and(lower, jnp.logical_and(c >= low, c < high))

            @pl.when(jnp.logical_and(mine, jnp.logical_not(away)))
            def _():
                own_work(c)

    def step(t, none):
        turn(t, produce)
        turn(t - 1, exchange, welcome)
        for d in range(2):
            work = functools.partial(reduce, d=d)
            turn(t - 1 - LAG * hops[d], work, work)
        for d in range(2):
            work = functools.partial(spread, d=d)
            turn(t - 1 - LAG * (ngroups - 1 + dist[d]), work, work)
        return none

    lax.fori_loop(0, nc + guests + 1 + 2 * LAG * (ngroups - 1), step, 0)

    def settle(ref, sem):
        if not guests:
            drain(ref, sem)
            return

        @pl.when(upper)
        def _():
            drain(ref, sem)

        @pl.when(lower)
        def _():
            drain(ref.at[pl.ds(0, low)], sem)
            drain(ref.at[pl.ds(high, nc - high)], sem)

    def settle_own(ref, sem):
        if not guests:
            drain(ref, sem)
            return
        drain(ref.at[pl.ds(0, low)], sem)
        drain(ref.at[pl.ds(high, nc - high)], sem)

        @pl.when(upper)
        def _():
            drain(ref.at[pl.ds(low, guests)], sem)

    for slot in range(min(2, nc)):
        drain(xs.at[slot], ex_send.at[slot])
    drain(xs_s, small_send.at[0])
    for d in range(2):

        @pl.when(dist[d] > 0)
        def _():
            settle(rr.at[d], r_send.at[d])
            drain(rr_s.at[d], small_send.at[1 + d])

        @pl.when(hops[d] > 0)
        def _():
            settle(ag.at[d], a_send.at[d])
            drain(ag_s.at[d], small_send.at[3 + d])

        @pl.when(p != dest)
        def _():
            drain(ag_s.at[d], small_send.at[5 + d])

        drain(ag_s.at[d], small_send.at[7 + d])

    for d in range(2):

        @pl.when(p != dest)
        def _():
            settle_own(ag.at[d], o_send.at[0])

        settle_own(ag.at[d], o_send.at[1])
    if guests:

        @pl.when(lower)
        def _():
            drain(gsrc, gx_send.at[0])

        @pl.when(upper)
        def _():
            for d in range(2):
                drain(ag.at[d, pl.ds(nc, guests)], guest_send.at[0])
                drain(ag.at[d, pl.ds(nc, guests)], guest_send.at[1])

    drain(out, o_recv.at[0])
    drain(out_small, small_recv.at[0])


def widen_kernel(
    ob, gb, rows, w, num, den, last,
    out, grad, g_in, g_out, g_key, g_val, g_rec, gain, bias, tmix, cmix, decay, bonus, fin_num, fin_den, fin_rows,
    stage, narrow, wide, sem, in_sem, out_sem,
):
    nblocks, width, _ = w.shape
    slots, step, _ = stage.shape
    nq, cuts = (nblocks - 5) // 2, width // step
    for n, src in enumerate((ob, gb)):
        local(src, narrow.at[n], in_sem.at[n]).start()

    def one(t, none):
        slot = lax.rem(t, slots)
        b = lax.div(t, cuts)
        cut = pl.ds(pl.multiple_of((t - b * cuts) * step, step), step)

        @pl.when(t >= slots)
        def _():
            drain(stage.at[slot], sem.at[slot])

        stage[slot] = w[b, cut].astype(F32)

        @pl.when(b < 3)
        def _():
            local(stage.at[slot], g_in.at[b, cut], sem.at[slot]).start()

        @pl.when(b == 3)
        def _():
            local(stage.at[slot], g_out.at[0, cut], sem.at[slot]).start()

        for q in range(nq):

            @pl.when(b == 4 + q)
            def _():
                local(stage.at[slot], g_key.at[cut, q * width : (q + 1) * width], sem.at[slot]).start()

        @pl.when(jnp.logical_and(b >= 4 + nq, b < 4 + 2 * nq))
        def _():
            local(stage.at[slot], g_val.at[b - 4 - nq, cut], sem.at[slot]).start()

        @pl.when(b == 4 + 2 * nq)
        def _():
            local(stage.at[slot], g_rec.at[0, cut], sem.at[slot]).start()

        return none

    lax.fori_loop(0, nblocks * cuts, one, 0)
    for n, dst in enumerate((out, grad)):
        drain(narrow.at[n], in_sem.at[n])
        wide[n] = narrow[n].astype(F32)
        local(wide.at[n], dst, out_sem.at[n]).start()
    at = 0
    for dst in (gain, bias, tmix, cmix, decay, bonus):
        n = dst.shape[0]
        dst[...] = rows[at : at + n].astype(F32).reshape(dst.shape)
        at += n
    for src, dst in ((num, fin_num), (den, fin_den), (last, fin_rows)):
        dst[...] = src[...]
    for slot in range(slots):
        drain(stage.at[slot], sem.at[slot])
    for n in range(2):
        drain(wide.at[n], out_sem.at[n])


def body(
    block_input, ln_gain, ln_bias, tm_mix, cm_mix, time_decay, time_first, tm_in, tm_out,
    cm_key, cm_value, cm_recept, wkv_num, wkv_den, last_rows, cotangent,
):
    npipe, ndp = lax.axis_size("pipe"), lax.axis_size("dp")
    seg, width = block_input.shape[1:]
    hidden = cm_key.shape[2]
    nq = hidden // width
    length = seg * npipe
    nt = min(TOKENS, seg)
    nm, per = length // nt, seg // nt
    anywhere = pl.BlockSpec(memory_space=pl.ANY)
    vmem = pl.BlockSpec(memory_space=pltpu.VMEM)
    dma = pltpu.SemaphoreType.DMA
    shape = jax.ShapeDtypeStruct
    nb = 6 + nq
    nblocks = 5 + 2 * nq
    xs, gs, small, fin_num, fin_den, fin_rows, ob, gb, turned = pl.pallas_call(
        functools.partial(layers_kernel, npipe),
        name="layers",
        out_shape=[
            shape((nm, nb * nt, width), BF),
            shape((nm, nb * nt, width), BF),
            shape((16, width), F32),
            shape((1, 1, width), F32),
            shape((1, 1, width), F32),
            shape((1, 2, 1, width), F32),
            shape((seg, width), BF),
            shape((seg, width), BF),
            shape((nblocks, width, width), BF),
        ],
        in_specs=[anywhere] * 16,
        out_specs=[anywhere, anywhere, vmem] + [anywhere] * 6,
        scratch_shapes=[
            pltpu.VMEM((nblocks, width, width), BF),
            pltpu.VMEM((2, width), F32),
            pltpu.VMEM((2, width), F32),
            pltpu.VMEM((3, 1, width), F32),
            pltpu.VMEM((2, width), F32),
            pltpu.VMEM((1, width), F32),
            pltpu.VMEM((1, width), F32),
            pltpu.VMEM((1, width), F32),
            pltpu.VMEM((1, width), F32),
            pltpu.VMEM((2, width), F32),
            pltpu.VMEM((nm, nt, width), BF),
            pltpu.VMEM((nm, nt, width), BF),
            *[pltpu.VMEM((nm, nt, width), F32)] * 4,
            *[pltpu.VMEM((nm, nt, width), BF)] * 5,
            pltpu.VMEM((nm, nq * nt, width), BF),
            *[pltpu.VMEM((nm, nt, 1), F32)] * 2,
            *[pltpu.VMEM((nm, 8, width), F32)] * 2,
            pltpu.VMEM((8, width), F32),
            pltpu.VMEM((16, 8, width), F32),
            pltpu.VMEM((2, 6 * nt, width), BF),
            pltpu.VMEM((2, nb * nt, width), BF),
            pltpu.VMEM((8, 8, width), F32),
            *[pltpu.VMEM((nt, width), F32)] * 4,
            dma((6 + nblocks,)), dma((6 + nblocks,)), dma((nm,)), dma((nm,)), dma((nm,)), dma((nm,)),
            dma((per,)), dma((per,)), dma((per,)), dma((per,)),
            dma((3,)), dma((3,)), dma((3,)), dma((3,)), dma((2,)), dma((2,)), dma((nm,)), dma((2,)), dma((nblocks,)),
        ],
        compiler_params=pltpu.CompilerParams(collective_id=0, has_side_effects=True, vmem_limit_bytes=VMEM_BYTES),
    )(block_input, cotangent, ln_gain, ln_bias, jnp.swapaxes(tm_mix, 0, 1), cm_mix, time_decay, time_first, wkv_num, wkv_den, last_rows,
      tm_in, tm_out, cm_key, cm_value, cm_recept)

    rows_c = width // SPLIT if width % (128 * SPLIT) == 0 else width // 2
    nc, half = nblocks * (width // rows_c), rows_c // 2
    quarter = half // 2
    guests = GUESTS if npipe == 4 else 0
    all_c = nc + guests
    out, out_small = pl.pallas_call(
        functools.partial(sums_kernel, npipe, ndp // 2, guests),
        name="sums",
        out_shape=[ON_CHIP((nblocks, width, width), BF), ON_CHIP((64, width), BF)],
        in_specs=[anywhere, anywhere, vmem],
        out_specs=[vmem, vmem],
        scratch_shapes=[
            pltpu.VMEM((2, nm, nt, rows_c), BF),
            pltpu.VMEM((2, nm, nt, width), BF),
            pltpu.VMEM((rows_c, width), F32),
            pltpu.VMEM((2, half, width), BF),
            pltpu.VMEM((all_c, half, width), F32),
            pltpu.VMEM((nc, half, width), BF),
            pltpu.VMEM((2, all_c, quarter, width), BF),
            pltpu.VMEM((2, all_c, quarter, width), BF),
            pltpu.VMEM((32, width), BF),
            pltpu.VMEM((32, width), F32),
            pltpu.VMEM((32, width), BF),
            pltpu.VMEM((2, 16, width), BF),
            pltpu.VMEM((2, 16, width), BF),
            pltpu.VMEM((max(guests, 1), half, width), BF),
            pltpu.VMEM((max(guests, 1), half, width), BF),
            dma((2,)), dma((2,)), dma((2,)), dma((nc + 1,)), dma((2,)), dma((2, all_c + 1)), dma((2,)), dma((2, all_c + 1)),
            dma((2,)), dma((1,)), dma((9,)), dma((1,)), dma((1,)), dma((max(guests, 1),)), dma((2,)), pltpu.SemaphoreType.REGULAR,
        ],
        compiler_params=pltpu.CompilerParams(collective_id=1, has_side_effects=True, vmem_limit_bytes=SUMS_BYTES),
    )(xs, gs, small)

    in_vmem = pltpu.with_memory_space_constraint(out, pltpu.VMEM)
    wide = pl.pallas_call(
        widen_kernel,
        name="widen",
        out_shape=[
            shape((seg, width), F32), shape((seg, width), F32), shape((3, width, width), F32), shape((1, width, width), F32),
            shape((width, hidden), F32), shape((nq, width, width), F32), shape((1, width, width), F32),
            shape((2, width), F32), shape((2, width), F32), shape((3, 1, width), F32), shape((2, width), F32),
            shape((1, width), F32), shape((1, width), F32),
            shape((1, 1, width), F32), shape((1, 1, width), F32), shape((1, 2, 1, width), F32),
        ],
        in_specs=[anywhere, anywhere, vmem, vmem, vmem, vmem, vmem],
        out_specs=[anywhere] * 7 + [vmem] * 9,
        scratch_shapes=[
            pltpu.VMEM((4, width // 2, width), F32),
            pltpu.VMEM((2, seg, width), BF),
            pltpu.VMEM((2, seg, width), F32),
            dma((4,)), dma((2,)), dma((2,)),
        ],
        compiler_params=pltpu.CompilerParams(vmem_limit_bytes=WIDEN_BYTES),
    )(ob, gb, out_small, in_vmem, fin_num, fin_den, fin_rows)
    return (
        wide[0][None],
        wide[1][None],
        wide[7][None],
        wide[8][None],
        jnp.swapaxes(wide[9], 0, 1),
        wide[10][None],
        wide[11],
        wide[12],
        wide[2][None],
        wide[3],
        wide[4][None],
        wide[5].reshape(1, hidden, width),
        wide[6],
        wide[13],
        wide[14],
        wide[15],
    )


def solution(mesh):
    args = (
        P("dp", "pipe", None),
        P("pipe", None, None),
        P("pipe", None, None),
        P("pipe", None, None),
        P("pipe", None, None),
        P("pipe", None),
        P("pipe", None),
        P("pipe", None, None, None),
        P("pipe", None, None),
        P("pipe", None, None),
        P("pipe", None, None),
        P("pipe", None, None),
        P("pipe", "dp", None),
        P("pipe", "dp", None),
        P("pipe", None, "dp", None),
        P("dp", "pipe", None),
    )
    outs = (
        P("dp", "pipe", None),
        P("dp", "pipe", None),
        P("pipe", None, None),
        P("pipe", None, None),
        P("pipe", None, None),
        P("pipe", None, None),
        P("pipe", None),
        P("pipe", None),
        P("pipe", None, None, None),
        P("pipe", None, None),
        P("pipe", None, None),
        P("pipe", None, None),
        P("pipe", None, None),
        P("pipe", "dp", None),
        P("pipe", "dp", None),
        P("pipe", None, "dp", None),
    )
    return jax.shard_map(body, mesh=mesh, in_specs=args, out_specs=outs, check_vma=False)
```

```python
import functools

import jax
import jax.numpy as jnp
from jax import lax
from jax.experimental import pallas as pl
from jax.experimental.pallas import tpu as pltpu
from jax.sharding import PartitionSpec as P

ON_CHIP = pltpu.VMEM
MESH = pl.DeviceIdType.MESH
BF, F32 = jnp.bfloat16, jnp.float32
TOKENS = 128
ROWS = 16
SPLIT = 6
LAG = 3
GUESTS = 3
GUEST_AT = 24
GUEST_TURN = 50
VMEM_BYTES = 62 * 1024 * 1024
SUMS_BYTES = 47 * 1024 * 1024
WIDEN_BYTES = 16 * 1024 * 1024


def position():
    p, i = lax.axis_index("pipe"), lax.axis_index("dp")
    y = lax.div(p, 2)
    k = p - 2 * y
    first = 2 * lax.div(i, 2)
    s = i - first
    return p, i, y, k, first, s, lax.rem(s + y, 2)


def home(layer, k, first):
    y = lax.div(layer, 2)
    return 2 * y + k, first + lax.rem(layer - y, 2)


def local(src, dst, sem):
    return pltpu.make_async_copy(src, dst, sem)


def remote(src, dst, send, recv, p, i):
    return pltpu.make_async_remote_copy(
        src_ref=src, dst_ref=dst, send_sem=send, recv_sem=recv, device_id=(p, i), device_id_type=MESH
    )


def drain(ref, sem):
    pltpu.make_async_copy(ref, ref, sem).wait()


def dot(a, b):
    return lax.dot_general(a, b, (((1,), (0,)), ((), ())), preferred_element_type=F32)


def dot_t(a, b):
    return lax.dot_general(a, b, (((1,), (1,)), ((), ())), preferred_element_type=F32)


def later(v, row):
    at = lax.broadcasted_iota(jnp.int32, v.shape, 0)
    return jnp.where(at == 0, row, pltpu.roll(v, 1, 0))


def earlier(v, row):
    n = v.shape[0]
    at = lax.broadcasted_iota(jnp.int32, v.shape, 0)
    return jnp.where(at == n - 1, row, pltpu.roll(v, n - 1, 0))


def fade_tables(table, rate):
    at = lax.broadcasted_iota(jnp.int32, table.shape[1:], 0)
    for n, by in enumerate((1, 2, 4)):
        fade = jnp.exp(-float(by) * rate)
        table[n] = jnp.where(at >= by, fade, 0.0)
        table[4 + n] = jnp.where(at < 8 - by, fade, 0.0)
    far = at.astype(F32)
    table[3] = jnp.exp(-(far + 1.0) * rate)
    table[7] = jnp.exp(-(8.0 - far) * rate)


def sums_before(v, carry, table):
    for n, by in enumerate((1, 2, 4)):
        v = v + table[n] * pltpu.roll(v, by, 0)
    v = v + table[3] * carry
    return later(v, carry), v[7:8]


def sums_behind(v, carry, table):
    for n, by in enumerate((1, 2, 4)):
        v = v + table[4 + n] * pltpu.roll(v, 8 - by, 0)
    v = v + table[7] * carry
    return earlier(v, carry), v[0:1]


def centred(v):
    c = v - jnp.mean(v, axis=-1, keepdims=True)
    r = lax.rsqrt(jnp.mean(c * c, axis=-1, keepdims=True) + 1e-05)
    return c * r, r


def layers_kernel(
    npipe,
    x_hbm, cot_hbm, gain_hbm, bias_hbm, tmix_hbm, cmix_hbm, decay_hbm, first_hbm, num_hbm, den_hbm, rows_hbm,
    win_hbm, wout_hbm, wck_hbm, wcv_hbm, wcr_hbm,
    xo, go, small, fin_num, fin_den, fin_rows, ob, gb, turned, tail,
    w, gain, bias, tmix, cmix, decay, bonus_s, num_s, den_s, rows_s, inbox, gbox,
    e_s, v_s, n_s, d_s, s_s, xh1, xh2, s2_s, c2_s, relu, r1, r2, car1, car2, back, acc, xst, gst, table, t0, t1, t2, t3,
    w_send, w_recv, in_send, in_recv, g_send, g_recv, x0_send, cot_send, ob_recv, gb_recv,
    st_send, st_recv, fin_send, fin_recv, x_sem, go_sem, relu_sem, turn_out, turn_in, tail_sem,
):
    p, i, y, k, first, s, m_chip = position()
    layer = 2 * y + m_chip
    last = npipe - 1
    nm, nt, width = inbox.shape
    nq = relu.shape[1] // nt
    per = x_hbm.shape[1] // nt
    nblocks = w.shape[0]
    key, val, rec = 4, 4 + nq, 4 + 2 * nq

    weights = [(gain_hbm.at[0], gain), (bias_hbm.at[0], bias), (tmix_hbm, tmix), (cmix_hbm.at[0], cmix),
               (decay_hbm, decay), (first_hbm, bonus_s)]
    base = len(weights)
    order = [0, 1, 2, 3] + [key + q for q in range(nq)] + [rec] + [val + q for q in range(nq)]
    source = {rec: wcr_hbm.at[0], 3: wout_hbm.at[0]}
    for c in range(3):
        source[c] = win_hbm.at[0, c]
    for q in range(nq):
        source[key + q] = wck_hbm.at[0, :, q * width : (q + 1) * width]
        source[val + q] = wcv_hbm.at[0, q * width : (q + 1) * width]
    weights += [(source[at], w.at[at]) for at in order]
    place = {at: base + n for n, at in enumerate(order)}
    owner = k == m_chip

    @pl.when(owner)
    def _():
        for a, (src, dst) in enumerate(weights):
            local(src, dst, w_recv.at[a]).start()

    barrier = pltpu.get_barrier_semaphore()
    for step in range(1, 2 * npipe):
        at = lax.rem(2 * p + s + step, 2 * npipe)
        op = lax.div(at, 2)
        pl.semaphore_signal(barrier, inc=1, device_id=(op, first + at - 2 * op), device_id_type=MESH)
    pl.semaphore_wait(barrier, 2 * npipe - 1)

    ip, ii = home(0, s, first)
    in_self = jnp.logical_and(ip == p, ii == i)
    cp, ci = home(last, s, first)
    cot_self = jnp.logical_and(cp == p, ci == i)
    tp, ti = home(p, s, first)
    st_self = jnp.logical_and(tp == p, ti == i)

    def give(src, dst, send, recv, dp, di, mine):
        @pl.when(mine)
        def _():
            local(src, dst, recv).start()

        @pl.when(jnp.logical_not(mine))
        def _():
            remote(src, dst, send, recv, dp, di).start()

    states = ((num_hbm.at[0], num_s), (den_hbm.at[0], den_s), (rows_hbm.at[0, :, 0], rows_s))

    @pl.when(owner)
    def _():
        for a, (src, dst) in enumerate(weights[:base]):
            remote(src, dst, w_send.at[a], w_recv.at[a], 2 * y + 1 - k, i).start()

    def give_input(u):
        give(x_hbm.at[0, pl.ds(u * nt, nt)], inbox.at[p * per + u], x0_send.at[u], in_recv.at[p * per + u], ip, ii, in_self)

    @pl.when(p == 0)
    def _():
        give_input(0)

    for a, (src, dst) in enumerate(states):
        give(src, dst, st_send.at[a], st_recv.at[a], tp, ti, st_self)

    @pl.when(owner)
    def _():
        for a, (src, dst) in enumerate(weights[base:]):
            remote(src, dst, w_send.at[base + a], w_recv.at[base + a], 2 * y + 1 - k, i).start()

    for a in range(base):
        drain(weights[a][1], w_recv.at[a])
    for a, (src, dst) in enumerate(states):
        drain(dst, st_recv.at[a])

    @pl.when(p > 0)
    def _():
        give_input(0)

    for u in range(1, per):
        give_input(u)
    for u in range(per):
        give(cot_hbm.at[0, pl.ds(u * nt, nt)], gbox.at[p * per + u], cot_send.at[u], g_recv.at[p * per + u], cp, ci, cot_self)
    np_, ni = home(layer + 1, k, first)
    bp, bi = home(layer - 1, k, first)
    rate = jnp.exp(decay[...])
    bonus = jnp.exp(bonus_s[...])
    fade = jnp.exp(-rate)
    fade_tables(table, rate)
    tmixes = [tmix[c] for c in range(3)]
    cmixes = [cmix[c : c + 1] for c in range(2)]

    @pl.when(layer == last)
    def _():
        for at in order:
            drain(w.at[at], w_recv.at[place[at]])

        def turn(n, none):
            slot = lax.rem(n, 2)
            at = lax.rem(n + val + 2, nblocks)

            @pl.when(n >= 2)
            def _():
                drain(gst.at[slot, pl.ds(0, width)], turn_out.at[slot])

            gst[slot, 0:width] = w[at].T
            local(gst.at[slot, pl.ds(0, width)], turned.at[at], turn_out.at[slot]).start()
            return none

        lax.fori_loop(0, nblocks, turn, 0)
        for slot in range(2):
            drain(gst.at[slot, pl.ds(0, width)], turn_out.at[slot])

    def forward(m, none, begin=False):
        slot = lax.rem(m, 2)

        def ready(*blocks):
            if begin:

                @pl.when(layer < last)
                def _():
                    for at in blocks:
                        drain(w.at[at], w_recv.at[place[at]])

        if not begin:

            @pl.when(m >= 2)
            def _():
                drain(xst.at[slot], x_sem.at[slot])

        drain(inbox.at[m], in_recv.at[m])
        def norm_mix(rows_of, which, xh_s, r_s, car, mixes, to):
            before = rows_s[which : which + 1]
            car[m, 0:1] = before
            for r in range(0, nt, ROWS):
                here = slice(r, r + ROWS)
                xh, rs = centred(rows_of(here))
                xh_s[m, here] = xh.astype(BF)
                r_s[m, here] = rs
                xn = xh * gain[which : which + 1] + bias[which : which + 1]
                xp = later(xn, before)
                before = xn[ROWS - 1 :]
                d = xn - xp
                for c, mix in enumerate(mixes):
                    xst[slot, (to + c) * nt + r : (to + c) * nt + r + ROWS] = (xp + mix * d).astype(BF)
            rows_s[which : which + 1] = before

        norm_mix(lambda here: inbox[m, here].astype(F32), 0, xh1, r1, car1, tmixes, 0)
        ready(0)
        t0[...] = dot(xst[slot, 0:nt], w[0])
        ready(1)
        v_s[m] = dot(xst[slot, nt : 2 * nt], w[1])
        ready(2)
        t2[...] = dot(xst[slot, 2 * nt : 3 * nt], w[2])
        nc, dc = num_s[...], den_s[...]
        for r in range(0, nt, ROWS):
            here = slice(r, r + ROWS)
            gate = jax.nn.sigmoid(t2[here])
            s_s[m, here] = gate.astype(BF)
            wkv = []
            for r8 in range(r, r + ROWS, 8):
                rows = slice(r8, r8 + 8)
                e = jnp.exp(t0[rows])
                v = v_s[m, rows]
                num, nc = sums_before(e * v, nc, table)
                den, dc = sums_before(e, dc, table)
                e_s[m, rows] = e
                n_s[m, rows] = num
                d_s[m, rows] = den
                b = bonus * e
                wkv.append((num + b * v) / (den + b))
            xst[slot, 3 * nt + r : 3 * nt + r + ROWS] = (gate * jnp.concatenate(wkv, axis=0)).astype(BF)
        num_s[...] = nc
        den_s[...] = dc
        ready(3)
        t1[...] = dot(xst[slot, 3 * nt : 4 * nt], w[3])

        def middle(here):
            mid = inbox[m, here].astype(F32) + t1[here]
            t1[here] = mid
            return mid

        norm_mix(middle, 1, xh2, r2, car2, cmixes, 4)
        squares = []
        for q in range(nq):
            ready(key + q)
            r = jnp.maximum(dot(xst[slot, 4 * nt : 5 * nt], w[key + q]), 0.0)
            relu[m, q * nt : (q + 1) * nt] = r.astype(BF)
            squares.append((r * r).astype(BF))
        ready(rec)
        t2[...] = dot(xst[slot, 5 * nt : 6 * nt], w[rec])
        if begin:
            for q in range(nq):
                ready(val + q)
                part = dot(squares[q], w[val + q])
                t0[...] = part if q == 0 else t0[...] + part
        else:
            t0[...] = dot(jnp.concatenate(squares, axis=1), w[val : val + nq].reshape(nq * width, width))
        for r in range(0, nt, ROWS):
            here = slice(r, r + ROWS)
            gate = jax.nn.sigmoid(t2[here])
            out = t0[here]
            s2_s[m, here] = gate.astype(BF)
            gated = gate * out
            c2_s[m, here] = (gated * (1.0 - gate)).astype(BF)
            inbox[m, here] = (t1[here] + gated).astype(BF)

        @pl.when(layer < last)
        def _():
            remote(inbox.at[m], inbox.at[m], in_send.at[m], in_recv.at[m], np_, ni).start()

        @pl.when(layer == last)
        def _():
            q = lax.div(m, per)
            u = m - q * per
            mine = jnp.logical_and(q == p, first + k == i)
            give(inbox.at[m], ob.at[pl.ds(pl.multiple_of(u * nt, nt), nt)], in_send.at[m], ob_recv.at[u], q, first + k, mine)

        local(xst.at[slot], xo.at[m, pl.ds(0, 6 * nt)], x_sem.at[slot]).start()
        local(relu.at[m], xo.at[m, pl.ds(6 * nt, nq * nt)], relu_sem.at[m]).start()
        return none

    forward(0, 0, True)
    lax.fori_loop(1, nm, forward, 0)

    wanted = [val + q for q in range(1, nq)] + [rec] + [key + q for q in range(nq)] + [3, 0, 1, 2]

    @pl.when(layer == last)
    def _():
        for at in wanted:
            local(turned.at[at], w.at[at], turn_in.at[at]).start()
        w[val] = gst[1, 0:width]

    finals = ((num_s, fin_num.at[0]), (den_s, fin_den.at[0]), (rows_s, fin_rows.at[0, :, 0]))
    fp, fi = layer, first + k
    fin_self = jnp.logical_and(fp == p, fi == i)
    for a, (src, dst) in enumerate(finals):
        give(src, dst, fin_send.at[a], fin_recv.at[a], fp, fi, fin_self)

    @pl.when(layer < last)
    def _():
        def turn(at, none):
            w[at] = w[at].T
            return none

        lax.fori_loop(0, nblocks, turn, 0)

    back[...] = jnp.zeros_like(back)
    acc[...] = jnp.zeros_like(acc)

    def note(at, v):
        acc[at] += v[0:8] + v[8:16]

    def mix_back(m, parts, xh_s, r_s, car, which, mixes, rows_of, put, back_at, acc_mix):
        gain_row, bias_row = gain[which : which + 1], bias[which : which + 1]
        behind = back[back_at : back_at + 1]
        for r in reversed(range(0, nt, ROWS)):
            here = slice(r, r + ROWS)
            xh = xh_s[m, here].astype(F32)
            xn = xh * gain_row + bias_row
            if r == 0:
                before = car[m, 0:1]
            else:
                before = xh_s[m, r - ROWS : r].astype(F32)[ROWS - 1 :] * gain_row + bias_row
            d = xn - later(xn, before)
            own, total = None, None
            for c, part in enumerate(parts):
                g = part[here]
                note(acc_mix + c, g * d)
                mixed = g * mixes[c]
                own = mixed if own is None else own + mixed
                total = g if total is None else total + g
            shifted = total - own
            gx = own + earlier(shifted, behind)
            behind = shifted[0:1]
            note(which, gx * xh)
            note(2 + which, gx)
            gp = gx * gain_row
            centre = jnp.mean(gp, axis=-1, keepdims=True)
            slope = jnp.mean(gp * xh, axis=-1, keepdims=True)
            put(here, rows_of(here) + r_s[m, here] * (gp - centre - xh * slope))
        back[back_at : back_at + 1] = behind

    def backward(step, none, begin=False):
        m = nm - 1 - step
        slot = lax.rem(step, 2)

        def ready(*blocks):
            if begin:

                @pl.when(layer == last)
                def _():
                    for at in blocks:
                        if at in wanted:
                            drain(w.at[at], turn_in.at[at])

        if not begin:

            @pl.when(step >= 2)
            def _():
                drain(gst.at[slot], go_sem.at[slot])

        drain(gbox.at[m], g_recv.at[m])
        for r in range(0, nt, ROWS):
            here = slice(r, r + ROWS)
            g = gbox[m, here].astype(F32)
            gst[slot, (4 + nq) * nt + r : (4 + nq) * nt + r + ROWS] = (g * s2_s[m, here].astype(F32)).astype(BF)
            gst[slot, (5 + nq) * nt + r : (5 + nq) * nt + r + ROWS] = (g * c2_s[m, here].astype(F32)).astype(BF)
        keys = []
        for q in range(nq):
            ready(val + q)
            gs = dot(gst[slot, (4 + nq) * nt : (5 + nq) * nt], w[val + q]).astype(BF)
            r = relu[m, q * nt : (q + 1) * nt]
            gk = gs * (r + r)
            gst[slot, (4 + q) * nt : (5 + q) * nt] = gk
            keys.append(gk)
        ready(rec)
        t1[...] = dot(gst[slot, (5 + nq) * nt : (6 + nq) * nt], w[rec])
        for q in range(nq):
            ready(key + q)
        t0[...] = dot(jnp.concatenate(keys, axis=1), w[key : key + nq].reshape(nq * width, width))

        def put_mid(here, v):
            t3[here] = v
            gst[slot, 3 * nt + here.start : 3 * nt + here.stop] = v.astype(BF)

        mix_back(m, (t0, t1), xh2, r2, car2, 1, cmixes, lambda here: gbox[m, here].astype(F32), put_mid, 3, 7)
        ready(3)
        t0[...] = dot(gst[slot, 3 * nt : 4 * nt], w[3])
        nc, dc = back[0:1], back[1:2]
        for r in reversed(range(0, nt, ROWS)):
            here = slice(r, r + ROWS)
            gates = s_s[m, here].astype(F32)
            outs = []
            for r8 in (r + 8, r):
                rows = slice(r8, r8 + 8)
                gg = t0[rows]
                gate = gates[r8 - r : r8 - r + 8]
                e, v, num, den = e_s[m, rows], v_s[m, rows], n_s[m, rows], d_s[m, rows]
                b = bonus * e
                inv = 1.0 / (den + b)
                wkv = (num + b * v) * inv
                gw = gg * gate
                gn = gw * inv
                gr = gw * wkv * (1.0 - gate)
                gd = -gn * wkv
                an, nc = sums_behind(gn, nc, table)
                ad, dc = sums_behind(gd, dc, table)
                now = b * (gn * v + gd)
                acc[10] += now
                acc[9] += an * num + ad * den
                outs.append((e * (an * v + ad) + now, b * gn + e * an, gr))
            for c in range(3):
                both = jnp.concatenate([outs[1][c], outs[0][c]], axis=0)
                gst[slot, c * nt + r : c * nt + r + ROWS] = both.astype(BF)
        back[0:1] = nc
        back[1:2] = dc
        ready(0, 1, 2)
        for c, t in enumerate((t0, t1, t2)):
            t[...] = dot(gst[slot, c * nt : (c + 1) * nt], w[c])

        def put_out(here, v):
            gbox[m, here] = v.astype(BF)

        mix_back(m, (t0, t1, t2), xh1, r1, car1, 0, tmixes, lambda here: t3[here], put_out, 2, 4)

        @pl.when(layer > 0)
        def _():
            remote(gbox.at[m], gbox.at[m], g_send.at[m], g_recv.at[m], bp, bi).start()

        @pl.when(jnp.logical_and(layer == 0, m == 0))
        def _():
            local(gbox.at[m], tail, tail_sem).start()

        @pl.when(jnp.logical_and(layer == 0, m > 0))
        def _():
            q = lax.div(m, per)
            u = m - q * per
            mine = jnp.logical_and(q == p, first + k == i)
            give(gbox.at[m], gb.at[pl.ds(pl.multiple_of(u * nt, nt), nt)], g_send.at[m], gb_recv.at[u], q, first + k, mine)

        local(gst.at[slot], go.at[m], go_sem.at[slot]).start()
        return none

    backward(0, 0, True)
    lax.fori_loop(1, nm, backward, 0)
    for at in range(16):
        row = jnp.sum(acc[at], axis=0, keepdims=True)
        small[at : at + 1] = row * (-rate * fade) if at == 9 else row

    for slot in range(min(2, nm)):
        drain(xst.at[slot], x_sem.at[slot])
        drain(gst.at[slot], go_sem.at[slot])

    def finish(m, none):
        drain(relu.at[m], relu_sem.at[m])
        mine = jnp.logical_and(lax.div(m, per) == p, first + k == i)

        @pl.when(jnp.logical_not(jnp.logical_and(layer == last, mine)))
        def _():
            drain(inbox.at[m], in_send.at[m])

        @pl.when(jnp.logical_not(jnp.logical_and(layer == 0, jnp.logical_or(mine, m == 0))))
        def _():
            drain(gbox.at[m], g_send.at[m])

        return none

    lax.fori_loop(0, nm, finish, 0)
    for u in range(per):
        part = pl.ds(u * nt, nt)
        drain(ob.at[part], ob_recv.at[u])
        if u > 0:
            drain(gb.at[part], gb_recv.at[u])

        @pl.when(jnp.logical_not(in_self))
        def _():
            drain(x_hbm.at[0, part], x0_send.at[u])

        @pl.when(jnp.logical_not(cot_self))
        def _():
            drain(cot_hbm.at[0, part], cot_send.at[u])

    @pl.when(p > 0)
    def _():
        drain(gb.at[pl.ds(0, nt)], gb_recv.at[0])

    @pl.when(layer == 0)
    def _():
        drain(tail, tail_sem)

    @pl.when(jnp.logical_not(st_self))
    def _():
        for a, (src, dst) in enumerate(states):
            drain(dst, st_send.at[a])

    @pl.when(jnp.logical_not(fin_self))
    def _():
        for a, (src, dst) in enumerate(finals):
            drain(src, fin_send.at[a])

    for a, (src, dst) in enumerate(finals):
        drain(dst, fin_recv.at[a])

    @pl.when(owner)
    def _():
        for a, (src, dst) in enumerate(weights):
            drain(dst, w_send.at[a])


def sums_kernel(
    npipe, ngroups, guests, x_hbm, g_hbm, small, tail, out, out_small, out_tail,
    xb, gbuf, dws, xs, own, rx, rr, ag, xs_s, own_s, rx_s, rr_s, ag_s, gx, gsrc,
    x_sem, g_sem, ex_send, ex_recv, r_send, r_recv, a_send, a_recv, o_send, o_recv, small_send, small_recv,
    gx_send, gx_recv, guest_send, guest_ready, tail_send, tail_recv,
):
    p, i, y, k, first, s, m_chip = position()
    j = lax.div(i, 2)
    sib = 2 * y + 1 - k
    half, width = own.shape[1:]
    nc = rx.shape[0]
    low, high = GUEST_AT, GUEST_AT + guests
    lower = y == 0
    upper = y == 1
    quarter = half // 2
    rows_c = 2 * half
    split = width // rows_c
    nm, nt = xb.shape[1:3]
    nq = x_hbm.shape[1] // nt - 6
    hops = (ngroups - 1 - j, j)
    dist = (j, ngroups - 1 - j)
    step_by = (-1, 1)
    dest = 2 * y + m_chip
    other = first + 1 - s

    barrier = pltpu.get_barrier_semaphore()
    for bp, bi in ((sib, i), (p, other), (sib, other)):
        pl.semaphore_signal(barrier, inc=1, device_id=(bp, bi), device_id_type=MESH)

    @pl.when(j > 0)
    def _():
        pl.semaphore_signal(barrier, inc=1, device_id=(p, i - 2), device_id_type=MESH)

    @pl.when(j < ngroups - 1)
    def _():
        pl.semaphore_signal(barrier, inc=1, device_id=(p, i + 2), device_id_type=MESH)

    greeted = 3 + jnp.where(j > 0, 1, 0) + jnp.where(j < ngroups - 1, 1, 0)
    if guests:

        @pl.when(upper)
        def _():
            for bp, bi in ((k, i), (s, first), (s, first + 1)):
                pl.semaphore_signal(barrier, inc=1, device_id=(bp, bi), device_id_type=MESH)

        greeted = greeted + jnp.where(lower, 3, 0)

    maker = jnp.logical_and(lower, m_chip == 0)

    def enter():
        pl.semaphore_wait(barrier, greeted)

        @pl.when(jnp.logical_and(maker, k == 0))
        def _():
            local(tail, out_tail, tail_recv).start()

        @pl.when(jnp.logical_and(maker, k > 0))
        def _():
            remote(tail, out_tail, tail_send, tail_recv, 0, first + 1).start()

        if guests:

            @pl.when(lower)
            def _():
                for op in (2, 3):
                    pl.semaphore_signal(guest_ready, inc=1, device_id=(op, first + k), device_id_type=MESH)

    def blocks(c):
        b = lax.div(c, split)
        xi = jnp.where(b < 4, b, jnp.where(b < 4 + nq, 4, jnp.where(b < 4 + 2 * nq, b - nq + 2, 5)))
        gi = jnp.where(b < 4 + nq, b, jnp.where(b < 4 + 2 * nq, 4 + nq, 5 + nq))
        return b, xi, gi

    def loads(c, slot):
        b, xi, gi = blocks(c)
        part = c - b * split
        cols = pl.ds(pl.multiple_of(part * rows_c, rows_c), rows_c)
        return (
            local(x_hbm.at[:, pl.ds(pl.multiple_of(xi * nt, nt), nt), cols], xb.at[slot], x_sem.at[slot]),
            local(g_hbm.at[:, pl.ds(pl.multiple_of(gi * nt, nt), nt)], gbuf.at[slot], g_sem.at[slot]),
        )

    for copy in loads(0, 0):
        copy.start()

    def produce(c):
        slot = lax.rem(c, 2)

        @pl.when(c + 1 < nc)
        def _():
            for copy in loads(c + 1, 1 - slot):
                copy.start()

        for copy in loads(c, slot):
            copy.wait()
        b = lax.div(c, split)

        @pl.when(jnp.logical_and(b >= 4 + nq, b < 4 + 2 * nq))
        def _():
            r = xb[slot].astype(F32)
            xb[slot] = (r * r).astype(BF)

        dws[...] = lax.dot_general(
            xb[slot].reshape(nm * nt, rows_c), gbuf[slot].reshape(nm * nt, width), (((0,), (0,)), ((), ())),
            preferred_element_type=F32,
        )

        @pl.when(c >= 2)
        def _():
            drain(xs.at[slot], ex_send.at[slot])

        @pl.when(c == 0)
        def _():
            enter()

        xs[slot] = dws[pl.ds(pl.multiple_of((1 - k) * half, half), half)].astype(BF)
        remote(xs.at[slot], rx.at[c], ex_send.at[slot], ex_recv.at[c], sib, i).start()
        own[c] = dws[pl.ds(pl.multiple_of(k * half, half), half)]

        @pl.when(c == 0)
        def _():
            n = small.shape[0]
            mine = jnp.where(k == 0, 1.0, 0.0)
            own_s[...] = jnp.zeros_like(own_s)
            xs_s[...] = jnp.zeros_like(xs_s)
            own_s[0:n] = small[...] * mine
            xs_s[0:n] = (small[...] * (1.0 - mine)).astype(BF)
            remote(xs_s, rx_s, small_send.at[0], ex_recv.at[nc], sib, i).start()

    def welcome(c):
        @pl.when(c == nc)
        def _():
            pl.semaphore_wait(guest_ready, 2)

        drain(gx.at[c - nc], gx_recv.at[c - nc])
        own[c] = gx[c - nc].astype(F32)

    def exchange(c):
        drain(rx.at[c], ex_recv.at[c])
        own[c] = own[c] + rx[c].astype(F32)
        if guests:

            @pl.when(jnp.logical_and(lower, jnp.logical_and(c >= low, c < high)))
            def _():
                gsrc[c - low] = own[c].astype(BF)
                remote(gsrc.at[c - low], gx.at[c - low], gx_send.at[0], gx_recv.at[c - low], p + 2, i).start()

        @pl.when(c == 0)
        def _():
            drain(rx_s, ex_recv.at[nc])
            own_s[...] = own_s[...] + rx_s[...].astype(F32)

    def reduce(c, d):
        def one(value, rr_at, ag_at, send, recv):
            @pl.when(hops[d] == 0)
            def _():
                rr_at[...] = value().astype(BF)

            @pl.when(hops[d] > 0)
            def _():
                drain(rr_at, recv)

                @pl.when(dist[d] > 0)
                def _():
                    rr_at[...] = (value() + rr_at[...].astype(F32)).astype(BF)

                @pl.when(dist[d] == 0)
                def _():
                    ag_at[...] = (value() + rr_at[...].astype(F32)).astype(BF)

            @pl.when(dist[d] > 0)
            def _():
                remote(rr_at, rr_at, send, recv, p, i + 2 * step_by[d]).start()

            @pl.when(jnp.logical_and(dist[d] == 0, hops[d] == 0))
            def _():
                ag_at[...] = rr_at[...]

        one(lambda: own[c, d * quarter : (d + 1) * quarter], rr.at[d, c], ag.at[d, c], r_send.at[d], r_recv.at[d, c])

        @pl.when(c == 0)
        def _():
            n = rr_s.shape[1]
            one(lambda: own_s[d * n : (d + 1) * n], rr_s.at[d], ag_s.at[d], small_send.at[1 + d], r_recv.at[d, nc + guests])

    def spread(c, d):
        def come(ag_at, forward_send, recv):
            @pl.when(dist[d] > 0)
            def _():
                drain(ag_at, recv)

            @pl.when(hops[d] > 0)
            def _():
                remote(ag_at, ag_at, forward_send, recv, p, i - 2 * step_by[d]).start()

        def one(ag_at, to, forward_send, recv, local_send, far_send, out_recv):
            come(ag_at, forward_send, recv)
            remote(ag_at, to, far_send, out_recv, dest, other).start()

            @pl.when(p == dest)
            def _():
                local(ag_at, to, out_recv).start()

            @pl.when(p != dest)
            def _():
                remote(ag_at, to, local_send, out_recv, dest, i).start()

        def place(c):
            b = lax.div(c, split)
            row = (c - b * split) * rows_c + k * half + d * quarter
            return out.at[b, pl.ds(pl.multiple_of(row, quarter), quarter)]

        def own_chunk():
            one(ag.at[d, c], place(c), a_send.at[d], a_recv.at[d, c], o_send.at[0], o_send.at[1], o_recv.at[0])

        if guests:
            pl.when(c < nc)(own_chunk)

            @pl.when(c >= nc)
            def _():
                come(ag.at[d, c], a_send.at[d], a_recv.at[d, c])
                to = place(c - nc + low)
                remote(ag.at[d, c], to, guest_send.at[0], o_recv.at[0], s, i).start()
                remote(ag.at[d, c], to, guest_send.at[1], o_recv.at[0], s, other).start()
        else:
            own_chunk()

        @pl.when(c == 0)
        def _():
            n = rr_s.shape[1]
            to_s = out_small.at[pl.ds(pl.multiple_of(k * 2 * n + d * n, n), n)]
            one(ag_s.at[d], to_s, small_send.at[3 + d], a_recv.at[d, nc + guests], small_send.at[5 + d], small_send.at[7 + d], small_recv.at[0])

    def turn(u, own_work, guest_work=None):
        if not guests:

            @pl.when(jnp.logical_and(u >= 0, u < nc))
            def _():
                own_work(u)

            return
        at = min(GUEST_TURN, nc)
        c = jnp.where(u < at, u, jnp.where(u < at + guests, nc + u - at, u - guests))
        c = jnp.where(upper, c, u)
        mine = jnp.logical_and(u >= 0, u < nc + jnp.where(upper, guests, 0))
        if guest_work is not own_work:

            @pl.when(jnp.logical_and(mine, c < nc))
            def _():
                own_work(c)

            if guest_work is not None:

                @pl.when(jnp.logical_and(mine, c >= nc))
                def _():
                    guest_work(c)

        else:
            away = jnp.logical_and(lower, jnp.logical_and(c >= low, c < high))

            @pl.when(jnp.logical_and(mine, jnp.logical_not(away)))
            def _():
                own_work(c)

    def step(t, none):
        turn(t, produce)
        turn(t - 1, exchange, welcome)
        for d in range(2):
            work = functools.partial(reduce, d=d)
            turn(t - 1 - LAG * hops[d], work, work)
        for d in range(2):
            work = functools.partial(spread, d=d)
            turn(t - 1 - LAG * (ngroups - 1 + dist[d]), work, work)
        return none

    lax.fori_loop(0, nc + guests + 1 + 2 * LAG * (ngroups - 1), step, 0)

    def settle(ref, sem):
        if not guests:
            drain(ref, sem)
            return

        @pl.when(upper)
        def _():
            drain(ref, sem)

        @pl.when(lower)
        def _():
            drain(ref.at[pl.ds(0, low)], sem)
            drain(ref.at[pl.ds(high, nc - high)], sem)

    def settle_own(ref, sem):
        if not guests:
            drain(ref, sem)
            return
        drain(ref.at[pl.ds(0, low)], sem)
        drain(ref.at[pl.ds(high, nc - high)], sem)

        @pl.when(upper)
        def _():
            drain(ref.at[pl.ds(low, guests)], sem)

    for slot in range(min(2, nc)):
        drain(xs.at[slot], ex_send.at[slot])
    drain(xs_s, small_send.at[0])
    for d in range(2):

        @pl.when(dist[d] > 0)
        def _():
            settle(rr.at[d], r_send.at[d])
            drain(rr_s.at[d], small_send.at[1 + d])

        @pl.when(hops[d] > 0)
        def _():
            settle(ag.at[d], a_send.at[d])
            drain(ag_s.at[d], small_send.at[3 + d])

        @pl.when(p != dest)
        def _():
            drain(ag_s.at[d], small_send.at[5 + d])

        drain(ag_s.at[d], small_send.at[7 + d])

    for d in range(2):

        @pl.when(p != dest)
        def _():
            settle_own(ag.at[d], o_send.at[0])

        settle_own(ag.at[d], o_send.at[1])
    if guests:

        @pl.when(lower)
        def _():
            drain(gsrc, gx_send.at[0])

        @pl.when(upper)
        def _():
            for d in range(2):
                drain(ag.at[d, pl.ds(nc, guests)], guest_send.at[0])
                drain(ag.at[d, pl.ds(nc, guests)], guest_send.at[1])

    @pl.when(jnp.logical_and(maker, k > 0))
    def _():
        drain(tail, tail_send)

    @pl.when(p == 0)
    def _():
        drain(out_tail, tail_recv)

    drain(out, o_recv.at[0])
    drain(out_small, small_recv.at[0])


def widen_kernel(
    ob, gb, rows, w, tail, num, den, last,
    out, grad, g_in, g_out, g_key, g_val, g_rec, gain, bias, tmix, cmix, decay, bonus, fin_num, fin_den, fin_rows,
    stage, narrow, wide, sem, in_sem, out_sem,
):
    nblocks, width, _ = w.shape
    slots, step, _ = stage.shape
    nq, cuts = (nblocks - 5) // 2, width // step
    for n, src in enumerate((ob, gb)):
        local(src, narrow.at[n], in_sem.at[n]).start()

    def one(t, none):
        slot = lax.rem(t, slots)
        b = lax.div(t, cuts)
        cut = pl.ds(pl.multiple_of((t - b * cuts) * step, step), step)

        @pl.when(t >= slots)
        def _():
            drain(stage.at[slot], sem.at[slot])

        stage[slot] = w[b, cut].astype(F32)

        @pl.when(b < 3)
        def _():
            local(stage.at[slot], g_in.at[b, cut], sem.at[slot]).start()

        @pl.when(b == 3)
        def _():
            local(stage.at[slot], g_out.at[0, cut], sem.at[slot]).start()

        for q in range(nq):

            @pl.when(b == 4 + q)
            def _():
                local(stage.at[slot], g_key.at[cut, q * width : (q + 1) * width], sem.at[slot]).start()

        @pl.when(jnp.logical_and(b >= 4 + nq, b < 4 + 2 * nq))
        def _():
            local(stage.at[slot], g_val.at[b - 4 - nq, cut], sem.at[slot]).start()

        @pl.when(b == 4 + 2 * nq)
        def _():
            local(stage.at[slot], g_rec.at[0, cut], sem.at[slot]).start()

        return none

    lax.fori_loop(0, nblocks * cuts, one, 0)
    for n, dst in enumerate((out, grad)):
        drain(narrow.at[n], in_sem.at[n])
        wide[n] = narrow[n].astype(F32)
        if n == 1:

            @pl.when(lax.axis_index("pipe") == 0)
            def _():
                wide[n, 0 : tail.shape[0]] = tail[...].astype(F32)

        local(wide.at[n], dst, out_sem.at[n]).start()
    at = 0
    for dst in (gain, bias, tmix, cmix, decay, bonus):
        n = dst.shape[0]
        dst[...] = rows[at : at + n].astype(F32).reshape(dst.shape)
        at += n
    for src, dst in ((num, fin_num), (den, fin_den), (last, fin_rows)):
        dst[...] = src[...]
    for slot in range(slots):
        drain(stage.at[slot], sem.at[slot])
    for n in range(2):
        drain(wide.at[n], out_sem.at[n])


def body(
    block_input, ln_gain, ln_bias, tm_mix, cm_mix, time_decay, time_first, tm_in, tm_out,
    cm_key, cm_value, cm_recept, wkv_num, wkv_den, last_rows, cotangent,
):
    npipe, ndp = lax.axis_size("pipe"), lax.axis_size("dp")
    seg, width = block_input.shape[1:]
    hidden = cm_key.shape[2]
    nq = hidden // width
    length = seg * npipe
    nt = min(TOKENS, seg)
    nm, per = length // nt, seg // nt
    anywhere = pl.BlockSpec(memory_space=pl.ANY)
    vmem = pl.BlockSpec(memory_space=pltpu.VMEM)
    dma = pltpu.SemaphoreType.DMA
    shape = jax.ShapeDtypeStruct
    nb = 6 + nq
    nblocks = 5 + 2 * nq
    xs, gs, small, fin_num, fin_den, fin_rows, ob, gb, turned, tail = pl.pallas_call(
        functools.partial(layers_kernel, npipe),
        name="layers",
        out_shape=[
            shape((nm, nb * nt, width), BF),
            shape((nm, nb * nt, width), BF),
            shape((16, width), F32),
            shape((1, 1, width), F32),
            shape((1, 1, width), F32),
            shape((1, 2, 1, width), F32),
            shape((seg, width), BF),
            shape((seg, width), BF),
            shape((nblocks, width, width), BF),
            shape((nt, width), BF),
        ],
        in_specs=[anywhere] * 16,
        out_specs=[anywhere, anywhere, vmem] + [anywhere] * 7,
        scratch_shapes=[
            pltpu.VMEM((nblocks, width, width), BF),
            pltpu.VMEM((2, width), F32),
            pltpu.VMEM((2, width), F32),
            pltpu.VMEM((3, 1, width), F32),
            pltpu.VMEM((2, width), F32),
            pltpu.VMEM((1, width), F32),
            pltpu.VMEM((1, width), F32),
            pltpu.VMEM((1, width), F32),
            pltpu.VMEM((1, width), F32),
            pltpu.VMEM((2, width), F32),
            pltpu.VMEM((nm, nt, width), BF),
            pltpu.VMEM((nm, nt, width), BF),
            *[pltpu.VMEM((nm, nt, width), F32)] * 4,
            *[pltpu.VMEM((nm, nt, width), BF)] * 5,
            pltpu.VMEM((nm, nq * nt, width), BF),
            *[pltpu.VMEM((nm, nt, 1), F32)] * 2,
            *[pltpu.VMEM((nm, 8, width), F32)] * 2,
            pltpu.VMEM((8, width), F32),
            pltpu.VMEM((16, 8, width), F32),
            pltpu.VMEM((2, 6 * nt, width), BF),
            pltpu.VMEM((2, nb * nt, width), BF),
            pltpu.VMEM((8, 8, width), F32),
            *[pltpu.VMEM((nt, width), F32)] * 4,
            dma((6 + nblocks,)), dma((6 + nblocks,)), dma((nm,)), dma((nm,)), dma((nm,)), dma((nm,)),
            dma((per,)), dma((per,)), dma((per,)), dma((per,)),
            dma((3,)), dma((3,)), dma((3,)), dma((3,)), dma((2,)), dma((2,)), dma((nm,)), dma((2,)), dma((nblocks,)), dma,
        ],
        compiler_params=pltpu.CompilerParams(collective_id=0, has_side_effects=True, vmem_limit_bytes=VMEM_BYTES),
    )(block_input, cotangent, ln_gain, ln_bias, jnp.swapaxes(tm_mix, 0, 1), cm_mix, time_decay, time_first, wkv_num, wkv_den, last_rows,
      tm_in, tm_out, cm_key, cm_value, cm_recept)

    rows_c = width // SPLIT if width % (128 * SPLIT) == 0 else width // 2
    nc, half = nblocks * (width // rows_c), rows_c // 2
    quarter = half // 2
    guests = GUESTS if npipe == 4 else 0
    all_c = nc + guests
    out, out_small, out_tail = pl.pallas_call(
        functools.partial(sums_kernel, npipe, ndp // 2, guests),
        name="sums",
        out_shape=[ON_CHIP((nblocks, width, width), BF), ON_CHIP((64, width), BF), ON_CHIP((nt, width), BF)],
        in_specs=[anywhere, anywhere, vmem, anywhere],
        out_specs=[vmem, vmem, vmem],
        scratch_shapes=[
            pltpu.VMEM((2, nm, nt, rows_c), BF),
            pltpu.VMEM((2, nm, nt, width), BF),
            pltpu.VMEM((rows_c, width), F32),
            pltpu.VMEM((2, half, width), BF),
            pltpu.VMEM((all_c, half, width), F32),
            pltpu.VMEM((nc, half, width), BF),
            pltpu.VMEM((2, all_c, quarter, width), BF),
            pltpu.VMEM((2, all_c, quarter, width), BF),
            pltpu.VMEM((32, width), BF),
            pltpu.VMEM((32, width), F32),
            pltpu.VMEM((32, width), BF),
            pltpu.VMEM((2, 16, width), BF),
            pltpu.VMEM((2, 16, width), BF),
            pltpu.VMEM((max(guests, 1), half, width), BF),
            pltpu.VMEM((max(guests, 1), half, width), BF),
            dma((2,)), dma((2,)), dma((2,)), dma((nc + 1,)), dma((2,)), dma((2, all_c + 1)), dma((2,)), dma((2, all_c + 1)),
            dma((2,)), dma((1,)), dma((9,)), dma((1,)), dma((1,)), dma((max(guests, 1),)), dma((2,)), pltpu.SemaphoreType.REGULAR, dma, dma,
        ],
        compiler_params=pltpu.CompilerParams(collective_id=1, has_side_effects=True, vmem_limit_bytes=SUMS_BYTES),
    )(xs, gs, small, tail)

    in_vmem = pltpu.with_memory_space_constraint(out, pltpu.VMEM)
    wide = pl.pallas_call(
        widen_kernel,
        name="widen",
        out_shape=[
            shape((seg, width), F32), shape((seg, width), F32), shape((3, width, width), F32), shape((1, width, width), F32),
            shape((width, hidden), F32), shape((nq, width, width), F32), shape((1, width, width), F32),
            shape((2, width), F32), shape((2, width), F32), shape((3, 1, width), F32), shape((2, width), F32),
            shape((1, width), F32), shape((1, width), F32),
            shape((1, 1, width), F32), shape((1, 1, width), F32), shape((1, 2, 1, width), F32),
        ],
        in_specs=[anywhere, anywhere, vmem, vmem, vmem, vmem, vmem, vmem],
        out_specs=[anywhere] * 7 + [vmem] * 9,
        scratch_shapes=[
            pltpu.VMEM((4, width // 2, width), F32),
            pltpu.VMEM((2, seg, width), BF),
            pltpu.VMEM((2, seg, width), F32),
            dma((4,)), dma((2,)), dma((2,)),
        ],
        compiler_params=pltpu.CompilerParams(vmem_limit_bytes=WIDEN_BYTES),
    )(ob, gb, out_small, in_vmem, out_tail, fin_num, fin_den, fin_rows)
    return (
        wide[0][None],
        wide[1][None],
        wide[7][None],
        wide[8][None],
        jnp.swapaxes(wide[9], 0, 1),
        wide[10][None],
        wide[11],
        wide[12],
        wide[2][None],
        wide[3],
        wide[4][None],
        wide[5].reshape(1, hidden, width),
        wide[6],
        wide[13],
        wide[14],
        wide[15],
    )


def solution(mesh):
    args = (
        P("dp", "pipe", None),
        P("pipe", None, None),
        P("pipe", None, None),
        P("pipe", None, None),
        P("pipe", None, None),
        P("pipe", None),
        P("pipe", None),
        P("pipe", None, None, None),
        P("pipe", None, None),
        P("pipe", None, None),
        P("pipe", None, None),
        P("pipe", None, None),
        P("pipe", "dp", None),
        P("pipe", "dp", None),
        P("pipe", None, "dp", None),
        P("dp", "pipe", None),
    )
    outs = (
        P("dp", "pipe", None),
        P("dp", "pipe", None),
        P("pipe", None, None),
        P("pipe", None, None),
        P("pipe", None, None),
        P("pipe", None, None),
        P("pipe", None),
        P("pipe", None),
        P("pipe", None, None, None),
        P("pipe", None, None),
        P("pipe", None, None),
        P("pipe", None, None),
        P("pipe", None, None),
        P("pipe", "dp", None),
        P("pipe", "dp", None),
        P("pipe", None, "dp", None),
    )
    return jax.shard_map(body, mesh=mesh, in_specs=args, out_specs=outs, check_vma=False)
```

```python
import functools

import jax
import jax.numpy as jnp
from jax import lax
from jax.experimental import pallas as pl
from jax.experimental.pallas import tpu as pltpu
from jax.sharding import PartitionSpec as P

ON_CHIP = pltpu.VMEM
MESH = pl.DeviceIdType.MESH
BF, F32 = jnp.bfloat16, jnp.float32
TOKENS = 128
ROWS = 16
SPLIT = 6
LAG = 3
GUESTS = 3
GUEST_AT = 24
GUEST_TURN = 50
VMEM_BYTES = 62 * 1024 * 1024
SUMS_BYTES = 47 * 1024 * 1024
WIDEN_BYTES = 16 * 1024 * 1024


def position():
    p, i = lax.axis_index("pipe"), lax.axis_index("dp")
    y = lax.div(p, 2)
    k = p - 2 * y
    first = 2 * lax.div(i, 2)
    s = i - first
    return p, i, y, k, first, s, lax.rem(s + y, 2)


def home(layer, k, first):
    y = lax.div(layer, 2)
    return 2 * y + k, first + lax.rem(layer - y, 2)


def local(src, dst, sem):
    return pltpu.make_async_copy(src, dst, sem)


def remote(src, dst, send, recv, p, i):
    return pltpu.make_async_remote_copy(
        src_ref=src, dst_ref=dst, send_sem=send, recv_sem=recv, device_id=(p, i), device_id_type=MESH
    )


def drain(ref, sem):
    pltpu.make_async_copy(ref, ref, sem).wait()


def dot(a, b):
    return lax.dot_general(a, b, (((1,), (0,)), ((), ())), preferred_element_type=F32)


def dot_t(a, b):
    return lax.dot_general(a, b, (((1,), (1,)), ((), ())), preferred_element_type=F32)


def later(v, row):
    at = lax.broadcasted_iota(jnp.int32, v.shape, 0)
    return jnp.where(at == 0, row, pltpu.roll(v, 1, 0))


def earlier(v, row):
    n = v.shape[0]
    at = lax.broadcasted_iota(jnp.int32, v.shape, 0)
    return jnp.where(at == n - 1, row, pltpu.roll(v, n - 1, 0))


def fade_tables(table, rate):
    at = lax.broadcasted_iota(jnp.int32, table.shape[1:], 0)
    for n, by in enumerate((1, 2, 4)):
        fade = jnp.exp(-float(by) * rate)
        table[n] = jnp.where(at >= by, fade, 0.0)
        table[4 + n] = jnp.where(at < 8 - by, fade, 0.0)
    far = at.astype(F32)
    table[3] = jnp.exp(-(far + 1.0) * rate)
    table[7] = jnp.exp(-(8.0 - far) * rate)


def sums_before(v, carry, table):
    for n, by in enumerate((1, 2, 4)):
        v = v + table[n] * pltpu.roll(v, by, 0)
    v = v + table[3] * carry
    return later(v, carry), v[7:8]


def sums_behind(v, carry, table):
    for n, by in enumerate((1, 2, 4)):
        v = v + table[4 + n] * pltpu.roll(v, 8 - by, 0)
    v = v + table[7] * carry
    return earlier(v, carry), v[0:1]


def centred(v):
    c = v - jnp.mean(v, axis=-1, keepdims=True)
    r = lax.rsqrt(jnp.mean(c * c, axis=-1, keepdims=True) + 1e-05)
    return c * r, r


def layers_kernel(
    npipe,
    x_hbm, cot_hbm, gain_hbm, bias_hbm, tmix_hbm, cmix_hbm, decay_hbm, first_hbm, num_hbm, den_hbm, rows_hbm,
    win_hbm, wout_hbm, wck_hbm, wcv_hbm, wcr_hbm,
    xo, go, small, fin_num, fin_den, fin_rows, ob, gb, turned, tail,
    w, gain, bias, tmix, cmix, decay, bonus_s, num_s, den_s, rows_s, inbox, gbox,
    e_s, v_s, n_s, d_s, s_s, xh1, xh2, s2_s, c2_s, relu, r1, r2, car1, car2, back, acc, xst, gst, table, t0, t1, t2, t3,
    w_send, w_recv, in_send, in_recv, g_send, g_recv, x0_send, cot_send, ob_recv, gb_recv,
    st_send, st_recv, fin_send, fin_recv, x_sem, go_sem, relu_sem, turn_out, turn_in, tail_sem,
):
    p, i, y, k, first, s, m_chip = position()
    layer = 2 * y + m_chip
    last = npipe - 1
    nm, nt, width = inbox.shape
    nq = relu.shape[1] // nt
    per = x_hbm.shape[1] // nt
    nblocks = w.shape[0]
    key, val, rec = 4, 4 + nq, 4 + 2 * nq

    weights = [(gain_hbm.at[0], gain), (bias_hbm.at[0], bias), (tmix_hbm, tmix), (cmix_hbm.at[0], cmix),
               (decay_hbm, decay), (first_hbm, bonus_s)]
    base = len(weights)
    order = [0, 1, 2, 3] + [key + q for q in range(nq)] + [rec] + [val + q for q in range(nq)]
    source = {rec: wcr_hbm.at[0], 3: wout_hbm.at[0]}
    for c in range(3):
        source[c] = win_hbm.at[0, c]
    for q in range(nq):
        source[key + q] = wck_hbm.at[0, :, q * width : (q + 1) * width]
        source[val + q] = wcv_hbm.at[0, q * width : (q + 1) * width]
    weights += [(source[at], w.at[at]) for at in order]
    place = {at: base + n for n, at in enumerate(order)}
    owner = k == m_chip

    barrier = pltpu.get_barrier_semaphore()
    for step in range(1, 2 * npipe):
        at = lax.rem(2 * p + s + step, 2 * npipe)
        op = lax.div(at, 2)
        pl.semaphore_signal(barrier, inc=1, device_id=(op, first + at - 2 * op), device_id_type=MESH)
    pl.semaphore_wait(barrier, 2 * npipe - 1)

    ip, ii = home(0, s, first)
    in_self = jnp.logical_and(ip == p, ii == i)
    cp, ci = home(last, s, first)
    cot_self = jnp.logical_and(cp == p, ci == i)
    tp, ti = home(p, s, first)
    st_self = jnp.logical_and(tp == p, ti == i)

    def give(src, dst, send, recv, dp, di, mine):
        @pl.when(mine)
        def _():
            local(src, dst, recv).start()

        @pl.when(jnp.logical_not(mine))
        def _():
            remote(src, dst, send, recv, dp, di).start()

    states = ((num_hbm.at[0], num_s), (den_hbm.at[0], den_s), (rows_hbm.at[0, :, 0], rows_s))

    @pl.when(owner)
    def _():
        for a, (src, dst) in enumerate(weights[:base]):
            remote(src, dst, w_send.at[a], w_recv.at[a], 2 * y + 1 - k, i).start()

    @pl.when(owner)
    def _():
        for a, (src, dst) in enumerate(weights[base:]):
            remote(src, dst, w_send.at[base + a], w_recv.at[base + a], 2 * y + 1 - k, i).start()

    @pl.when(owner)
    def _():
        for a, (src, dst) in enumerate(weights):
            local(src, dst, w_recv.at[a]).start()

    def give_input(u):
        give(x_hbm.at[0, pl.ds(u * nt, nt)], inbox.at[p * per + u], x0_send.at[u], in_recv.at[p * per + u], ip, ii, in_self)

    @pl.when(p == 0)
    def _():
        give_input(0)

    for a, (src, dst) in enumerate(states):
        give(src, dst, st_send.at[a], st_recv.at[a], tp, ti, st_self)

    for a in range(base):
        drain(weights[a][1], w_recv.at[a])
    for a, (src, dst) in enumerate(states):
        drain(dst, st_recv.at[a])

    @pl.when(p > 0)
    def _():
        give_input(0)

    for u in range(1, per):
        give_input(u)
    for u in range(per):
        give(cot_hbm.at[0, pl.ds(u * nt, nt)], gbox.at[p * per + u], cot_send.at[u], g_recv.at[p * per + u], cp, ci, cot_self)
    np_, ni = home(layer + 1, k, first)
    bp, bi = home(layer - 1, k, first)
    rate = jnp.exp(decay[...])
    bonus = jnp.exp(bonus_s[...])
    fade = jnp.exp(-rate)
    fade_tables(table, rate)
    tmixes = [tmix[c] for c in range(3)]
    cmixes = [cmix[c : c + 1] for c in range(2)]

    @pl.when(layer == last)
    def _():
        for at in order:
            drain(w.at[at], w_recv.at[place[at]])

        def turn(n, none):
            slot = lax.rem(n, 2)
            at = lax.rem(n + val + 2, nblocks)

            @pl.when(n >= 2)
            def _():
                drain(gst.at[slot, pl.ds(0, width)], turn_out.at[slot])

            gst[slot, 0:width] = w[at].T
            local(gst.at[slot, pl.ds(0, width)], turned.at[at], turn_out.at[slot]).start()
            return none

        lax.fori_loop(0, nblocks, turn, 0)
        for slot in range(2):
            drain(gst.at[slot, pl.ds(0, width)], turn_out.at[slot])

    def forward(m, none, begin=False):
        slot = lax.rem(m, 2)

        def ready(*blocks):
            if begin:

                @pl.when(layer < last)
                def _():
                    for at in blocks:
                        drain(w.at[at], w_recv.at[place[at]])

        if not begin:

            @pl.when(m >= 2)
            def _():
                drain(xst.at[slot], x_sem.at[slot])

        drain(inbox.at[m], in_recv.at[m])
        def norm_mix(rows_of, which, xh_s, r_s, car, mixes, to):
            before = rows_s[which : which + 1]
            car[m, 0:1] = before
            for r in range(0, nt, ROWS):
                here = slice(r, r + ROWS)
                xh, rs = centred(rows_of(here))
                xh_s[m, here] = xh.astype(BF)
                r_s[m, here] = rs
                xn = xh * gain[which : which + 1] + bias[which : which + 1]
                xp = later(xn, before)
                before = xn[ROWS - 1 :]
                d = xn - xp
                for c, mix in enumerate(mixes):
                    xst[slot, (to + c) * nt + r : (to + c) * nt + r + ROWS] = (xp + mix * d).astype(BF)
            rows_s[which : which + 1] = before

        norm_mix(lambda here: inbox[m, here].astype(F32), 0, xh1, r1, car1, tmixes, 0)
        ready(0)
        t0[...] = dot(xst[slot, 0:nt], w[0])
        ready(1)
        v_s[m] = dot(xst[slot, nt : 2 * nt], w[1])
        ready(2)
        t2[...] = dot(xst[slot, 2 * nt : 3 * nt], w[2])
        nc, dc = num_s[...], den_s[...]
        for r in range(0, nt, ROWS):
            here = slice(r, r + ROWS)
            gate = jax.nn.sigmoid(t2[here])
            s_s[m, here] = gate.astype(BF)
            wkv = []
            for r8 in range(r, r + ROWS, 8):
                rows = slice(r8, r8 + 8)
                e = jnp.exp(t0[rows])
                v = v_s[m, rows]
                num, nc = sums_before(e * v, nc, table)
                den, dc = sums_before(e, dc, table)
                e_s[m, rows] = e
                n_s[m, rows] = num
                d_s[m, rows] = den
                b = bonus * e
                wkv.append((num + b * v) / (den + b))
            xst[slot, 3 * nt + r : 3 * nt + r + ROWS] = (gate * jnp.concatenate(wkv, axis=0)).astype(BF)
        num_s[...] = nc
        den_s[...] = dc
        ready(3)
        t1[...] = dot(xst[slot, 3 * nt : 4 * nt], w[3])

        def middle(here):
            mid = inbox[m, here].astype(F32) + t1[here]
            t1[here] = mid
            return mid

        norm_mix(middle, 1, xh2, r2, car2, cmixes, 4)
        squares = []
        for q in range(nq):
            ready(key + q)
            r = jnp.maximum(dot(xst[slot, 4 * nt : 5 * nt], w[key + q]), 0.0)
            relu[m, q * nt : (q + 1) * nt] = r.astype(BF)
            squares.append((r * r).astype(BF))
        ready(rec)
        t2[...] = dot(xst[slot, 5 * nt : 6 * nt], w[rec])
        if begin:
            for q in range(nq):
                ready(val + q)
                part = dot(squares[q], w[val + q])
                t0[...] = part if q == 0 else t0[...] + part
        else:
            t0[...] = dot(jnp.concatenate(squares, axis=1), w[val : val + nq].reshape(nq * width, width))
        for r in range(0, nt, ROWS):
            here = slice(r, r + ROWS)
            gate = jax.nn.sigmoid(t2[here])
            out = t0[here]
            s2_s[m, here] = gate.astype(BF)
            gated = gate * out
            c2_s[m, here] = (gated * (1.0 - gate)).astype(BF)
            inbox[m, here] = (t1[here] + gated).astype(BF)

        @pl.when(layer < last)
        def _():
            remote(inbox.at[m], inbox.at[m], in_send.at[m], in_recv.at[m], np_, ni).start()

        @pl.when(layer == last)
        def _():
            q = lax.div(m, per)
            u = m - q * per
            mine = jnp.logical_and(q == p, first + k == i)
            give(inbox.at[m], ob.at[pl.ds(pl.multiple_of(u * nt, nt), nt)], in_send.at[m], ob_recv.at[u], q, first + k, mine)

        local(xst.at[slot], xo.at[m, pl.ds(0, 6 * nt)], x_sem.at[slot]).start()
        local(relu.at[m], xo.at[m, pl.ds(6 * nt, nq * nt)], relu_sem.at[m]).start()
        return none

    forward(0, 0, True)
    lax.fori_loop(1, nm, forward, 0)

    wanted = [val + q for q in range(1, nq)] + [rec] + [key + q for q in range(nq)] + [3, 0, 1, 2]

    @pl.when(layer == last)
    def _():
        for at in wanted:
            local(turned.at[at], w.at[at], turn_in.at[at]).start()
        w[val] = gst[1, 0:width]

    finals = ((num_s, fin_num.at[0]), (den_s, fin_den.at[0]), (rows_s, fin_rows.at[0, :, 0]))
    fp, fi = layer, first + k
    fin_self = jnp.logical_and(fp == p, fi == i)
    for a, (src, dst) in enumerate(finals):
        give(src, dst, fin_send.at[a], fin_recv.at[a], fp, fi, fin_self)

    @pl.when(layer < last)
    def _():
        def turn(at, none):
            w[at] = w[at].T
            return none

        lax.fori_loop(0, nblocks, turn, 0)

    back[...] = jnp.zeros_like(back)
    acc[...] = jnp.zeros_like(acc)

    def note(at, v):
        acc[at] += v[0:8] + v[8:16]

    def mix_back(m, parts, xh_s, r_s, car, which, mixes, rows_of, put, back_at, acc_mix):
        gain_row, bias_row = gain[which : which + 1], bias[which : which + 1]
        behind = back[back_at : back_at + 1]
        for r in reversed(range(0, nt, ROWS)):
            here = slice(r, r + ROWS)
            xh = xh_s[m, here].astype(F32)
            xn = xh * gain_row + bias_row
            if r == 0:
                before = car[m, 0:1]
            else:
                before = xh_s[m, r - ROWS : r].astype(F32)[ROWS - 1 :] * gain_row + bias_row
            d = xn - later(xn, before)
            own, total = None, None
            for c, part in enumerate(parts):
                g = part[here]
                note(acc_mix + c, g * d)
                mixed = g * mixes[c]
                own = mixed if own is None else own + mixed
                total = g if total is None else total + g
            shifted = total - own
            gx = own + earlier(shifted, behind)
            behind = shifted[0:1]
            note(which, gx * xh)
            note(2 + which, gx)
            gp = gx * gain_row
            centre = jnp.mean(gp, axis=-1, keepdims=True)
            slope = jnp.mean(gp * xh, axis=-1, keepdims=True)
            put(here, rows_of(here) + r_s[m, here] * (gp - centre - xh * slope))
        back[back_at : back_at + 1] = behind

    def backward(step, none, begin=False):
        m = nm - 1 - step
        slot = lax.rem(step, 2)

        def ready(*blocks):
            if begin:

                @pl.when(layer == last)
                def _():
                    for at in blocks:
                        if at in wanted:
                            drain(w.at[at], turn_in.at[at])

        if not begin:

            @pl.when(step >= 2)
            def _():
                drain(gst.at[slot], go_sem.at[slot])

        drain(gbox.at[m], g_recv.at[m])
        for r in range(0, nt, ROWS):
            here = slice(r, r + ROWS)
            g = gbox[m, here].astype(F32)
            gst[slot, (4 + nq) * nt + r : (4 + nq) * nt + r + ROWS] = (g * s2_s[m, here].astype(F32)).astype(BF)
            gst[slot, (5 + nq) * nt + r : (5 + nq) * nt + r + ROWS] = (g * c2_s[m, here].astype(F32)).astype(BF)
        keys = []
        for q in range(nq):
            ready(val + q)
            gs = dot(gst[slot, (4 + nq) * nt : (5 + nq) * nt], w[val + q]).astype(BF)
            r = relu[m, q * nt : (q + 1) * nt]
            gk = gs * (r + r)
            gst[slot, (4 + q) * nt : (5 + q) * nt] = gk
            keys.append(gk)
        ready(rec)
        t1[...] = dot(gst[slot, (5 + nq) * nt : (6 + nq) * nt], w[rec])
        for q in range(nq):
            ready(key + q)
        t0[...] = dot(jnp.concatenate(keys, axis=1), w[key : key + nq].reshape(nq * width, width))

        def put_mid(here, v):
            t3[here] = v
            gst[slot, 3 * nt + here.start : 3 * nt + here.stop] = v.astype(BF)

        mix_back(m, (t0, t1), xh2, r2, car2, 1, cmixes, lambda here: gbox[m, here].astype(F32), put_mid, 3, 7)
        ready(3)
        t0[...] = dot(gst[slot, 3 * nt : 4 * nt], w[3])
        nc, dc = back[0:1], back[1:2]
        for r in reversed(range(0, nt, ROWS)):
            here = slice(r, r + ROWS)
            gates = s_s[m, here].astype(F32)
            outs = []
            for r8 in (r + 8, r):
                rows = slice(r8, r8 + 8)
                gg = t0[rows]
                gate = gates[r8 - r : r8 - r + 8]
                e, v, num, den = e_s[m, rows], v_s[m, rows], n_s[m, rows], d_s[m, rows]
                b = bonus * e
                inv = 1.0 / (den + b)
                wkv = (num + b * v) * inv
                gw = gg * gate
                gn = gw * inv
                gr = gw * wkv * (1.0 - gate)
                gd = -gn * wkv
                an, nc = sums_behind(gn, nc, table)
                ad, dc = sums_behind(gd, dc, table)
                now = b * (gn * v + gd)
                acc[10] += now
                acc[9] += an * num + ad * den
                outs.append((e * (an * v + ad) + now, b * gn + e * an, gr))
            for c in range(3):
                both = jnp.concatenate([outs[1][c], outs[0][c]], axis=0)
                gst[slot, c * nt + r : c * nt + r + ROWS] = both.astype(BF)
        back[0:1] = nc
        back[1:2] = dc
        ready(0, 1, 2)
        for c, t in enumerate((t0, t1, t2)):
            t[...] = dot(gst[slot, c * nt : (c + 1) * nt], w[c])

        def put_out(here, v):
            gbox[m, here] = v.astype(BF)

        mix_back(m, (t0, t1, t2), xh1, r1, car1, 0, tmixes, lambda here: t3[here], put_out, 2, 4)

        @pl.when(layer > 0)
        def _():
            remote(gbox.at[m], gbox.at[m], g_send.at[m], g_recv.at[m], bp, bi).start()

        @pl.when(jnp.logical_and(layer == 0, m == 0))
        def _():
            local(gbox.at[m], tail, tail_sem).start()

        @pl.when(jnp.logical_and(layer == 0, m > 0))
        def _():
            q = lax.div(m, per)
            u = m - q * per
            mine = jnp.logical_and(q == p, first + k == i)
            give(gbox.at[m], gb.at[pl.ds(pl.multiple_of(u * nt, nt), nt)], g_send.at[m], gb_recv.at[u], q, first + k, mine)

        local(gst.at[slot], go.at[m], go_sem.at[slot]).start()
        return none

    backward(0, 0, True)
    lax.fori_loop(1, nm, backward, 0)
    for at in range(16):
        row = jnp.sum(acc[at], axis=0, keepdims=True)
        small[at : at + 1] = row * (-rate * fade) if at == 9 else row

    for slot in range(min(2, nm)):
        drain(xst.at[slot], x_sem.at[slot])
        drain(gst.at[slot], go_sem.at[slot])

    def finish(m, none):
        drain(relu.at[m], relu_sem.at[m])
        mine = jnp.logical_and(lax.div(m, per) == p, first + k == i)

        @pl.when(jnp.logical_not(jnp.logical_and(layer == last, mine)))
        def _():
            drain(inbox.at[m], in_send.at[m])

        @pl.when(jnp.logical_not(jnp.logical_and(layer == 0, jnp.logical_or(mine, m == 0))))
        def _():
            drain(gbox.at[m], g_send.at[m])

        return none

    lax.fori_loop(0, nm, finish, 0)
    for u in range(per):
        part = pl.ds(u * nt, nt)
        drain(ob.at[part], ob_recv.at[u])
        if u > 0:
            drain(gb.at[part], gb_recv.at[u])

        @pl.when(jnp.logical_not(in_self))
        def _():
            drain(x_hbm.at[0, part], x0_send.at[u])

        @pl.when(jnp.logical_not(cot_self))
        def _():
            drain(cot_hbm.at[0, part], cot_send.at[u])

    @pl.when(p > 0)
    def _():
        drain(gb.at[pl.ds(0, nt)], gb_recv.at[0])

    @pl.when(layer == 0)
    def _():
        drain(tail, tail_sem)

    @pl.when(jnp.logical_not(st_self))
    def _():
        for a, (src, dst) in enumerate(states):
            drain(dst, st_send.at[a])

    @pl.when(jnp.logical_not(fin_self))
    def _():
        for a, (src, dst) in enumerate(finals):
            drain(src, fin_send.at[a])

    for a, (src, dst) in enumerate(finals):
        drain(dst, fin_recv.at[a])

    @pl.when(owner)
    def _():
        for a, (src, dst) in enumerate(weights):
            drain(dst, w_send.at[a])


def sums_kernel(
    npipe, ngroups, guests, x_hbm, g_hbm, small, tail, out, out_small, out_tail,
    xb, gbuf, dws, xs, own, rx, rr, ag, xs_s, own_s, rx_s, rr_s, ag_s, gx, gsrc,
    x_sem, g_sem, ex_send, ex_recv, r_send, r_recv, a_send, a_recv, o_send, o_recv, small_send, small_recv,
    gx_send, gx_recv, guest_send, guest_ready, tail_send, tail_recv,
):
    p, i, y, k, first, s, m_chip = position()
    j = lax.div(i, 2)
    sib = 2 * y + 1 - k
    half, width = own.shape[1:]
    nc = rx.shape[0]
    low, high = GUEST_AT, GUEST_AT + guests
    lower = y == 0
    upper = y == 1
    quarter = half // 2
    rows_c = 2 * half
    split = width // rows_c
    nm, nt = xb.shape[1:3]
    nq = x_hbm.shape[1] // nt - 6
    hops = (ngroups - 1 - j, j)
    dist = (j, ngroups - 1 - j)
    step_by = (-1, 1)
    dest = 2 * y + m_chip
    other = first + 1 - s

    barrier = pltpu.get_barrier_semaphore()
    for bp, bi in ((sib, i), (p, other), (sib, other)):
        pl.semaphore_signal(barrier, inc=1, device_id=(bp, bi), device_id_type=MESH)

    @pl.when(j > 0)
    def _():
        pl.semaphore_signal(barrier, inc=1, device_id=(p, i - 2), device_id_type=MESH)

    @pl.when(j < ngroups - 1)
    def _():
        pl.semaphore_signal(barrier, inc=1, device_id=(p, i + 2), device_id_type=MESH)

    greeted = 3 + jnp.where(j > 0, 1, 0) + jnp.where(j < ngroups - 1, 1, 0)
    if guests:

        @pl.when(upper)
        def _():
            for bp, bi in ((k, i), (s, first), (s, first + 1)):
                pl.semaphore_signal(barrier, inc=1, device_id=(bp, bi), device_id_type=MESH)

        greeted = greeted + jnp.where(lower, 3, 0)

    maker = jnp.logical_and(lower, m_chip == 0)

    def enter():
        pl.semaphore_wait(barrier, greeted)

        @pl.when(jnp.logical_and(maker, k == 0))
        def _():
            local(tail, out_tail, tail_recv).start()

        @pl.when(jnp.logical_and(maker, k > 0))
        def _():
            remote(tail, out_tail, tail_send, tail_recv, 0, first + 1).start()

        if guests:

            @pl.when(lower)
            def _():
                for op in (2, 3):
                    pl.semaphore_signal(guest_ready, inc=1, device_id=(op, first + k), device_id_type=MESH)

    def blocks(c):
        b = lax.div(c, split)
        xi = jnp.where(b < 4, b, jnp.where(b < 4 + nq, 4, jnp.where(b < 4 + 2 * nq, b - nq + 2, 5)))
        gi = jnp.where(b < 4 + nq, b, jnp.where(b < 4 + 2 * nq, 4 + nq, 5 + nq))
        return b, xi, gi

    def loads(c, slot):
        b, xi, gi = blocks(c)
        part = c - b * split
        cols = pl.ds(pl.multiple_of(part * rows_c, rows_c), rows_c)
        return (
            local(x_hbm.at[:, pl.ds(pl.multiple_of(xi * nt, nt), nt), cols], xb.at[slot], x_sem.at[slot]),
            local(g_hbm.at[:, pl.ds(pl.multiple_of(gi * nt, nt), nt)], gbuf.at[slot], g_sem.at[slot]),
        )

    for copy in loads(0, 0):
        copy.start()

    def produce(c):
        slot = lax.rem(c, 2)

        @pl.when(c + 1 < nc)
        def _():
            for copy in loads(c + 1, 1 - slot):
                copy.start()

        for copy in loads(c, slot):
            copy.wait()
        b = lax.div(c, split)

        @pl.when(jnp.logical_and(b >= 4 + nq, b < 4 + 2 * nq))
        def _():
            r = xb[slot].astype(F32)
            xb[slot] = (r * r).astype(BF)

        dws[...] = lax.dot_general(
            xb[slot].reshape(nm * nt, rows_c), gbuf[slot].reshape(nm * nt, width), (((0,), (0,)), ((), ())),
            preferred_element_type=F32,
        )

        @pl.when(c >= 2)
        def _():
            drain(xs.at[slot], ex_send.at[slot])

        @pl.when(c == 0)
        def _():
            enter()

        xs[slot] = dws[pl.ds(pl.multiple_of((1 - k) * half, half), half)].astype(BF)
        remote(xs.at[slot], rx.at[c], ex_send.at[slot], ex_recv.at[c], sib, i).start()
        own[c] = dws[pl.ds(pl.multiple_of(k * half, half), half)]

        @pl.when(c == 0)
        def _():
            n = small.shape[0]
            mine = jnp.where(k == 0, 1.0, 0.0)
            own_s[...] = jnp.zeros_like(own_s)
            xs_s[...] = jnp.zeros_like(xs_s)
            own_s[0:n] = small[...] * mine
            xs_s[0:n] = (small[...] * (1.0 - mine)).astype(BF)
            remote(xs_s, rx_s, small_send.at[0], ex_recv.at[nc], sib, i).start()

    def welcome(c):
        @pl.when(c == nc)
        def _():
            pl.semaphore_wait(guest_ready, 2)

        drain(gx.at[c - nc], gx_recv.at[c - nc])
        own[c] = gx[c - nc].astype(F32)

    def exchange(c):
        drain(rx.at[c], ex_recv.at[c])
        own[c] = own[c] + rx[c].astype(F32)
        if guests:

            @pl.when(jnp.logical_and(lower, jnp.logical_and(c >= low, c < high)))
            def _():
                gsrc[c - low] = own[c].astype(BF)
                remote(gsrc.at[c - low], gx.at[c - low], gx_send.at[0], gx_recv.at[c - low], p + 2, i).start()

        @pl.when(c == 0)
        def _():
            drain(rx_s, ex_recv.at[nc])
            own_s[...] = own_s[...] + rx_s[...].astype(F32)

    def reduce(c, d):
        def one(value, rr_at, ag_at, send, recv):
            @pl.when(hops[d] == 0)
            def _():
                rr_at[...] = value().astype(BF)

            @pl.when(hops[d] > 0)
            def _():
                drain(rr_at, recv)

                @pl.when(dist[d] > 0)
                def _():
                    rr_at[...] = (value() + rr_at[...].astype(F32)).astype(BF)

                @pl.when(dist[d] == 0)
                def _():
                    ag_at[...] = (value() + rr_at[...].astype(F32)).astype(BF)

            @pl.when(dist[d] > 0)
            def _():
                remote(rr_at, rr_at, send, recv, p, i + 2 * step_by[d]).start()

            @pl.when(jnp.logical_and(dist[d] == 0, hops[d] == 0))
            def _():
                ag_at[...] = rr_at[...]

        one(lambda: own[c, d * quarter : (d + 1) * quarter], rr.at[d, c], ag.at[d, c], r_send.at[d], r_recv.at[d, c])

        @pl.when(c == 0)
        def _():
            n = rr_s.shape[1]
            one(lambda: own_s[d * n : (d + 1) * n], rr_s.at[d], ag_s.at[d], small_send.at[1 + d], r_recv.at[d, nc + guests])

    def spread(c, d):
        def come(ag_at, forward_send, recv):
            @pl.when(dist[d] > 0)
            def _():
                drain(ag_at, recv)

            @pl.when(hops[d] > 0)
            def _():
                remote(ag_at, ag_at, forward_send, recv, p, i - 2 * step_by[d]).start()

        def one(ag_at, to, forward_send, recv, local_send, far_send, out_recv):
            come(ag_at, forward_send, recv)
            remote(ag_at, to, far_send, out_recv, dest, other).start()

            @pl.when(p == dest)
            def _():
                local(ag_at, to, out_recv).start()

            @pl.when(p != dest)
            def _():
                remote(ag_at, to, local_send, out_recv, dest, i).start()

        def place(c):
            b = lax.div(c, split)
            row = (c - b * split) * rows_c + k * half + d * quarter
            return out.at[b, pl.ds(pl.multiple_of(row, quarter), quarter)]

        def own_chunk():
            one(ag.at[d, c], place(c), a_send.at[d], a_recv.at[d, c], o_send.at[0], o_send.at[1], o_recv.at[0])

        if guests:
            pl.when(c < nc)(own_chunk)

            @pl.when(c >= nc)
            def _():
                come(ag.at[d, c], a_send.at[d], a_recv.at[d, c])
                to = place(c - nc + low)
                remote(ag.at[d, c], to, guest_send.at[0], o_recv.at[0], s, i).start()
                remote(ag.at[d, c], to, guest_send.at[1], o_recv.at[0], s, other).start()
        else:
            own_chunk()

        @pl.when(c == 0)
        def _():
            n = rr_s.shape[1]
            to_s = out_small.at[pl.ds(pl.multiple_of(k * 2 * n + d * n, n), n)]
            one(ag_s.at[d], to_s, small_send.at[3 + d], a_recv.at[d, nc + guests], small_send.at[5 + d], small_send.at[7 + d], small_recv.at[0])

    def turn(u, own_work, guest_work=None):
        if not guests:

            @pl.when(jnp.logical_and(u >= 0, u < nc))
            def _():
                own_work(u)

            return
        at = min(GUEST_TURN, nc)
        c = jnp.where(u < at, u, jnp.where(u < at + guests, nc + u - at, u - guests))
        c = jnp.where(upper, c, u)
        mine = jnp.logical_and(u >= 0, u < nc + jnp.where(upper, guests, 0))
        if guest_work is not own_work:

            @pl.when(jnp.logical_and(mine, c < nc))
            def _():
                own_work(c)

            if guest_work is not None:

                @pl.when(jnp.logical_and(mine, c >= nc))
                def _():
                    guest_work(c)

        else:
            away = jnp.logical_and(lower, jnp.logical_and(c >= low, c < high))

            @pl.when(jnp.logical_and(mine, jnp.logical_not(away)))
            def _():
                own_work(c)

    def step(t, none):
        turn(t, produce)
        turn(t - 1, exchange, welcome)
        for d in range(2):
            work = functools.partial(reduce, d=d)
            turn(t - 1 - LAG * hops[d], work, work)
        for d in range(2):
            work = functools.partial(spread, d=d)
            turn(t - 1 - LAG * (ngroups - 1 + dist[d]), work, work)
        return none

    lax.fori_loop(0, nc + guests + 1 + 2 * LAG * (ngroups - 1), step, 0)

    def settle(ref, sem):
        if not guests:
            drain(ref, sem)
            return

        @pl.when(upper)
        def _():
            drain(ref, sem)

        @pl.when(lower)
        def _():
            drain(ref.at[pl.ds(0, low)], sem)
            drain(ref.at[pl.ds(high, nc - high)], sem)

    def settle_own(ref, sem):
        if not guests:
            drain(ref, sem)
            return
        drain(ref.at[pl.ds(0, low)], sem)
        drain(ref.at[pl.ds(high, nc - high)], sem)

        @pl.when(upper)
        def _():
            drain(ref.at[pl.ds(low, guests)], sem)

    for slot in range(min(2, nc)):
        drain(xs.at[slot], ex_send.at[slot])
    drain(xs_s, small_send.at[0])
    for d in range(2):

        @pl.when(dist[d] > 0)
        def _():
            settle(rr.at[d], r_send.at[d])
            drain(rr_s.at[d], small_send.at[1 + d])

        @pl.when(hops[d] > 0)
        def _():
            settle(ag.at[d], a_send.at[d])
            drain(ag_s.at[d], small_send.at[3 + d])

        @pl.when(p != dest)
        def _():
            drain(ag_s.at[d], small_send.at[5 + d])

        drain(ag_s.at[d], small_send.at[7 + d])

    for d in range(2):

        @pl.when(p != dest)
        def _():
            settle_own(ag.at[d], o_send.at[0])

        settle_own(ag.at[d], o_send.at[1])
    if guests:

        @pl.when(lower)
        def _():
            drain(gsrc, gx_send.at[0])

        @pl.when(upper)
        def _():
            for d in range(2):
                drain(ag.at[d, pl.ds(nc, guests)], guest_send.at[0])
                drain(ag.at[d, pl.ds(nc, guests)], guest_send.at[1])

    @pl.when(jnp.logical_and(maker, k > 0))
    def _():
        drain(tail, tail_send)

    @pl.when(p == 0)
    def _():
        drain(out_tail, tail_recv)

    drain(out, o_recv.at[0])
    drain(out_small, small_recv.at[0])


def widen_kernel(
    ob, gb, rows, w, tail, num, den, last,
    out, grad, g_in, g_out, g_key, g_val, g_rec, gain, bias, tmix, cmix, decay, bonus, fin_num, fin_den, fin_rows,
    stage, narrow, wide, sem, in_sem, out_sem,
):
    nblocks, width, _ = w.shape
    slots, step, _ = stage.shape
    nq, cuts = (nblocks - 5) // 2, width // step
    for n, src in enumerate((ob, gb)):
        local(src, narrow.at[n], in_sem.at[n]).start()

    def one(t, none):
        slot = lax.rem(t, slots)
        b = lax.div(t, cuts)
        cut = pl.ds(pl.multiple_of((t - b * cuts) * step, step), step)

        @pl.when(t >= slots)
        def _():
            drain(stage.at[slot], sem.at[slot])

        stage[slot] = w[b, cut].astype(F32)

        @pl.when(b < 3)
        def _():
            local(stage.at[slot], g_in.at[b, cut], sem.at[slot]).start()

        @pl.when(b == 3)
        def _():
            local(stage.at[slot], g_out.at[0, cut], sem.at[slot]).start()

        for q in range(nq):

            @pl.when(b == 4 + q)
            def _():
                local(stage.at[slot], g_key.at[cut, q * width : (q + 1) * width], sem.at[slot]).start()

        @pl.when(jnp.logical_and(b >= 4 + nq, b < 4 + 2 * nq))
        def _():
            local(stage.at[slot], g_val.at[b - 4 - nq, cut], sem.at[slot]).start()

        @pl.when(b == 4 + 2 * nq)
        def _():
            local(stage.at[slot], g_rec.at[0, cut], sem.at[slot]).start()

        return none

    lax.fori_loop(0, nblocks * cuts, one, 0)
    for n, dst in enumerate((out, grad)):
        drain(narrow.at[n], in_sem.at[n])
        wide[n] = narrow[n].astype(F32)
        if n == 1:

            @pl.when(lax.axis_index("pipe") == 0)
            def _():
                wide[n, 0 : tail.shape[0]] = tail[...].astype(F32)

        local(wide.at[n], dst, out_sem.at[n]).start()
    at = 0
    for dst in (gain, bias, tmix, cmix, decay, bonus):
        n = dst.shape[0]
        dst[...] = rows[at : at + n].astype(F32).reshape(dst.shape)
        at += n
    for src, dst in ((num, fin_num), (den, fin_den), (last, fin_rows)):
        dst[...] = src[...]
    for slot in range(slots):
        drain(stage.at[slot], sem.at[slot])
    for n in range(2):
        drain(wide.at[n], out_sem.at[n])


def body(
    block_input, ln_gain, ln_bias, tm_mix, cm_mix, time_decay, time_first, tm_in, tm_out,
    cm_key, cm_value, cm_recept, wkv_num, wkv_den, last_rows, cotangent,
):
    npipe, ndp = lax.axis_size("pipe"), lax.axis_size("dp")
    seg, width = block_input.shape[1:]
    hidden = cm_key.shape[2]
    nq = hidden // width
    length = seg * npipe
    nt = min(TOKENS, seg)
    nm, per = length // nt, seg // nt
    anywhere = pl.BlockSpec(memory_space=pl.ANY)
    vmem = pl.BlockSpec(memory_space=pltpu.VMEM)
    dma = pltpu.SemaphoreType.DMA
    shape = jax.ShapeDtypeStruct
    nb = 6 + nq
    nblocks = 5 + 2 * nq
    xs, gs, small, fin_num, fin_den, fin_rows, ob, gb, turned, tail = pl.pallas_call(
        functools.partial(layers_kernel, npipe),
        name="layers",
        out_shape=[
            shape((nm, nb * nt, width), BF),
            shape((nm, nb * nt, width), BF),
            shape((16, width), F32),
            shape((1, 1, width), F32),
            shape((1, 1, width), F32),
            shape((1, 2, 1, width), F32),
            shape((seg, width), BF),
            shape((seg, width), BF),
            shape((nblocks, width, width), BF),
            shape((nt, width), BF),
        ],
        in_specs=[anywhere] * 16,
        out_specs=[anywhere, anywhere, vmem] + [anywhere] * 7,
        scratch_shapes=[
            pltpu.VMEM((nblocks, width, width), BF),
            pltpu.VMEM((2, width), F32),
            pltpu.VMEM((2, width), F32),
            pltpu.VMEM((3, 1, width), F32),
            pltpu.VMEM((2, width), F32),
            pltpu.VMEM((1, width), F32),
            pltpu.VMEM((1, width), F32),
            pltpu.VMEM((1, width), F32),
            pltpu.VMEM((1, width), F32),
            pltpu.VMEM((2, width), F32),
            pltpu.VMEM((nm, nt, width), BF),
            pltpu.VMEM((nm, nt, width), BF),
            *[pltpu.VMEM((nm, nt, width), F32)] * 4,
            *[pltpu.VMEM((nm, nt, width), BF)] * 5,
            pltpu.VMEM((nm, nq * nt, width), BF),
            *[pltpu.VMEM((nm, nt, 1), F32)] * 2,
            *[pltpu.VMEM((nm, 8, width), F32)] * 2,
            pltpu.VMEM((8, width), F32),
            pltpu.VMEM((16, 8, width), F32),
            pltpu.VMEM((2, 6 * nt, width), BF),
            pltpu.VMEM((2, nb * nt, width), BF),
            pltpu.VMEM((8, 8, width), F32),
            *[pltpu.VMEM((nt, width), F32)] * 4,
            dma((6 + nblocks,)), dma((6 + nblocks,)), dma((nm,)), dma((nm,)), dma((nm,)), dma((nm,)),
            dma((per,)), dma((per,)), dma((per,)), dma((per,)),
            dma((3,)), dma((3,)), dma((3,)), dma((3,)), dma((2,)), dma((2,)), dma((nm,)), dma((2,)), dma((nblocks,)), dma,
        ],
        compiler_params=pltpu.CompilerParams(collective_id=0, has_side_effects=True, vmem_limit_bytes=VMEM_BYTES),
    )(block_input, cotangent, ln_gain, ln_bias, jnp.swapaxes(tm_mix, 0, 1), cm_mix, time_decay, time_first, wkv_num, wkv_den, last_rows,
      tm_in, tm_out, cm_key, cm_value, cm_recept)

    rows_c = width // SPLIT if width % (128 * SPLIT) == 0 else width // 2
    nc, half = nblocks * (width // rows_c), rows_c // 2
    quarter = half // 2
    guests = GUESTS if npipe == 4 else 0
    all_c = nc + guests
    out, out_small, out_tail = pl.pallas_call(
        functools.partial(sums_kernel, npipe, ndp // 2, guests),
        name="sums",
        out_shape=[ON_CHIP((nblocks, width, width), BF), ON_CHIP((64, width), BF), ON_CHIP((nt, width), BF)],
        in_specs=[anywhere, anywhere, vmem, anywhere],
        out_specs=[vmem, vmem, vmem],
        scratch_shapes=[
            pltpu.VMEM((2, nm, nt, rows_c), BF),
            pltpu.VMEM((2, nm, nt, width), BF),
            pltpu.VMEM((rows_c, width), F32),
            pltpu.VMEM((2, half, width), BF),
            pltpu.VMEM((all_c, half, width), F32),
            pltpu.VMEM((nc, half, width), BF),
            pltpu.VMEM((2, all_c, quarter, width), BF),
            pltpu.VMEM((2, all_c, quarter, width), BF),
            pltpu.VMEM((32, width), BF),
            pltpu.VMEM((32, width), F32),
            pltpu.VMEM((32, width), BF),
            pltpu.VMEM((2, 16, width), BF),
            pltpu.VMEM((2, 16, width), BF),
            pltpu.VMEM((max(guests, 1), half, width), BF),
            pltpu.VMEM((max(guests, 1), half, width), BF),
            dma((2,)), dma((2,)), dma((2,)), dma((nc + 1,)), dma((2,)), dma((2, all_c + 1)), dma((2,)), dma((2, all_c + 1)),
            dma((2,)), dma((1,)), dma((9,)), dma((1,)), dma((1,)), dma((max(guests, 1),)), dma((2,)), pltpu.SemaphoreType.REGULAR, dma, dma,
        ],
        compiler_params=pltpu.CompilerParams(collective_id=1, has_side_effects=True, vmem_limit_bytes=SUMS_BYTES),
    )(xs, gs, small, tail)

    in_vmem = pltpu.with_memory_space_constraint(out, pltpu.VMEM)
    wide = pl.pallas_call(
        widen_kernel,
        name="widen",
        out_shape=[
            shape((seg, width), F32), shape((seg, width), F32), shape((3, width, width), F32), shape((1, width, width), F32),
            shape((width, hidden), F32), shape((nq, width, width), F32), shape((1, width, width), F32),
            shape((2, width), F32), shape((2, width), F32), shape((3, 1, width), F32), shape((2, width), F32),
            shape((1, width), F32), shape((1, width), F32),
            shape((1, 1, width), F32), shape((1, 1, width), F32), shape((1, 2, 1, width), F32),
        ],
        in_specs=[anywhere, anywhere, vmem, vmem, vmem, vmem, vmem, vmem],
        out_specs=[anywhere] * 7 + [vmem] * 9,
        scratch_shapes=[
            pltpu.VMEM((4, width // 2, width), F32),
            pltpu.VMEM((2, seg, width), BF),
            pltpu.VMEM((2, seg, width), F32),
            dma((4,)), dma((2,)), dma((2,)),
        ],
        compiler_params=pltpu.CompilerParams(vmem_limit_bytes=WIDEN_BYTES),
    )(ob, gb, out_small, in_vmem, out_tail, fin_num, fin_den, fin_rows)
    return (
        wide[0][None],
        wide[1][None],
        wide[7][None],
        wide[8][None],
        jnp.swapaxes(wide[9], 0, 1),
        wide[10][None],
        wide[11],
        wide[12],
        wide[2][None],
        wide[3],
        wide[4][None],
        wide[5].reshape(1, hidden, width),
        wide[6],
        wide[13],
        wide[14],
        wide[15],
    )


def solution(mesh):
    args = (
        P("dp", "pipe", None),
        P("pipe", None, None),
        P("pipe", None, None),
        P("pipe", None, None),
        P("pipe", None, None),
        P("pipe", None),
        P("pipe", None),
        P("pipe", None, None, None),
        P("pipe", None, None),
        P("pipe", None, None),
        P("pipe", None, None),
        P("pipe", None, None),
        P("pipe", "dp", None),
        P("pipe", "dp", None),
        P("pipe", None, "dp", None),
        P("dp", "pipe", None),
    )
    outs = (
        P("dp", "pipe", None),
        P("dp", "pipe", None),
        P("pipe", None, None),
        P("pipe", None, None),
        P("pipe", None, None),
        P("pipe", None, None),
        P("pipe", None),
        P("pipe", None),
        P("pipe", None, None, None),
        P("pipe", None, None),
        P("pipe", None, None),
        P("pipe", None, None),
        P("pipe", None, None),
        P("pipe", "dp", None),
        P("pipe", "dp", None),
        P("pipe", None, "dp", None),
    )
    return jax.shard_map(body, mesh=mesh, in_specs=args, out_specs=outs, check_vma=False)
```
